256 devices in a mesh: var: 16 (over y, x_lo, core), seq: 16 (over x_hi, z).
Axes of the slice: x: 4 (x_hi: 2, x_lo: 2; x = x_hi * 2 + x_lo), y: 4, z: 8, core: 2. Of those that a mesh axis runs over, the one named last changes fastest.
Arguments:
- patches: bfloat16 [96, 2048, 64], P('var', 'seq'), may hold values from -6 to 6
- patch_weight: bfloat16 [96, 64, 4096], P('var'), may hold values from -0.75 to 0.75
- var_embed: bfloat16 [96, 4096], P('var'), may hold values from -1.71 to 4.5
- agg_query: bfloat16 [4096, 32], replicated, may hold values from -1.5 to 1000
- norm_gain: bfloat16 [4096], replicated, may hold values from 0.5 to 1.5
- qkv_weight: bfloat16 [4096, 3, 4096], P(None, None, 'var'), may hold values from -0.21875 to 0.21875
- out_weight: bfloat16 [4096, 4096], P('var'), may hold values from -0.09375 to 0.09375
- head_cot: bfloat16 [2048, 6144], P('seq', 'var'), may hold values from -0.125 to 0.125
Outputs:
- head_grad: float32 [4096, 6144], P('seq', 'var')
The draws below stay inside these ranges and needn't reach their ends.
All inputs are finite; a program needn't handle non-finite values.
Results may differ from the reference program's by a relative error of at most 0.033.
The reference program's roundings to bfloat16 on the way count: a program that leaves them out, or rounds other values in their place, can miss the bound.
Values may be sent and summed in bfloat16 or wider, within the bound.
No kernel may reach another device: no remote copies, remote signals or barrier semaphores. Data moves between devices by JAX's collectives and lax.ppermute only.
A program may use at most 128 MiB of HBM per device.

```python
import math
import jax
import jax.numpy as jnp
from jax import lax

D = 4096
HEADS = 32
HD = 128
P_SIZE = 64
V = 96
C = 6144
TOK_DEV = 128
TOKENS = 2048


def draw_var_embed(key, part):
    key = jax.random.fold_in(key, 13)
    base = jax.random.uniform(key, (V, D), jnp.float32, -1.7, 1.7)
    return base.astype(jnp.bfloat16)


def draw_agg_query(key, part):
    key = jax.random.fold_in(key, 11)
    return jnp.clip(0.25 * jax.random.normal(key, (D, HEADS), jnp.float32), -1.5, 1.5).astype(jnp.bfloat16)


def draw_qkv_weight(key, part):
    key = jax.random.fold_in(key, 17)
    factor = D ** (-0.5)
    base = jnp.clip(jax.random.normal(key, (D, 3, D), jnp.float32), -4.0, 4.0) * factor
    return jnp.stack([3.0 * base[:, 0, :], base[:, 1, :], base[:, 2, :]], axis=1).astype(jnp.bfloat16)


def level_of(stream_key, dims, split, low, top_value):
    level, own = 1.0, jax.random.fold_in(stream_key, 6)
    for axis_at, blocks in split:
        heights = jnp.exp(jax.random.uniform(jax.random.fold_in(own, axis_at), (blocks,), jnp.float32, low / len(split), top_value / len(split)))
        level = level * jnp.repeat(heights, dims[axis_at] // blocks).reshape([-1 if axis == axis_at else 1 for axis in range(len(dims))])
    return level


def normal_values(stream_key, extent, scale, reach, split=(), kind=jnp.bfloat16):
    factor_of = level_of(stream_key, extent, split, -0.22, 0.18) if split else 1.0
    array = jax.random.normal(stream_key, extent, jnp.float32) * scale * factor_of
    return jnp.minimum(jnp.maximum(array, -reach), reach).astype(kind)


def setup_inputs(seed: int = 0) -> dict:
    seeds = jax.random.split(jax.random.key(seed), 9)
    patches = normal_values(seeds[0], (V, TOKENS, P_SIZE), 1.0, 6.0, ((0, 16), (1, 16)))
    patch_weight = normal_values(seeds[1], (V, P_SIZE, D), P_SIZE ** -0.5, 0.75, ((0, 16),))
    var_embed = draw_var_embed(jax.random.fold_in(seeds[8], 71), 0)
    agg_query = draw_agg_query(jax.random.fold_in(seeds[8], 71), 0)
    norm_gain = jnp.clip(1.0 + 0.1 * jax.random.normal(seeds[4], (D,), jnp.float32), 0.5, 1.5).astype(jnp.bfloat16)
    qkv_weight = draw_qkv_weight(jax.random.fold_in(seeds[8], 71), 0)
    out_weight = normal_values(seeds[6], (D, D), D ** -0.5, 0.09375, ((0, 16),))
    head_cot = normal_values(seeds[7], (TOKENS, C), TOKENS ** -0.5, 0.125, ((0, 16), (1, 16)))
    return dict(patches=patches, patch_weight=patch_weight, var_embed=var_embed, agg_query=agg_query, norm_gain=norm_gain, qkv_weight=qkv_weight, out_weight=out_weight, head_cot=head_cot)


eps = 1e-05

def aggregate_block(patch_block, patch_weight, var_embed, agg_query):
    embedded = jnp.einsum('vrp,vpd->vrd', patch_block.astype(jnp.float32), patch_weight.astype(jnp.float32))
    embedded = (embedded + var_embed.astype(jnp.float32)[:, None, :]).astype(jnp.bfloat16)
    count, rows, width = embedded.shape
    scores = jnp.dot(embedded.reshape(count * rows, width), agg_query, preferred_element_type=jnp.float32)
    scores = scores.reshape(count, rows, HEADS) / math.sqrt(HD)
    peak = lax.optimization_barrier(jnp.max(scores, axis=0))
    weights = jnp.exp(scores - peak[None])
    total = lax.optimization_barrier(jnp.sum(weights, axis=0))
    values = embedded.reshape(count, rows, HEADS, HD).astype(jnp.float32)
    numer = lax.optimization_barrier(jnp.sum(weights[..., None] * values, axis=0))
    return (numer / total[..., None]).reshape(rows, width).astype(jnp.bfloat16)

def layer_norm(tokens, gain):
    values = tokens.astype(jnp.float32)
    center = lax.optimization_barrier(jnp.mean(values, axis=-1, keepdims=True))
    shifted = values - center
    spread = lax.optimization_barrier(jnp.mean(shifted * shifted, axis=-1, keepdims=True))
    return (shifted * lax.rsqrt(spread + eps) * gain.astype(jnp.float32)).astype(jnp.bfloat16)

def attend_head(operands):
    query, keys, values = operands
    scores = jnp.dot(query, keys.T, preferred_element_type=jnp.float32) / math.sqrt(HD)
    peak = lax.optimization_barrier(jnp.max(scores, axis=-1, keepdims=True))
    weights = jnp.exp(scores - peak)
    total = lax.optimization_barrier(jnp.sum(weights, axis=-1, keepdims=True))
    mixed = jnp.dot(weights.astype(jnp.bfloat16), values, preferred_element_type=jnp.float32)
    return (mixed / total).astype(jnp.bfloat16)

def reference(patches, patch_weight, var_embed, agg_query, norm_gain, qkv_weight, out_weight, head_cot):
    blocks = TOKENS // TOK_DEV
    grouped = patches.reshape(V, blocks, TOK_DEV, P_SIZE).transpose(1, 0, 2, 3)
    aggregated = lax.map(lambda block: aggregate_block(block, patch_weight, var_embed, agg_query), grouped)
    aggregated = aggregated.reshape(TOKENS, D)
    normed = layer_norm(aggregated, norm_gain)
    qkv = jnp.dot(normed, qkv_weight.reshape(D, 3 * D), preferred_element_type=jnp.float32).astype(jnp.bfloat16)
    qkv = qkv.reshape(TOKENS, 3, HEADS, HD).transpose(1, 2, 0, 3)
    attended = lax.map(attend_head, (qkv[0], qkv[1], qkv[2]))
    attended = attended.transpose(1, 0, 2).reshape(TOKENS, D)
    projected = jnp.dot(attended, out_weight, preferred_element_type=jnp.float32)
    layer = (aggregated.astype(jnp.float32) + projected).astype(jnp.bfloat16)
    return lax.dot_general(layer, head_cot, (((0,), (0,)), ((), ())), preferred_element_type=jnp.float32)
```

```python
import math

import jax
import jax.numpy as jnp
from jax import lax
from jax.experimental import pallas as pl
from jax.experimental.pallas import tpu as pltpu
from jax.sharding import Mesh, PartitionSpec as P

EPS = 1e-05
HD = 128
F32 = jnp.float32
BF16 = jnp.bfloat16
VAR = ("y", "xl", "c")
CHIPS = ("y", "xl")
SEQ = ("xh", "z")
NT = (((1,), (1,)), ((), ()))
TN = (((0,), (0,)), ((), ()))
NN = (((1,), (0,)), ((), ()))
MB = 1024 * 1024


def dot(a, b, dims):
    return lax.dot_general(a, b, dims, preferred_element_type=F32)


def params():
    return pltpu.CompilerParams(vmem_limit_bytes=40 * MB)


def in_three(x):
    high = x.astype(BF16).astype(F32)
    rest = x - high
    middle = rest.astype(BF16).astype(F32)
    return high, middle, rest - middle


def embed_kernel(pixels_ref, weight_ref, shift_ref, query_ref, out_ref, embedded, scores):
    member = pl.program_id(0)
    count = embedded.shape[0]
    width = weight_ref.shape[2]
    heads = query_ref.shape[0]
    rows = pixels_ref.shape[2]
    chosen = lax.broadcasted_iota(jnp.int32, shift_ref.shape, 0) == member
    shift = jnp.sum(jnp.where(chosen, shift_ref[...].astype(F32), 0.0), axis=0, keepdims=True)
    step = 1024
    total = jnp.zeros((rows, heads), F32)
    for at in range(0, width, step):
        block = dot(pixels_ref[0], weight_ref[0, :, at : at + step], TN)
        block = (block + shift[:, at : at + step]).astype(BF16)
        embedded[member, :, at : at + step] = block
        total = total + dot(block, query_ref[:, at : at + step], NT)
    scores[member] = total / math.sqrt(HD)

    @pl.when(member == count - 1)
    def _():
        every = scores[...]
        peak = jnp.max(every, axis=0)
        weights = jnp.exp(every - peak[None])
        total = jnp.sum(weights, axis=0)
        for h in range(heads):
            cols = slice(h * HD, (h + 1) * HD)
            numer = weights[0][:, h : h + 1] * embedded[0, :, cols].astype(F32)
            for v in range(1, count):
                numer = numer + weights[v][:, h : h + 1] * embedded[v, :, cols].astype(F32)
            out_ref[:, cols] = numer.astype(BF16)
        p0, p1, p2 = in_three(peak)
        t0, t1, t2 = in_three(total)
        blank = jnp.zeros_like(peak)
        out_ref[:, width : width + 128] = jnp.concatenate([p0, p1, p2, t0], axis=1).astype(BF16)
        out_ref[:, width + 128 : width + 256] = jnp.concatenate(
            [t1, t2, blank, blank], axis=1
        ).astype(BF16)


def embed(pixels, weight, shift, query):
    count, depth, rows = pixels.shape
    width = weight.shape[2]
    heads = query.shape[0]
    return pl.pallas_call(
        embed_kernel,
        grid=(count,),
        in_specs=[
            pl.BlockSpec((1, depth, rows), lambda v: (v, 0, 0)),
            pl.BlockSpec((1, depth, width), lambda v: (v, 0, 0)),
            pl.BlockSpec((count, width), lambda v: (0, 0)),
            pl.BlockSpec((heads, width), lambda v: (0, 0)),
        ],
        out_specs=pl.BlockSpec((rows, width + 256), lambda v: (0, 0)),
        out_shape=jax.ShapeDtypeStruct((rows, width + 256), BF16),
        scratch_shapes=[
            pltpu.VMEM((count, rows, width), BF16),
            pltpu.VMEM((count, rows, heads), F32),
        ],
        compiler_params=params(),
        name="embed",
    )(pixels, weight, shift, query)


def merge_kernel(parts_ref, gain_ref, normed_ref, kept_ref, whole):
    rows, padded = parts_ref.shape
    width = padded - 256
    heads = width // HD
    share = 8
    sources = rows // share
    stats = parts_ref[:, width:].astype(F32)
    peak = stats[:, 0:32] + stats[:, 32:64] + stats[:, 64:96]
    total = stats[:, 96:128] + stats[:, 128:160] + stats[:, 160:192]
    peak = peak.reshape(sources, share, heads)
    total = total.reshape(sources, share, heads)
    top = jnp.max(peak, axis=0)
    scale = jnp.exp(peak - top[None])
    total = jnp.sum(total * scale, axis=0)
    scale = scale.reshape(rows, heads)
    sums = jnp.zeros((share, HD), F32)
    last = None
    for h in range(heads):
        cols = slice(h * HD, (h + 1) * HD)
        numer = jnp.zeros((share, HD), F32)
        for at in range(0, rows, 16):
            block = parts_ref[at : at + 16, cols].astype(F32) * scale[at : at + 16, h : h + 1]
            numer = numer + block[:8] + block[8:]
        value = (numer / total[:, h : h + 1]).astype(BF16).astype(F32)
        whole[:, cols] = value
        sums = sums + value
        if h % 2 == 0:
            last = value
        else:
            kept_ref[(h // 2) * 16 : (h // 2) * 16 + 16, :] = jnp.concatenate(
                [last, value], axis=0
            ).astype(BF16)
    center = jnp.sum(sums, axis=1, keepdims=True) / width
    squares = jnp.zeros((share, HD), F32)
    for h in range(heads):
        shifted = whole[:, h * HD : (h + 1) * HD] - center
        squares = squares + shifted * shifted
    factor = lax.rsqrt(jnp.sum(squares, axis=1, keepdims=True) / width + EPS)
    for h in range(heads):
        cols = slice(h * HD, (h + 1) * HD)
        value = (whole[:, cols] - center) * factor * gain_ref[:, cols].astype(F32)
        twice = jnp.concatenate([value, value], axis=0).astype(BF16)
        for at in range(0, normed_ref.shape[0], 16):
            normed_ref[at : at + 16, cols] = twice


def merge(parts, gain, copies):
    rows, padded = parts.shape
    width = padded - 256
    return pl.pallas_call(
        merge_kernel,
        out_shape=(
            jax.ShapeDtypeStruct((copies * 8, width), BF16),
            jax.ShapeDtypeStruct((width // 16, HD), BF16),
        ),
        scratch_shapes=[pltpu.VMEM((8, width), F32)],
        compiler_params=params(),
        name="merge",
    )(parts, gain)


def qkv_kernel(place_ref, mine_ref, other_ref, weight_ref, kv_ref, keep_ref, send_ref, tokens, made):
    step = pl.program_id(0)
    core = place_ref[0]
    parity = place_ref[1]
    half = mine_ref.shape[0]

    @pl.when(step == 0)
    def _():
        tokens[pl.ds(pl.multiple_of(core * half, half), half), :] = mine_ref[...]
        tokens[pl.ds(pl.multiple_of((1 - core) * half, half), half), :] = other_ref[...]

    made[step] = dot(tokens[...], weight_ref[0], NN).astype(BF16)

    @pl.when(step == 2)
    def _():
        query = made[0]
        first, second = query[:, :HD], query[:, HD:]
        keep_ref[...] = jnp.where(parity == 0, first, second)
        send_ref[...] = jnp.where(parity == 0, second, first)
        rows = 2 * half
        for p in range(2):
            cols = slice(p * HD, (p + 1) * HD)
            keys, values = made[1, :, cols], made[2, :, cols]
            for to in range(p, 16, 2):
                kv_ref[to * rows : (to + 1) * rows, :HD] = keys
                kv_ref[to * rows : (to + 1) * rows, HD:] = values


def project(place, mine, other, weight):
    half, width = mine.shape
    cols = weight.shape[2]
    rows = 2 * half
    whole = lambda s: (0, 0)
    return pl.pallas_call(
        qkv_kernel,
        grid=(3,),
        in_specs=[
            pl.BlockSpec(memory_space=pltpu.SMEM),
            pl.BlockSpec((half, width), whole),
            pl.BlockSpec((half, width), whole),
            pl.BlockSpec((1, width, cols), lambda s: (s, 0, 0)),
        ],
        out_specs=[
            pl.BlockSpec((16 * rows, 2 * HD), whole),
            pl.BlockSpec((rows, HD), whole),
            pl.BlockSpec((rows, HD), whole),
        ],
        out_shape=[
            jax.ShapeDtypeStruct((16 * rows, 2 * HD), BF16),
            jax.ShapeDtypeStruct((rows, HD), BF16),
            jax.ShapeDtypeStruct((rows, HD), BF16),
        ],
        scratch_shapes=[pltpu.VMEM((rows, width), BF16), pltpu.VMEM((3, rows, cols), BF16)],
        compiler_params=params(),
        name="project",
    )(place, mine, other, weight)


def attend_kernel(place_ref, keep_ref, got_ref, kv_ref, out_ref):
    parity = place_ref[1]
    keys, values = kv_ref[:, :HD], kv_ref[:, HD:]
    mixed = []
    for band in range(2):
        query = jnp.where(parity == band, keep_ref[...], got_ref[...])
        scores = dot(query, keys, NT) / math.sqrt(HD)
        peak = jnp.max(scores, axis=1, keepdims=True)
        weights = jnp.exp(scores - peak)
        total = jnp.sum(weights, axis=1, keepdims=True)
        mixed.append(dot(weights.astype(BF16), values, NN) / total)
    for chip in range(8):
        for core in range(2):
            at = core * 64 + chip * 8
            to = (chip * 2 + core) * 16
            out_ref[to : to + 16, :] = jnp.concatenate(
                [mixed[0][at : at + 8], mixed[1][at : at + 8]], axis=0
            ).astype(BF16)


def attend(place, keep, got, kv):
    return pl.pallas_call(
        attend_kernel,
        in_specs=[pl.BlockSpec(memory_space=pltpu.SMEM)] + [pl.BlockSpec(memory_space=pltpu.VMEM)] * 3,
        out_shape=jax.ShapeDtypeStruct((256, HD), BF16),
        compiler_params=params(),
        name="attend",
    )(place, keep, got, kv)


def output_kernel(parts_ref, weight_ref, out_ref, attended):
    for pair in range(8):
        for parity in range(2):
            for source in range(16):
                head = 2 * source + parity
                attended[pair * 16 : pair * 16 + 16, head * HD : (head + 1) * HD] = parts_ref[
                    2 * pair + parity, source * 16 : source * 16 + 16, :
                ]
    product = dot(attended[...], weight_ref[...], NN)
    rows = product.shape[0]
    for band in range(0, 16, 2):
        residual = []
        for b in (band, band + 1):
            kept = parts_ref[b, 256:272, :].astype(F32)
            residual.append(jnp.concatenate([kept[:8], kept[8:]], axis=1))
        at = band * 8
        block = (jnp.concatenate(residual, axis=0) + product[at : at + 16]).astype(BF16)
        for copy in range(out_ref.shape[0] // rows):
            out_ref[copy * rows + at : copy * rows + at + 16, :] = block


def output(parts, weight, copies):
    width, cols = weight.shape
    rows = 128
    return pl.pallas_call(
        output_kernel,
        out_shape=jax.ShapeDtypeStruct((copies * rows, cols), BF16),
        scratch_shapes=[pltpu.VMEM((rows, width), BF16)],
        compiler_params=params(),
        name="output",
    )(parts, weight)


def swap(x, axis, size):
    return lax.ppermute(x, axis, [(k, k ^ 1) for k in range(size)])


def exchange(x, axes):
    return lax.all_to_all(x, axes, 0, 0, tiled=True)


def body(patches, patch_weight, var_embed, agg_query, norm_gain, qkv_weight, out_weight, head_cot):
    core = lax.axis_index("c")
    place = jnp.stack([core, lax.axis_index("z") % 2]).astype(jnp.int32)
    band = lax.axis_index(SEQ)
    width = out_weight.shape[1]

    cols = lax.dynamic_slice_in_dim(out_weight, band * 256, 256, 1)
    cols = lax.all_gather(cols, VAR, axis=0, tiled=True)
    cot = lax.all_gather(head_cot, SEQ, axis=0, tiled=True)
    cot = cot.reshape(16, 8, 2, 8, 384).transpose(2, 1, 0, 3, 4).reshape(2, 1024, 384)

    parts = embed(patches.transpose(0, 2, 1), patch_weight, var_embed, agg_query.T)
    parts = exchange(parts, VAR)
    normed, kept = merge(parts, norm_gain.reshape(1, width), 8)
    normed = exchange(normed, CHIPS)
    other = swap(normed, "c", 2)
    kv, query, query_out = project(place, normed, other, qkv_weight.transpose(1, 0, 2))
    query_in = swap(query_out, "z", 8)
    kv = exchange(kv, SEQ)
    attended = attend(place, query, query_in, kv)
    attended = exchange(attended, VAR)
    sent = jnp.concatenate(
        [jnp.broadcast_to(attended[None], (16, 256, HD)), kept.reshape(16, 16, HD)], axis=1
    )
    got = exchange(sent, SEQ)
    layer = output(got, cols, 8)
    layer = exchange(layer, CHIPS)
    other = swap(layer, "c", 2)
    first = lax.dynamic_index_in_dim(cot, core, 0, keepdims=False)
    second = lax.dynamic_index_in_dim(cot, 1 - core, 0, keepdims=False)
    return dot(layer, first, TN) + dot(other, second, TN)


def solution(mesh):
    whole = Mesh(mesh.devices.reshape(4, 2, 2, 2, 8), ("y", "xl", "c", "xh", "z"))
    return jax.shard_map(
        body,
        mesh=whole,
        in_specs=(
            P(VAR, SEQ, None),
            P(VAR, None, None),
            P(VAR, None),
            P(),
            P(),
            P(None, None, VAR),
            P(VAR, None),
            P(SEQ, VAR),
        ),
        out_specs=P(SEQ, VAR),
        check_vma=False,
    )
```

```python
import math

import jax
import jax.numpy as jnp
from jax import lax
from jax.experimental import pallas as pl
from jax.experimental.pallas import tpu as pltpu
from jax.sharding import Mesh, PartitionSpec as P

EPS = 1e-05
HD = 128
F32 = jnp.float32
BF16 = jnp.bfloat16
VAR = ("y", "xl", "c")
CHIPS = ("y", "xl")
SEQ = ("xh", "z")
NT = (((1,), (1,)), ((), ()))
TN = (((0,), (0,)), ((), ()))
NN = (((1,), (0,)), ((), ()))
MB = 1024 * 1024


def dot(a, b, dims):
    return lax.dot_general(a, b, dims, preferred_element_type=F32)


def params(megabytes):
    return pltpu.CompilerParams(vmem_limit_bytes=megabytes * MB)


def in_three(x):
    high = x.astype(BF16).astype(F32)
    rest = x - high
    middle = rest.astype(BF16).astype(F32)
    return high, middle, rest - middle


def embed_kernel(place_ref, pixels_ref, weight_ref, shift_ref, query_ref, keep_ref, send_ref, embedded, scores):
    member = pl.program_id(0)
    core = place_ref[0]
    count = embedded.shape[0]
    width = weight_ref.shape[2]
    heads = query_ref.shape[0]
    rows = pixels_ref.shape[2]
    chosen = lax.broadcasted_iota(jnp.int32, shift_ref.shape, 0) == member
    shift = jnp.sum(jnp.where(chosen, shift_ref[...].astype(F32), 0.0), axis=0, keepdims=True)
    step = 1024
    total = jnp.zeros((rows, heads), F32)
    for at in range(0, width, step):
        block = dot(pixels_ref[0], weight_ref[0, :, at : at + step], TN)
        block = (block + shift[:, at : at + step]).astype(BF16)
        embedded[member, :, at : at + step] = block
        total = total + dot(block, query_ref[:, at : at + step], NT)
    scores[member] = total / math.sqrt(HD)

    def split(value, cols):
        for at in range(0, rows, 16):
            even, odd = value[at : at + 8], value[at + 8 : at + 16]
            to = at // 2
            keep_ref[to : to + 8, cols] = jnp.where(core == 0, even, odd)
            send_ref[to : to + 8, cols] = jnp.where(core == 0, odd, even)

    @pl.when(member == count - 1)
    def _():
        every = scores[...]
        peak = jnp.max(every, axis=0)
        weights = jnp.exp(every - peak[None])
        total = jnp.sum(weights, axis=0)
        for h in range(heads):
            cols = slice(h * HD, (h + 1) * HD)
            numer = weights[0][:, h : h + 1] * embedded[0, :, cols].astype(F32)
            for v in range(1, count):
                numer = numer + weights[v][:, h : h + 1] * embedded[v, :, cols].astype(F32)
            split(numer, cols)
        blank = jnp.zeros_like(peak)
        split(jnp.concatenate([peak, total, blank, blank], axis=1), slice(width, width + 128))


def embed(place, pixels, weight, shift, query):
    count, depth, rows = pixels.shape
    width = weight.shape[2]
    heads = query.shape[0]
    half = jax.ShapeDtypeStruct((rows // 2, width + 128), F32)
    return pl.pallas_call(
        embed_kernel,
        grid=(count,),
        in_specs=[
            pl.BlockSpec(memory_space=pltpu.SMEM),
            pl.BlockSpec((1, depth, rows), lambda v: (v, 0, 0)),
            pl.BlockSpec((1, depth, width), lambda v: (v, 0, 0)),
            pl.BlockSpec((count, width), lambda v: (0, 0)),
            pl.BlockSpec((heads, width), lambda v: (0, 0)),
        ],
        out_specs=[pl.BlockSpec((rows // 2, width + 128), lambda v: (0, 0))] * 2,
        out_shape=[half, half],
        scratch_shapes=[
            pltpu.VMEM((count, rows, width), BF16),
            pltpu.VMEM((count, rows, heads), F32),
        ],
        compiler_params=params(56),
        name="embed",
    )(place, pixels, weight, shift, query)


def pair_kernel(mine_ref, other_ref, out_ref):
    rows, padded = mine_ref.shape
    width = padded - 128
    heads = width // HD
    mine, other = mine_ref[:, width:], other_ref[:, width:]
    peak_a, total_a = mine[:, :32], mine[:, 32:64]
    peak_b, total_b = other[:, :32], other[:, 32:64]
    top = jnp.maximum(peak_a, peak_b)
    scale_a = jnp.exp(peak_a - top)
    scale_b = jnp.exp(peak_b - top)
    for h in range(heads):
        cols = slice(h * HD, (h + 1) * HD)
        numer = mine_ref[:, cols] * scale_a[:, h : h + 1] + other_ref[:, cols] * scale_b[:, h : h + 1]
        out_ref[:, cols] = numer.astype(BF16)
    p0, p1, p2 = in_three(top)
    t0, t1, t2 = in_three(total_a * scale_a + total_b * scale_b)
    blank = jnp.zeros_like(top)
    out_ref[:, width : width + 128] = jnp.concatenate([p0, p1, p2, t0], axis=1).astype(BF16)
    out_ref[:, width + 128 : width + 256] = jnp.concatenate(
        [t1, t2, blank, blank], axis=1
    ).astype(BF16)


def pair(mine, other):
    rows, padded = mine.shape
    return pl.pallas_call(
        pair_kernel,
        out_shape=jax.ShapeDtypeStruct((rows, padded + 128), BF16),
        compiler_params=params(12),
        name="pair",
    )(mine, other)


def merge_kernel(place_ref, parts_ref, gain_ref, normed_ref, keep_ref, send_ref, whole):
    x_hi = place_ref[1]
    rows, padded = parts_ref.shape
    width = padded - 256
    heads = width // HD
    share = 8
    sources = rows // share
    stats = parts_ref[:, width:].astype(F32)
    peak = stats[:, 0:32] + stats[:, 32:64] + stats[:, 64:96]
    total = stats[:, 96:128] + stats[:, 128:160] + stats[:, 160:192]
    peak = peak.reshape(sources, share, heads)
    total = total.reshape(sources, share, heads)
    top = jnp.max(peak, axis=0)
    scale = jnp.exp(peak - top[None])
    total = jnp.sum(total * scale, axis=0)
    scale = scale.reshape(rows, heads)
    sums = jnp.zeros((share, HD), F32)
    for h in range(heads):
        cols = slice(h * HD, (h + 1) * HD)
        numer = jnp.zeros((share, HD), F32)
        for at in range(0, rows, 16):
            block = parts_ref[at : at + 16, cols].astype(F32) * scale[at : at + 16, h : h + 1]
            numer = numer + block[:8] + block[8:]
        value = (numer / total[:, h : h + 1]).astype(BF16).astype(F32)
        whole[:, cols] = value
        sums = sums + value
    half = width // 2
    for at in range(0, half, 512):
        for side in range(2):
            low = slice(at + side * 128, at + side * 128 + 128)
            high = slice(at + side * 128 + 256, at + side * 128 + 384)
            first = jnp.concatenate([whole[:, low], whole[:, high]], axis=0)
            low = slice(half + at + side * 128, half + at + side * 128 + 128)
            high = slice(half + at + side * 128 + 256, half + at + side * 128 + 384)
            second = jnp.concatenate([whole[:, low], whole[:, high]], axis=0)
            to = at // 512 * 16
            cols = slice(side * 128, side * 128 + 128)
            keep_ref[to : to + 16, cols] = jnp.where(x_hi == 0, first, second).astype(BF16)
            send_ref[to : to + 16, cols] = jnp.where(x_hi == 0, second, first).astype(BF16)
    center = jnp.sum(sums, axis=1, keepdims=True) / width
    squares = jnp.zeros((share, HD), F32)
    for h in range(heads):
        shifted = whole[:, h * HD : (h + 1) * HD] - center
        squares = squares + shifted * shifted
    factor = lax.rsqrt(jnp.sum(squares, axis=1, keepdims=True) / width + EPS)
    for h in range(heads):
        cols = slice(h * HD, (h + 1) * HD)
        value = (whole[:, cols] - center) * factor * gain_ref[:, cols].astype(F32)
        twice = jnp.concatenate([value, value], axis=0).astype(BF16)
        for at in range(0, normed_ref.shape[0], 16):
            normed_ref[at : at + 16, cols] = twice


def merge(place, parts, gain, copies):
    rows, padded = parts.shape
    width = padded - 256
    vmem = pl.BlockSpec(memory_space=pltpu.VMEM)
    return pl.pallas_call(
        merge_kernel,
        in_specs=[pl.BlockSpec(memory_space=pltpu.SMEM), vmem, vmem],
        out_shape=(
            jax.ShapeDtypeStruct((copies * 8, width), BF16),
            jax.ShapeDtypeStruct((64, 256), BF16),
            jax.ShapeDtypeStruct((64, 256), BF16),
        ),
        scratch_shapes=[pltpu.VMEM((8, width), F32)],
        compiler_params=params(12),
        name="merge",
    )(place, parts, gain)


def qkv_kernel(place_ref, mine_ref, other_ref, weight_ref, keep_q, keep_kv, send_q, send_kv, tokens):
    step = pl.program_id(0)
    core = place_ref[0]
    x_hi = place_ref[1]
    half = mine_ref.shape[0]

    @pl.when(step == 0)
    def _():
        tokens[pl.ds(pl.multiple_of(core * half, half), half), :] = mine_ref[...]
        tokens[pl.ds(pl.multiple_of((1 - core) * half, half), half), :] = other_ref[...]

    made = dot(tokens[...], weight_ref[0], NN)
    first, second = made[:, :HD], made[:, HD:]
    keep = jnp.where(x_hi == 0, first, second).astype(BF16)
    send = jnp.where(x_hi == 0, second, first).astype(BF16)

    @pl.when(step == 0)
    def _():
        keep_q[...] = keep
        send_q[...] = send

    for part in (1, 2):

        @pl.when(step == part)
        def _():
            cols = slice((part - 1) * HD, part * HD)
            keep_kv[:, cols] = keep
            send_kv[:, cols] = send


def project(place, mine, other, weight):
    half, width = mine.shape
    cols = weight.shape[2]
    rows = 2 * half
    whole = lambda s: (0, 0)
    shapes = [(rows, HD), (rows, 2 * HD)] * 2
    return pl.pallas_call(
        qkv_kernel,
        grid=(3,),
        in_specs=[
            pl.BlockSpec(memory_space=pltpu.SMEM),
            pl.BlockSpec((half, width), whole),
            pl.BlockSpec((half, width), whole),
            pl.BlockSpec((1, width, cols), lambda s: (s, 0, 0)),
        ],
        out_specs=[pl.BlockSpec(shape, whole) for shape in shapes],
        out_shape=[jax.ShapeDtypeStruct(shape, BF16) for shape in shapes],
        scratch_shapes=[pltpu.VMEM((rows, width), BF16)],
        compiler_params=params(16),
        name="project",
    )(place, mine, other, weight)


def attend_kernel(place_ref, keep_ref, got_ref, band_ref, out_ref, kept_ref, scores):
    x_hi = place_ref[1]
    z = place_ref[2]
    bands = band_ref.shape[0]
    mixed = []
    for side in range(2):
        query = jnp.where(x_hi == side, keep_ref[...], got_ref[...])
        for band in range(bands):
            scores[:, band * 256 : band * 256 + 256] = dot(
                query, band_ref[band, :256, :HD], NT
            ) / math.sqrt(HD)
        every = scores[...]
        peak = jnp.max(every, axis=1, keepdims=True)
        weights = jnp.exp(every - peak)
        total = jnp.sum(weights, axis=1, keepdims=True)
        weights = weights.astype(BF16)
        update = jnp.zeros((query.shape[0], HD), F32)
        for band in range(bands):
            update = update + dot(
                weights[:, band * 256 : band * 256 + 256], band_ref[band, :256, HD:], NN
            )
        mixed.append(update / total)
    for chip in range(8):
        for core in range(2):
            at = core * 64 + chip * 8
            to = (chip * 2 + core) * 16
            out_ref[to : to + 16, :] = jnp.concatenate(
                [mixed[0][at : at + 8], mixed[1][at : at + 8]], axis=0
            ).astype(BF16)
    for band in range(bands):
        rows = band_ref[band, pl.ds(pl.multiple_of(256 + z * 16, 16), 16), :].astype(F32)
        mine, other = rows[:8], rows[8:]
        first = jnp.where(x_hi == 0, mine, other)
        second = jnp.where(x_hi == 0, other, mine)
        kept_ref[band * 16 : band * 16 + 16, :] = jnp.concatenate([first, second], axis=0).astype(BF16)


def attend(place, keep, got, bands):
    return pl.pallas_call(
        attend_kernel,
        in_specs=[pl.BlockSpec(memory_space=pltpu.SMEM)] + [pl.BlockSpec(memory_space=pltpu.VMEM)] * 3,
        out_shape=(
            jax.ShapeDtypeStruct((256, HD), BF16),
            jax.ShapeDtypeStruct((128, 256), BF16),
        ),
        scratch_shapes=[pltpu.VMEM((128, 2048), F32)],
        compiler_params=params(16),
        name="attend",
    )(place, keep, got, bands)


def output_kernel(place_ref, parts_ref, kept_ref, mine_ref, other_ref, out_ref, attended):
    core = place_ref[0]
    x_hi = place_ref[1]
    bands = parts_ref.shape[0]
    half = mine_ref.shape[0]
    for side in range(2):
        owner = core if side == 0 else 1 - core
        for chip in range(8):
            for parity in range(2):
                place = jnp.where(x_hi == parity, 0, 256) + (2 * chip + owner) * 16
                place = pl.multiple_of(place, 16)
                to = side * half + chip * 256 + parity * HD
                for band in range(bands):
                    attended[band * 16 : band * 16 + 16, to : to + HD] = parts_ref[
                        band, pl.ds(place, 16), :
                    ]
    product = dot(attended[:, :half], mine_ref[...], NN) + dot(attended[:, half:], other_ref[...], NN)
    layer = (kept_ref[...].astype(F32) + product).astype(BF16)
    rows = layer.shape[0]
    for copy in range(out_ref.shape[0] // rows):
        out_ref[copy * rows : (copy + 1) * rows, :] = layer


def output(place, parts, kept, mine, other, copies):
    half, cols = mine.shape
    rows = kept.shape[0]
    return pl.pallas_call(
        output_kernel,
        in_specs=[pl.BlockSpec(memory_space=pltpu.SMEM)] + [pl.BlockSpec(memory_space=pltpu.VMEM)] * 4,
        out_shape=jax.ShapeDtypeStruct((copies * rows, cols), BF16),
        scratch_shapes=[pltpu.VMEM((rows, 2 * half), BF16)],
        compiler_params=params(12),
        name="output",
    )(place, parts, kept, mine, other)


def swap(x, axis, pieces=1):
    rows = x.shape[0] // pieces
    parts = [
        lax.ppermute(x[k * rows : (k + 1) * rows], axis, [(0, 1), (1, 0)]) for k in range(pieces)
    ]
    return parts[0] if pieces == 1 else jnp.concatenate(parts, axis=0)


def exchange(x, axes):
    return lax.all_to_all(x, axes, 0, 0, tiled=True)


def body(patches, patch_weight, var_embed, agg_query, norm_gain, qkv_weight, out_weight, head_cot):
    core, x_hi, z = lax.axis_index("c"), lax.axis_index("xh"), lax.axis_index("z")
    place = jnp.stack([core, x_hi, z]).astype(jnp.int32)
    width = out_weight.shape[1]

    cot = lax.all_gather(head_cot, "z", axis=0, tiled=True)
    cols = lax.dynamic_slice_in_dim(out_weight, (x_hi * 8 + z) * 256, 256, 1)
    cols = lax.all_gather(cols, CHIPS, axis=0, tiled=True)
    other_cols = swap(cols, "c", 2)
    other_cot = swap(cot, "xh", 4)
    both = jnp.stack([jnp.where(x_hi == 0, cot, other_cot), jnp.where(x_hi == 0, other_cot, cot)])
    both = both.reshape(2, 8, 8, 2, 8, 384).transpose(3, 2, 1, 0, 4, 5).reshape(2, 1024, 384)
    first = lax.dynamic_index_in_dim(both, core, 0, keepdims=False)
    second = lax.dynamic_index_in_dim(both, 1 - core, 0, keepdims=False)

    keep, send = embed(place, patches.transpose(0, 2, 1), patch_weight, var_embed, agg_query.T)
    parts = pair(keep, swap(send, "c"))
    parts = exchange(parts, CHIPS)
    normed, kept, kept_send = merge(place, parts, norm_gain.reshape(1, width), 8)
    kept_got = swap(kept_send, "xh")
    normed = exchange(normed, CHIPS)
    query, kv, query_send, kv_send = project(
        place, normed, swap(normed, "c"), qkv_weight.transpose(1, 0, 2)
    )
    kv_got = swap(kv_send, "xh")
    query_got = swap(query_send, "xh")
    residual = jnp.stack([kept.reshape(8, 8, 256), kept_got.reshape(8, 8, 256)], axis=1)
    block = jnp.concatenate([kv, kv_got, residual.reshape(128, 256)], axis=0)
    bands = lax.all_gather(block, "z", axis=0, tiled=False)
    attended, kept = attend(place, query, query_got, bands)
    attended = exchange(attended, VAR)
    attended = jnp.concatenate([attended, swap(attended, "xh", 2)], axis=0)
    attended = lax.all_gather(attended, "z", axis=0, tiled=False)
    layer = output(place, attended, kept, cols, other_cols, 8)
    layer = exchange(layer, CHIPS)
    return dot(layer, first, TN) + dot(swap(layer, "c"), second, TN)


def solution(mesh):
    whole = Mesh(mesh.devices.reshape(4, 2, 2, 2, 8), ("y", "xl", "c", "xh", "z"))
    return jax.shard_map(
        body,
        mesh=whole,
        in_specs=(
            P(VAR, SEQ, None),
            P(VAR, None, None),
            P(VAR, None),
            P(),
            P(),
            P(None, None, VAR),
            P(VAR, None),
            P(SEQ, VAR),
        ),
        out_specs=P(SEQ, VAR),
        check_vma=False,
    )
```

```python
import math

import jax
import jax.numpy as jnp
from jax import lax
from jax.experimental import pallas as pl
from jax.experimental.pallas import tpu as pltpu
from jax.sharding import Mesh, PartitionSpec as P

EPS = 1e-05
HD = 128
F32 = jnp.float32
BF16 = jnp.bfloat16
VAR = ("y", "xl", "c")
CHIPS = ("y", "xl")
SEQ = ("xh", "z")
NT = (((1,), (1,)), ((), ()))
TN = (((0,), (0,)), ((), ()))
NN = (((1,), (0,)), ((), ()))
MB = 1024 * 1024


def dot(a, b, dims):
    return lax.dot_general(a, b, dims, preferred_element_type=F32)


def params(megabytes):
    return pltpu.CompilerParams(vmem_limit_bytes=megabytes * MB)


def in_three(x):
    high = x.astype(BF16).astype(F32)
    rest = x - high
    middle = rest.astype(BF16).astype(F32)
    return high, middle, rest - middle


def embed_kernel(place_ref, pixels_ref, weight_ref, shift_ref, query_ref, keep_ref, send_ref, embedded, scores):
    member = pl.program_id(0)
    core = place_ref[0]
    count = embedded.shape[0]
    width = weight_ref.shape[2]
    heads = query_ref.shape[0]
    rows = pixels_ref.shape[2]
    chosen = lax.broadcasted_iota(jnp.int32, shift_ref.shape, 0) == member
    shift = jnp.sum(jnp.where(chosen, shift_ref[...].astype(F32), 0.0), axis=0, keepdims=True)
    step = 1024
    total = jnp.zeros((rows, heads), F32)
    for at in range(0, width, step):
        block = dot(pixels_ref[0], weight_ref[0, :, at : at + step], TN)
        block = (block + shift[:, at : at + step]).astype(BF16)
        embedded[member, :, at : at + step] = block
        total = total + dot(block, query_ref[:, at : at + step], NT)
    scores[member] = total / math.sqrt(HD)

    def split(value, cols):
        for at in range(0, rows, 16):
            even, odd = value[at : at + 8], value[at + 8 : at + 16]
            to = at // 2
            keep_ref[to : to + 8, cols] = jnp.where(core == 0, even, odd)
            send_ref[to : to + 8, cols] = jnp.where(core == 0, odd, even)

    @pl.when(member == count - 1)
    def _():
        every = scores[...]
        peak = jnp.max(every, axis=0)
        weights = jnp.exp(every - peak[None])
        total = jnp.sum(weights, axis=0)
        for h in range(heads):
            cols = slice(h * HD, (h + 1) * HD)
            numer = weights[0][:, h : h + 1] * embedded[0, :, cols].astype(F32)
            for v in range(1, count):
                numer = numer + weights[v][:, h : h + 1] * embedded[v, :, cols].astype(F32)
            split(numer, cols)
        blank = jnp.zeros_like(peak)
        split(jnp.concatenate([peak, total, blank, blank], axis=1), slice(width, width + 128))


def embed(place, pixels, weight, shift, query):
    count, depth, rows = pixels.shape
    width = weight.shape[2]
    heads = query.shape[0]
    half = jax.ShapeDtypeStruct((rows // 2, width + 128), F32)
    return pl.pallas_call(
        embed_kernel,
        grid=(count,),
        in_specs=[
            pl.BlockSpec(memory_space=pltpu.SMEM),
            pl.BlockSpec((1, depth, rows), lambda v: (v, 0, 0)),
            pl.BlockSpec((1, depth, width), lambda v: (v, 0, 0)),
            pl.BlockSpec((count, width), lambda v: (0, 0)),
            pl.BlockSpec((heads, width), lambda v: (0, 0)),
        ],
        out_specs=[pl.BlockSpec((rows // 2, width + 128), lambda v: (0, 0))] * 2,
        out_shape=[half, half],
        scratch_shapes=[
            pltpu.VMEM((count, rows, width), BF16),
            pltpu.VMEM((count, rows, heads), F32),
        ],
        compiler_params=params(56),
        name="embed",
    )(place, pixels, weight, shift, query)


def pair_kernel(mine_ref, other_ref, out_ref):
    rows, padded = mine_ref.shape
    width = padded - 128
    heads = width // HD
    mine, other = mine_ref[:, width:], other_ref[:, width:]
    peak_a, total_a = mine[:, :32], mine[:, 32:64]
    peak_b, total_b = other[:, :32], other[:, 32:64]
    top = jnp.maximum(peak_a, peak_b)
    scale_a = jnp.exp(peak_a - top)
    scale_b = jnp.exp(peak_b - top)
    for h in range(heads):
        cols = slice(h * HD, (h + 1) * HD)
        numer = mine_ref[:, cols] * scale_a[:, h : h + 1] + other_ref[:, cols] * scale_b[:, h : h + 1]
        out_ref[:, cols] = numer.astype(BF16)
    p0, p1, p2 = in_three(top)
    t0, t1, t2 = in_three(total_a * scale_a + total_b * scale_b)
    blank = jnp.zeros_like(top)
    out_ref[:, width : width + 128] = jnp.concatenate([p0, p1, p2, t0], axis=1).astype(BF16)
    out_ref[:, width + 128 : width + 256] = jnp.concatenate(
        [t1, t2, blank, blank], axis=1
    ).astype(BF16)


def pair(mine, other):
    rows, padded = mine.shape
    return pl.pallas_call(
        pair_kernel,
        out_shape=jax.ShapeDtypeStruct((rows, padded + 128), BF16),
        compiler_params=params(12),
        name="pair",
    )(mine, other)


def merge_kernel(parts_ref, gain_ref, normed_ref, kept_ref, whole):
    rows, padded = parts_ref.shape
    width = padded - 256
    heads = width // HD
    share = 8
    sources = rows // share
    stats = parts_ref[:, width:].astype(F32)
    peak = stats[:, 0:32] + stats[:, 32:64] + stats[:, 64:96]
    total = stats[:, 96:128] + stats[:, 128:160] + stats[:, 160:192]
    peak = peak.reshape(sources, share, heads)
    total = total.reshape(sources, share, heads)
    top = jnp.max(peak, axis=0)
    scale = jnp.exp(peak - top[None])
    total = jnp.sum(total * scale, axis=0)
    scale = scale.reshape(rows, heads)
    sums = jnp.zeros((share, HD), F32)
    last = None
    for h in range(heads):
        cols = slice(h * HD, (h + 1) * HD)
        numer = jnp.zeros((share, HD), F32)
        for at in range(0, rows, 16):
            block = parts_ref[at : at + 16, cols].astype(F32) * scale[at : at + 16, h : h + 1]
            numer = numer + block[:8] + block[8:]
        value = (numer / total[:, h : h + 1]).astype(BF16).astype(F32)
        whole[:, cols] = value
        sums = sums + value
        if h % 2 == 0:
            last = value
        else:
            block = h // 2
            to = (block % 8 * 2 + block // 8) * 16
            kept_ref[to : to + 16, :] = jnp.concatenate([last, value], axis=0).astype(BF16)
    center = jnp.sum(sums, axis=1, keepdims=True) / width
    squares = jnp.zeros((share, HD), F32)
    for h in range(heads):
        shifted = whole[:, h * HD : (h + 1) * HD] - center
        squares = squares + shifted * shifted
    factor = lax.rsqrt(jnp.sum(squares, axis=1, keepdims=True) / width + EPS)
    for h in range(heads):
        cols = slice(h * HD, (h + 1) * HD)
        value = (whole[:, cols] - center) * factor * gain_ref[:, cols].astype(F32)
        twice = jnp.concatenate([value, value], axis=0).astype(BF16)
        for at in range(0, normed_ref.shape[0], 16):
            normed_ref[at : at + 16, cols] = twice


def merge(parts, gain, copies):
    rows, padded = parts.shape
    width = padded - 256
    return pl.pallas_call(
        merge_kernel,
        out_shape=(
            jax.ShapeDtypeStruct((copies * 8, width), BF16),
            jax.ShapeDtypeStruct((width // 16, HD), BF16),
        ),
        scratch_shapes=[pltpu.VMEM((8, width), F32)],
        compiler_params=params(12),
        name="merge",
    )(parts, gain)


def qkv_kernel(
    place_ref, mine_ref, other_ref, weight_ref, tie_ref, kv_ref, keep_ref, send_ref, tokens
):
    step = pl.program_id(0)
    core = place_ref[0]
    x_hi = place_ref[1]
    half = mine_ref.shape[0]
    rows = 2 * half

    @pl.when(step == 0)
    def _():
        tokens[pl.ds(pl.multiple_of(core * half, half), half), :] = mine_ref[...]
        tokens[pl.ds(pl.multiple_of((1 - core) * half, half), half), :] = other_ref[...]

    made = dot(tokens[...], weight_ref[0], NN)
    first, second = made[:, :HD], made[:, HD:]

    @pl.when(step == 0)
    def _():
        keep_ref[...] = jnp.where(x_hi == 0, first, second).astype(BF16)
        send_ref[...] = jnp.where(x_hi == 0, second, first).astype(BF16)

    for part in (1, 2):

        @pl.when(step == part)
        def _():
            cols = slice((part - 1) * HD, part * HD)
            for to in range(16):
                value = first if to < 8 else second
                kv_ref[to * rows : (to + 1) * rows, cols] = value.astype(BF16)


def project(place, mine, other, weight, tie):
    half, width = mine.shape
    cols = weight.shape[2]
    rows = 2 * half
    whole = lambda s: (0, 0)
    shapes = [(16 * rows, 2 * HD), (rows, HD), (rows, HD)]
    return pl.pallas_call(
        qkv_kernel,
        grid=(3,),
        in_specs=[
            pl.BlockSpec(memory_space=pltpu.SMEM),
            pl.BlockSpec((half, width), whole),
            pl.BlockSpec((half, width), whole),
            pl.BlockSpec((1, width, cols), lambda s: (s, 0, 0)),
            pl.BlockSpec(memory_space=pltpu.HBM),
        ],
        out_specs=[pl.BlockSpec(shape, whole) for shape in shapes],
        out_shape=[jax.ShapeDtypeStruct(shape, BF16) for shape in shapes],
        scratch_shapes=[pltpu.VMEM((rows, width), BF16)],
        compiler_params=params(16),
        name="project",
    )(place, mine, other, weight, tie)


def attend_kernel(place_ref, keep_ref, got_ref, kv_ref, out_ref, scores):
    x_hi = place_ref[1]
    count = kv_ref.shape[0]
    step = 256
    mixed = []
    for side in range(2):
        query = jnp.where(x_hi == side, keep_ref[...], got_ref[...])
        for at in range(0, count, step):
            scores[:, at : at + step] = dot(query, kv_ref[at : at + step, :HD], NT) / math.sqrt(HD)
        every = scores[...]
        peak = jnp.max(every, axis=1, keepdims=True)
        weights = jnp.exp(every - peak)
        total = jnp.sum(weights, axis=1, keepdims=True)
        mixed.append(dot(weights.astype(BF16), kv_ref[:, HD:], NN) / total)
    for chip in range(8):
        for core in range(2):
            at = core * 64 + chip * 8
            to = (chip * 2 + core) * 16
            out_ref[to : to + 16, :] = jnp.concatenate(
                [mixed[0][at : at + 8], mixed[1][at : at + 8]], axis=0
            ).astype(BF16)


def attend(place, keep, got, kv):
    return pl.pallas_call(
        attend_kernel,
        in_specs=[pl.BlockSpec(memory_space=pltpu.SMEM)] + [pl.BlockSpec(memory_space=pltpu.VMEM)] * 3,
        out_shape=jax.ShapeDtypeStruct((256, HD), BF16),
        scratch_shapes=[pltpu.VMEM((128, 2048), F32)],
        compiler_params=params(16),
        name="attend",
    )(place, keep, got, kv)


def output_kernel(parts_ref, weight_ref, out_ref, attended):
    bands = parts_ref.shape[0]
    cols = weight_ref.shape[1]
    for band in range(0, bands, 2):
        to = band * 8
        for source in range(16):
            at = source * 16
            a = parts_ref[band, at : at + 16, :].astype(F32)
            b = parts_ref[band + 1, at : at + 16, :].astype(F32)
            for x_hi in range(2):
                head = 2 * source + x_hi
                rows = slice(x_hi * 8, x_hi * 8 + 8)
                attended[to : to + 16, head * HD : (head + 1) * HD] = jnp.concatenate(
                    [a[rows], b[rows]], axis=0
                ).astype(BF16)
    product = dot(attended[...], weight_ref[...], NN)
    half = cols // 2
    count = out_ref.shape[0] // 64
    for band in range(0, bands, 2):
        residual = []
        for b in (band, band + 1):
            kept = parts_ref[b, 256:288, :].astype(F32)
            residual.append(
                jnp.concatenate([kept[k : k + 8] for k in range(0, 32, 8)], axis=1)
            )
        at = band * 8
        layer = (jnp.concatenate(residual, axis=0) + product[at : at + 16]).astype(BF16)
        for to in range(count):
            side = to % 2
            out_ref[to * 64 + at : to * 64 + at + 16, :] = layer[:, side * half : (side + 1) * half]


def output(parts, weight):
    width, cols = weight.shape
    return pl.pallas_call(
        output_kernel,
        out_shape=jax.ShapeDtypeStruct((16 * 64, cols // 2), BF16),
        scratch_shapes=[pltpu.VMEM((64, width), BF16)],
        compiler_params=params(12),
        name="output",
    )(parts, weight)


def swap(x, axis):
    return lax.ppermute(x, axis, [(0, 1), (1, 0)])


def exchange(x, axes):
    return lax.all_to_all(x, axes, 0, 0, tiled=True)


def body(patches, patch_weight, var_embed, agg_query, norm_gain, qkv_weight, out_weight, head_cot):
    core, x_hi, z = lax.axis_index("c"), lax.axis_index("xh"), lax.axis_index("z")
    place = jnp.stack([core, x_hi, z]).astype(jnp.int32)
    width = out_weight.shape[1]

    other_cot = swap(head_cot, "xh")
    cot = jnp.stack([jnp.where(x_hi == 0, head_cot, other_cot), jnp.where(x_hi == 0, other_cot, head_cot)])
    cot = lax.all_gather(cot.reshape(256, 384), "z", axis=0, tiled=True)
    cols = jnp.concatenate(
        [lax.dynamic_slice_in_dim(out_weight, side * 2048 + z * 256, 256, 1) for side in range(2)],
        axis=1,
    )
    cols = lax.all_gather(cols, VAR, axis=0, tiled=True)

    keep, send = embed(place, patches.transpose(0, 2, 1), patch_weight, var_embed, agg_query.T)
    parts = pair(keep, swap(send, "c"))
    parts = exchange(parts, CHIPS)
    normed, kept = merge(parts, norm_gain.reshape(1, width), 8)
    normed = exchange(normed, CHIPS)
    kv, query, query_send = project(
        place, normed, swap(normed, "c"), qkv_weight.transpose(1, 0, 2), cot
    )
    query_got = swap(query_send, "xh")
    kv = exchange(kv, SEQ)
    attended = attend(place, query, query_got, kv)
    attended = exchange(attended, VAR + ("xh",))
    sent = jnp.concatenate(
        [jnp.broadcast_to(attended[None], (8, 256, HD)), kept.reshape(8, 32, HD)], axis=1
    )
    got = exchange(sent, "z")
    layer = output(got, cols)
    layer = exchange(layer, CHIPS + ("xh",))
    cot = cot.reshape(8, 2, 8, 2, 8, 384).transpose(3, 2, 1, 0, 4, 5).reshape(2, 1024, 384)
    first = lax.dynamic_index_in_dim(cot, core, 0, keepdims=False)
    second = lax.dynamic_index_in_dim(cot, 1 - core, 0, keepdims=False)
    return dot(layer, first, TN) + dot(swap(layer, "c"), second, TN)


def solution(mesh):
    whole = Mesh(mesh.devices.reshape(4, 2, 2, 2, 8), ("y", "xl", "c", "xh", "z"))
    return jax.shard_map(
        body,
        mesh=whole,
        in_specs=(
            P(VAR, SEQ, None),
            P(VAR, None, None),
            P(VAR, None),
            P(),
            P(),
            P(None, None, VAR),
            P(VAR, None),
            P(SEQ, VAR),
        ),
        out_specs=P(SEQ, VAR),
        check_vma=False,
    )
```

```python
import math

import jax
import jax.numpy as jnp
from jax import lax
from jax.experimental import pallas as pl
from jax.experimental.pallas import tpu as pltpu
from jax.sharding import Mesh, PartitionSpec as P

EPS = 1e-05
HD = 128
F32 = jnp.float32
BF16 = jnp.bfloat16
VAR = ("y", "xl", "c")
CHIPS = ("y", "xl")
SEQ = ("xh", "zq", "z0")
BANDS = ("xh", "zq")
NT = (((1,), (1,)), ((), ()))
TN = (((0,), (0,)), ((), ()))
NN = (((1,), (0,)), ((), ()))
MB = 1024 * 1024


def dot(a, b, dims):
    return lax.dot_general(a, b, dims, preferred_element_type=F32)


def params(megabytes):
    return pltpu.CompilerParams(vmem_limit_bytes=megabytes * MB)


def in_three(x):
    high = x.astype(BF16).astype(F32)
    rest = x - high
    middle = rest.astype(BF16).astype(F32)
    return high, middle, rest - middle


def packed(peak, total):
    p0, p1, p2 = in_three(peak)
    t0, t1, t2 = in_three(total)
    blank = jnp.zeros_like(peak)
    parts = [p0, p1, p2, t0, t1, t2, blank, blank]
    return jnp.concatenate(parts, axis=1).astype(BF16)


def unpacked(stats):
    stats = stats.astype(F32)
    peak = stats[:, 0:32] + stats[:, 32:64] + stats[:, 64:96]
    total = stats[:, 96:128] + stats[:, 128:160] + stats[:, 160:192]
    return peak, total


def embed_kernel(pixels_ref, weight_ref, shift_ref, query_ref, keep_ref, send_ref, embedded, scores, held, sems):
    core = lax.axis_index("c")
    count, rows, width = embedded.shape
    heads = query_ref.shape[0]
    half = rows // 2
    copies = [
        pltpu.make_async_copy(weight_ref.at[v], held.at[v], sems.at[v]) for v in range(count)
    ]
    for copy in copies:
        copy.start()
    new = lax.broadcasted_iota(jnp.int32, (rows, rows), 0)
    old = lax.broadcasted_iota(jnp.int32, (rows, rows), 1)
    group = (new % half) // 8 * 2 + jnp.where(new < half, core, 1 - core)
    order = jnp.where(old == group * 8 + new % 8, 1.0, 0.0).astype(BF16)
    step = 1024
    for v in range(count):
        tokens = dot(order, pixels_ref[v], NT).astype(BF16)
        copies[v].wait()
        total = jnp.zeros((rows, heads), F32)
        for at in range(0, width, step):
            block = dot(tokens, held[v, :, at : at + step], NN)
            shift = shift_ref[v : v + 1, at : at + step].astype(F32)
            block = (block + shift).astype(BF16)
            embedded[v, :, at : at + step] = block
            total = total + dot(block, query_ref[:, at : at + step], NT)
        scores[v] = total / math.sqrt(HD)
    every = scores[...]
    peak = jnp.max(every, axis=0)
    weights = jnp.exp(every - peak[None])
    total = jnp.sum(weights, axis=0)
    for h in range(heads):
        cols = slice(h * HD, (h + 1) * HD)
        numer = weights[0][:, h : h + 1] * embedded[0, :, cols].astype(F32)
        for v in range(1, count):
            numer = numer + weights[v][:, h : h + 1] * embedded[v, :, cols].astype(F32)
        keep_ref[:, cols] = numer[:half]
        send_ref[:, cols] = numer[half:].astype(BF16)
    blank = jnp.zeros((half, 128 - 2 * heads), F32)
    keep_ref[:, width:] = jnp.concatenate([peak[:half], total[:half], blank], axis=1)
    send_ref[:, width:] = packed(peak[half:], total[half:])


def embed(pixels, weight, shift, query):
    count, depth, rows = pixels.shape
    width = weight.shape[2]
    heads = query.shape[0]
    vmem = pl.BlockSpec(memory_space=pltpu.VMEM)
    return pl.pallas_call(
        embed_kernel,
        in_specs=[vmem, pl.BlockSpec(memory_space=pltpu.HBM), vmem, vmem],
        out_shape=(
            jax.ShapeDtypeStruct((rows // 2, width + 128), F32),
            jax.ShapeDtypeStruct((rows // 2, width + 256), BF16),
        ),
        scratch_shapes=[
            pltpu.VMEM((count, rows, width), BF16),
            pltpu.VMEM((count, rows, heads), F32),
            pltpu.VMEM((count, depth, width), BF16),
            pltpu.SemaphoreType.DMA((count,)),
        ],
        compiler_params=params(32),
        name="embed",
    )(pixels, weight, shift, query)


def pair_kernel(mine_ref, other_ref, out_ref):
    rows, padded = mine_ref.shape
    width = padded - 128
    heads = width // HD
    mine = mine_ref[:, width:]
    peak_a, total_a = mine[:, :heads], mine[:, heads : 2 * heads]
    peak_b, total_b = unpacked(other_ref[:, width:])
    top = jnp.maximum(peak_a, peak_b)
    scale_a = jnp.exp(peak_a - top)
    scale_b = jnp.exp(peak_b - top)
    for h in range(heads):
        cols = slice(h * HD, (h + 1) * HD)
        first = mine_ref[:, cols] * scale_a[:, h : h + 1]
        second = other_ref[:, cols].astype(F32) * scale_b[:, h : h + 1]
        out_ref[:, cols] = (first + second).astype(BF16)
    out_ref[:, width:] = packed(top, total_a * scale_a + total_b * scale_b)


def pair(mine, other):
    return pl.pallas_call(
        pair_kernel,
        out_shape=jax.ShapeDtypeStruct(other.shape, BF16),
        compiler_params=params(12),
        name="pair",
    )(mine, other)


def merge_kernel(parts_ref, gain_ref, normed_ref, kept_ref, whole):
    rows, padded = parts_ref.shape
    width = padded - 256
    heads = width // HD
    share = 8
    sources = rows // share
    peak, total = unpacked(parts_ref[:, width:])
    peak = peak.reshape(sources, share, heads)
    total = total.reshape(sources, share, heads)
    top = jnp.max(peak, axis=0)
    scale = jnp.exp(peak - top[None])
    total = jnp.sum(total * scale, axis=0)
    scale = scale.reshape(rows, heads)
    sums = jnp.zeros((share, HD), F32)
    last = None
    for h in range(heads):
        cols = slice(h * HD, (h + 1) * HD)
        numer = jnp.zeros((share, HD), F32)
        for at in range(0, rows, 16):
            block = parts_ref[at : at + 16, cols].astype(F32) * scale[at : at + 16, h : h + 1]
            numer = numer + block[:8] + block[8:]
        value = (numer / total[:, h : h + 1]).astype(BF16).astype(F32)
        whole[:, cols] = value
        sums = sums + value
        if h % 2 == 0:
            last = value
        else:
            to = h // 2 * 16
            kept_ref[to : to + 16, :] = jnp.concatenate([last, value], axis=0).astype(BF16)
    center = jnp.sum(sums, axis=1, keepdims=True) / width
    squares = jnp.zeros((share, HD), F32)
    for h in range(heads):
        shifted = whole[:, h * HD : (h + 1) * HD] - center
        squares = squares + shifted * shifted
    factor = lax.rsqrt(jnp.sum(squares, axis=1, keepdims=True) / width + EPS)
    for h in range(heads):
        cols = slice(h * HD, (h + 1) * HD)
        value = (whole[:, cols] - center) * factor * gain_ref[:, cols].astype(F32)
        twice = jnp.concatenate([value, value], axis=0).astype(BF16)
        for at in range(0, normed_ref.shape[0], 16):
            normed_ref[at : at + 16, cols] = twice


def merge(parts, gain, copies):
    rows, padded = parts.shape
    width = padded - 256
    return pl.pallas_call(
        merge_kernel,
        out_shape=(
            jax.ShapeDtypeStruct((copies * 8, width), BF16),
            jax.ShapeDtypeStruct((width // 16, HD), BF16),
        ),
        scratch_shapes=[pltpu.VMEM((8, width), F32)],
        compiler_params=params(12),
        name="merge",
    )(parts, gain)


def qkv_kernel(mine_ref, other_ref, weight_ref, tie_ref, kv_ref, keep_ref, send_ref, tokens, held, sems):
    core = lax.axis_index("c")
    z0 = lax.axis_index("z0")
    half, width = mine_ref.shape
    rows = 2 * half
    parts = sems.shape[1]
    depth = width // parts
    copies = [
        [
            pltpu.make_async_copy(
                weight_ref.at[k, pl.ds(part * depth, depth), :],
                held.at[k, pl.ds(part * depth, depth), :],
                sems.at[k, part],
            )
            for part in range(parts)
        ]
        for k in range(3)
    ]
    for k in range(3):
        for copy in copies[k]:
            copy.start()
    tokens[pl.ds(pl.multiple_of(core * half, half), half), :] = mine_ref[...]
    tokens[pl.ds(pl.multiple_of((1 - core) * half, half), half), :] = other_ref[...]
    for k in range(3):
        made = jnp.zeros((rows, 2 * HD), F32)
        for part in range(parts):
            copies[k][part].wait()
            at = slice(part * depth, (part + 1) * depth)
            made = made + dot(tokens[:, at], held[k, at, :], NN)
        first, second = made[:, :HD], made[:, HD:]
        if k == 0:
            keep_ref[...] = jnp.where(z0 == 0, first, second).astype(BF16)
            send_ref[...] = jnp.where(z0 == 0, second, first).astype(BF16)
        else:
            cols = slice((k - 1) * HD, k * HD)
            for to in range(16):
                value = first if to % 2 == 0 else second
                kv_ref[to * rows : (to + 1) * rows, cols] = value.astype(BF16)


def project(mine, other, weight, tie):
    half, width = mine.shape
    cols = weight.shape[2]
    rows = 2 * half
    parts = 4
    vmem = pl.BlockSpec(memory_space=pltpu.VMEM)
    hbm = pl.BlockSpec(memory_space=pltpu.HBM)
    shapes = [(16 * rows, 2 * HD), (rows, HD), (rows, HD)]
    return pl.pallas_call(
        qkv_kernel,
        in_specs=[vmem, vmem, hbm, hbm],
        out_shape=[jax.ShapeDtypeStruct(shape, BF16) for shape in shapes],
        scratch_shapes=[
            pltpu.VMEM((rows, width), BF16),
            pltpu.VMEM((3, width, cols), BF16),
            pltpu.SemaphoreType.DMA((3, parts)),
        ],
        compiler_params=params(24),
        name="project",
    )(mine, other, weight, tie)


def attend_kernel(keep_ref, got_ref, kv_ref, out_ref, scores):
    z0 = lax.axis_index("z0")
    count = kv_ref.shape[0]
    step = 256
    mixed = []
    for side in range(2):
        query = jnp.where(z0 == side, keep_ref[...], got_ref[...])
        for at in range(0, count, step):
            scores[:, at : at + step] = dot(query, kv_ref[at : at + step, :HD], NT) / math.sqrt(HD)
        every = scores[...]
        peak = jnp.max(every, axis=1, keepdims=True)
        weights = jnp.exp(every - peak)
        total = jnp.sum(weights, axis=1, keepdims=True)
        mixed.append(dot(weights.astype(BF16), kv_ref[:, HD:], NN) / total)
    for chip in range(8):
        for core in range(2):
            at = core * 64 + chip * 8
            to = (chip * 2 + core) * 16
            out_ref[to : to + 16, :] = jnp.concatenate(
                [mixed[0][at : at + 8], mixed[1][at : at + 8]], axis=0
            ).astype(BF16)


def attend(keep, got, kv):
    return pl.pallas_call(
        attend_kernel,
        out_shape=jax.ShapeDtypeStruct((256, HD), BF16),
        scratch_shapes=[pltpu.VMEM((128, 2048), F32)],
        compiler_params=params(16),
        name="attend",
    )(keep, got, kv)


def output_kernel(parts_ref, weight_ref, out_ref, attended, held, sems):
    bands = parts_ref.shape[0]
    width, cols = weight_ref.shape
    pieces = sems.shape[0]
    depth = width // pieces
    copies = [
        pltpu.make_async_copy(
            weight_ref.at[pl.ds(k * depth, depth), :], held.at[pl.ds(k * depth, depth), :], sems.at[k]
        )
        for k in range(pieces)
    ]
    for copy in copies:
        copy.start()
    for band in range(0, bands, 2):
        to = band * 8
        for source in range(16):
            at = source * 16
            a = parts_ref[band, at : at + 16, :].astype(F32)
            b = parts_ref[band + 1, at : at + 16, :].astype(F32)
            for side in range(2):
                head = 2 * source + side
                rows = slice(side * 8, side * 8 + 8)
                attended[to : to + 16, head * HD : (head + 1) * HD] = jnp.concatenate(
                    [a[rows], b[rows]], axis=0
                ).astype(BF16)
    product = jnp.zeros((attended.shape[0], cols), F32)
    for k in range(pieces):
        copies[k].wait()
        at = slice(k * depth, (k + 1) * depth)
        product = product + dot(attended[:, at], held[at, :], NN)
    half = cols // 2
    count = out_ref.shape[0] // 64
    for band in range(0, bands, 2):
        residual = []
        for b in (band, band + 1):
            kept = parts_ref[b, 256:288, :].astype(F32)
            residual.append(
                jnp.concatenate([kept[k : k + 8] for k in range(0, 32, 8)], axis=1)
            )
        at = band * 8
        layer = (jnp.concatenate(residual, axis=0) + product[at : at + 16]).astype(BF16)
        for to in range(count):
            side = to % 2
            out_ref[to * 64 + at : to * 64 + at + 16, :] = layer[:, side * half : (side + 1) * half]


def output(parts, weight):
    width, cols = weight.shape
    return pl.pallas_call(
        output_kernel,
        in_specs=[pl.BlockSpec(memory_space=pltpu.VMEM), pl.BlockSpec(memory_space=pltpu.HBM)],
        out_shape=jax.ShapeDtypeStruct((16 * 64, cols // 2), BF16),
        scratch_shapes=[
            pltpu.VMEM((64, width), BF16),
            pltpu.VMEM((width, cols), BF16),
            pltpu.SemaphoreType.DMA((8,)),
        ],
        compiler_params=params(16),
        name="output",
    )(parts, weight)


def swap(x, axis):
    return lax.ppermute(x, axis, [(0, 1), (1, 0)])


def exchange(x, axes):
    return lax.all_to_all(x, axes, 0, 0, tiled=True)


def body(patches, patch_weight, var_embed, agg_query, norm_gain, qkv_weight, out_weight, head_cot):
    core, z0 = lax.axis_index("c"), lax.axis_index("z0")
    width = out_weight.shape[1]

    keep, send = embed(patches.transpose(0, 2, 1), patch_weight, var_embed, agg_query.T)
    send, cot, cols = lax.optimization_barrier((send, head_cot, out_weight))
    parts = pair(keep, swap(send, "c"))

    other_cot = swap(cot, "z0")
    cot = jnp.stack([jnp.where(z0 == 0, cot, other_cot), jnp.where(z0 == 0, other_cot, cot)])
    cot = lax.all_gather(cot.reshape(256, 384), BANDS, axis=0, tiled=True)
    cols = lax.dynamic_slice_in_dim(cols, lax.axis_index(BANDS) * 512, 512, 1)
    cols = lax.all_gather(cols, VAR, axis=0, tiled=True)

    parts = exchange(parts, CHIPS)
    normed, kept = merge(parts, norm_gain.reshape(1, width), 8)
    normed = exchange(normed, CHIPS)
    kv, query, query_send = project(normed, swap(normed, "c"), qkv_weight.transpose(1, 0, 2), cot)
    query_got = swap(query_send, "z0")
    kv = exchange(kv, SEQ)
    attended = attend(query, query_got, kv)
    attended = exchange(attended, VAR + ("z0",))
    sent = jnp.concatenate(
        [jnp.broadcast_to(attended[None], (8, 256, HD)), kept.reshape(8, 32, HD)], axis=1
    )
    got = exchange(sent, BANDS)
    layer = output(got, cols)
    layer = exchange(layer, CHIPS + ("z0",))
    cot = cot.reshape(8, 2, 8, 2, 8, 384).transpose(3, 2, 1, 0, 4, 5).reshape(2, 1024, 384)
    first = lax.dynamic_index_in_dim(cot, core, 0, keepdims=False)
    second = lax.dynamic_index_in_dim(cot, 1 - core, 0, keepdims=False)
    return dot(layer, first, TN) + dot(swap(layer, "c"), second, TN)


def solution(mesh):
    whole = Mesh(mesh.devices.reshape(4, 2, 2, 2, 4, 2), ("y", "xl", "c", "xh", "zq", "z0"))
    return jax.shard_map(
        body,
        mesh=whole,
        in_specs=(
            P(VAR, SEQ, None),
            P(VAR, None, None),
            P(VAR, None),
            P(),
            P(),
            P(None, None, VAR),
            P(VAR, None),
            P(SEQ, VAR),
        ),
        out_specs=P(SEQ, VAR),
        check_vma=False,
    )
```

```python
import math

import jax
import jax.numpy as jnp
from jax import lax
from jax.experimental import pallas as pl
from jax.experimental.pallas import tpu as pltpu
from jax.sharding import Mesh, PartitionSpec as P

EPS = 1e-05
HD = 128
F32 = jnp.float32
BF16 = jnp.bfloat16
VAR = ("y", "xl", "c")
CHIPS = ("y", "xl")
SEQ = ("xh", "zq", "z0")
BANDS = ("xh", "zq")
NT = (((1,), (1,)), ((), ()))
TN = (((0,), (0,)), ((), ()))
NN = (((1,), (0,)), ((), ()))
MB = 1024 * 1024


def dot(a, b, dims):
    return lax.dot_general(a, b, dims, preferred_element_type=F32)


def params(megabytes):
    return pltpu.CompilerParams(vmem_limit_bytes=megabytes * MB)


def in_three(x):
    high = x.astype(BF16).astype(F32)
    rest = x - high
    middle = rest.astype(BF16).astype(F32)
    return high, middle, rest - middle


def packed(peak, total):
    p0, p1, p2 = in_three(peak)
    t0, t1, t2 = in_three(total)
    blank = jnp.zeros_like(peak)
    parts = [p0, p1, p2, t0, t1, t2, blank, blank]
    return jnp.concatenate(parts, axis=1).astype(BF16)


def unpacked(stats):
    stats = stats.astype(F32)
    peak = stats[:, 0:32] + stats[:, 32:64] + stats[:, 64:96]
    total = stats[:, 96:128] + stats[:, 128:160] + stats[:, 160:192]
    return peak, total


def embed_kernel(pixels_ref, weight_ref, shift_ref, query_ref, keep_ref, send_ref, embedded, scores, held, sems):
    core = lax.axis_index("c")
    count, rows, width = embedded.shape
    heads = query_ref.shape[0]
    half = rows // 2
    copies = [
        pltpu.make_async_copy(weight_ref.at[v], held.at[v], sems.at[v]) for v in range(count)
    ]
    for copy in copies:
        copy.start()
    new = lax.broadcasted_iota(jnp.int32, (rows, rows), 0)
    old = lax.broadcasted_iota(jnp.int32, (rows, rows), 1)
    group = (new % half) // 8 * 2 + jnp.where(new < half, core, 1 - core)
    order = jnp.where(old == group * 8 + new % 8, 1.0, 0.0).astype(BF16)
    step = 1024
    for v in range(count):
        tokens = dot(order, pixels_ref[v], NT).astype(BF16)
        copies[v].wait()
        total = jnp.zeros((rows, heads), F32)
        for at in range(0, width, step):
            block = dot(tokens, held[v, :, at : at + step], NN)
            shift = shift_ref[v : v + 1, at : at + step].astype(F32)
            block = (block + shift).astype(BF16)
            embedded[v, :, at : at + step] = block
            total = total + dot(block, query_ref[:, at : at + step], NT)
        scores[v] = total / math.sqrt(HD)
    every = scores[...]
    peak = jnp.max(every, axis=0)
    weights = jnp.exp(every - peak[None])
    total = jnp.sum(weights, axis=0)
    for h in range(heads):
        cols = slice(h * HD, (h + 1) * HD)
        numer = weights[0][:, h : h + 1] * embedded[0, :, cols].astype(F32)
        for v in range(1, count):
            numer = numer + weights[v][:, h : h + 1] * embedded[v, :, cols].astype(F32)
        keep_ref[:, cols] = numer[:half].astype(BF16)
        send_ref[:, cols] = numer[half:].astype(BF16)
    keep_ref[:, width:] = packed(peak[:half], total[:half])
    send_ref[:, width:] = packed(peak[half:], total[half:])


def embed(pixels, weight, shift, query):
    count, depth, rows = pixels.shape
    width = weight.shape[2]
    heads = query.shape[0]
    vmem = pl.BlockSpec(memory_space=pltpu.VMEM)
    part = jax.ShapeDtypeStruct((rows // 2, width + 256), BF16)
    return pl.pallas_call(
        embed_kernel,
        in_specs=[vmem, pl.BlockSpec(memory_space=pltpu.HBM), vmem, vmem],
        out_shape=(part, part),
        scratch_shapes=[
            pltpu.VMEM((count, rows, width), BF16),
            pltpu.VMEM((count, rows, heads), F32),
            pltpu.VMEM((count, depth, width), BF16),
            pltpu.SemaphoreType.DMA((count,)),
        ],
        compiler_params=params(60),
        name="embed",
    )(pixels, weight, shift, query)


def pair_kernel(mine_ref, other_ref, out_ref):
    rows, padded = mine_ref.shape
    width = padded - 256
    heads = width // HD
    peak_a, total_a = unpacked(mine_ref[:, width:])
    peak_b, total_b = unpacked(other_ref[:, width:])
    top = jnp.maximum(peak_a, peak_b)
    scale_a = jnp.exp(peak_a - top)
    scale_b = jnp.exp(peak_b - top)
    for h in range(heads):
        cols = slice(h * HD, (h + 1) * HD)
        first = mine_ref[:, cols].astype(F32) * scale_a[:, h : h + 1]
        second = other_ref[:, cols].astype(F32) * scale_b[:, h : h + 1]
        out_ref[:, cols] = (first + second).astype(BF16)
    out_ref[:, width:] = packed(top, total_a * scale_a + total_b * scale_b)


def pair(mine, other):
    return pl.pallas_call(
        pair_kernel,
        out_shape=jax.ShapeDtypeStruct(other.shape, BF16),
        compiler_params=params(12),
        name="pair",
    )(mine, other)


def merge_kernel(parts_ref, gain_ref, normed_ref, kept_ref, whole):
    rows, padded = parts_ref.shape
    width = padded - 256
    heads = width // HD
    share = 8
    sources = rows // share
    peak, total = unpacked(parts_ref[:, width:])
    peak = peak.reshape(sources, share, heads)
    total = total.reshape(sources, share, heads)
    top = jnp.max(peak, axis=0)
    scale = jnp.exp(peak - top[None])
    total = jnp.sum(total * scale, axis=0)
    scale = scale.reshape(rows, heads)
    sums = jnp.zeros((share, HD), F32)
    last = None
    for h in range(heads):
        cols = slice(h * HD, (h + 1) * HD)
        numer = jnp.zeros((share, HD), F32)
        for at in range(0, rows, 16):
            block = parts_ref[at : at + 16, cols].astype(F32) * scale[at : at + 16, h : h + 1]
            numer = numer + block[:8] + block[8:]
        value = (numer / total[:, h : h + 1]).astype(BF16).astype(F32)
        whole[:, cols] = value
        sums = sums + value
        if h % 2 == 0:
            last = value
        else:
            to = h // 2 * 16
            kept_ref[to : to + 16, :] = jnp.concatenate([last, value], axis=0).astype(BF16)
    center = jnp.sum(sums, axis=1, keepdims=True) / width
    squares = jnp.zeros((share, HD), F32)
    for h in range(heads):
        shifted = whole[:, h * HD : (h + 1) * HD] - center
        squares = squares + shifted * shifted
    factor = lax.rsqrt(jnp.sum(squares, axis=1, keepdims=True) / width + EPS)
    for h in range(heads):
        cols = slice(h * HD, (h + 1) * HD)
        value = (whole[:, cols] - center) * factor * gain_ref[:, cols].astype(F32)
        twice = jnp.concatenate([value, value], axis=0).astype(BF16)
        for at in range(0, normed_ref.shape[0], 16):
            normed_ref[at : at + 16, cols] = twice


def merge(parts, gain, copies):
    rows, padded = parts.shape
    width = padded - 256
    return pl.pallas_call(
        merge_kernel,
        out_shape=(
            jax.ShapeDtypeStruct((copies * 8, width), BF16),
            jax.ShapeDtypeStruct((width // 16, HD), BF16),
        ),
        scratch_shapes=[pltpu.VMEM((8, width), F32)],
        compiler_params=params(12),
        name="merge",
    )(parts, gain)


def qkv_kernel(mine_ref, other_ref, weight_ref, kv_ref, keep_ref, send_ref, tokens, held, sems):
    core = lax.axis_index("c")
    z0 = lax.axis_index("z0")
    half, width = mine_ref.shape
    rows = 2 * half
    parts = sems.shape[1]
    depth = width // parts
    copies = [
        [
            pltpu.make_async_copy(
                weight_ref.at[k, pl.ds(part * depth, depth), :],
                held.at[k, pl.ds(part * depth, depth), :],
                sems.at[k, part],
            )
            for part in range(parts)
        ]
        for k in range(3)
    ]
    for k in range(3):
        for copy in copies[k]:
            copy.start()
    tokens[pl.ds(pl.multiple_of(core * half, half), half), :] = mine_ref[...]
    tokens[pl.ds(pl.multiple_of((1 - core) * half, half), half), :] = other_ref[...]
    for k in range(3):
        made = jnp.zeros((rows, 2 * HD), F32)
        for part in range(parts):
            copies[k][part].wait()
            at = slice(part * depth, (part + 1) * depth)
            made = made + dot(tokens[:, at], held[k, at, :], NN)
        first, second = made[:, :HD], made[:, HD:]
        if k == 0:
            keep_ref[...] = jnp.where(z0 == 0, first, second).astype(BF16)
            send_ref[...] = jnp.where(z0 == 0, second, first).astype(BF16)
        else:
            cols = slice((k - 1) * HD, k * HD)
            for to in range(16):
                value = first if to % 2 == 0 else second
                kv_ref[to * rows : (to + 1) * rows, cols] = value.astype(BF16)


def project(mine, other, weight):
    half, width = mine.shape
    cols = weight.shape[2]
    rows = 2 * half
    parts = 4
    vmem = pl.BlockSpec(memory_space=pltpu.VMEM)
    hbm = pl.BlockSpec(memory_space=pltpu.HBM)
    shapes = [(16 * rows, 2 * HD), (rows, HD), (rows, HD)]
    return pl.pallas_call(
        qkv_kernel,
        in_specs=[vmem, vmem, hbm],
        out_shape=[jax.ShapeDtypeStruct(shape, BF16) for shape in shapes],
        scratch_shapes=[
            pltpu.VMEM((rows, width), BF16),
            pltpu.VMEM((3, width, cols), BF16),
            pltpu.SemaphoreType.DMA((3, parts)),
        ],
        compiler_params=params(50),
        name="project",
    )(mine, other, weight)


def attend_kernel(keep_ref, got_ref, kv_ref, out_ref, scores):
    z0 = lax.axis_index("z0")
    count = kv_ref.shape[0]
    step = 256
    mixed = []
    for side in range(2):
        query = jnp.where(z0 == side, keep_ref[...], got_ref[...])
        for at in range(0, count, step):
            scores[:, at : at + step] = dot(query, kv_ref[at : at + step, :HD], NT) / math.sqrt(HD)
        every = scores[...]
        peak = jnp.max(every, axis=1, keepdims=True)
        weights = jnp.exp(every - peak)
        total = jnp.sum(weights, axis=1, keepdims=True)
        mixed.append(dot(weights.astype(BF16), kv_ref[:, HD:], NN) / total)
    for chip in range(8):
        for core in range(2):
            at = core * 64 + chip * 8
            to = (chip * 2 + core) * 16
            out_ref[to : to + 16, :] = jnp.concatenate(
                [mixed[0][at : at + 8], mixed[1][at : at + 8]], axis=0
            ).astype(BF16)


def attend(keep, got, kv):
    return pl.pallas_call(
        attend_kernel,
        out_shape=jax.ShapeDtypeStruct((256, HD), BF16),
        scratch_shapes=[pltpu.VMEM((128, 2048), F32)],
        compiler_params=params(16),
        name="attend",
    )(keep, got, kv)


def output_kernel(parts_ref, weight_ref, out_ref, attended, held, sems):
    bands = parts_ref.shape[0]
    width, cols = weight_ref.shape
    pieces = sems.shape[0]
    depth = width // pieces
    copies = [
        pltpu.make_async_copy(
            weight_ref.at[pl.ds(k * depth, depth), :], held.at[pl.ds(k * depth, depth), :], sems.at[k]
        )
        for k in range(pieces)
    ]
    for copy in copies:
        copy.start()
    for band in range(0, bands, 2):
        to = band * 8
        for source in range(16):
            at = source * 16
            a = parts_ref[band, at : at + 16, :].astype(F32)
            b = parts_ref[band + 1, at : at + 16, :].astype(F32)
            for side in range(2):
                head = 2 * source + side
                rows = slice(side * 8, side * 8 + 8)
                attended[to : to + 16, head * HD : (head + 1) * HD] = jnp.concatenate(
                    [a[rows], b[rows]], axis=0
                ).astype(BF16)
    product = jnp.zeros((attended.shape[0], cols), F32)
    for k in range(pieces):
        copies[k].wait()
        at = slice(k * depth, (k + 1) * depth)
        product = product + dot(attended[:, at], held[at, :], NN)
    half = cols // 2
    count = out_ref.shape[0] // 64
    for band in range(0, bands, 2):
        residual = []
        for b in (band, band + 1):
            kept = parts_ref[b, 256:288, :].astype(F32)
            residual.append(
                jnp.concatenate([kept[k : k + 8] for k in range(0, 32, 8)], axis=1)
            )
        at = band * 8
        layer = (jnp.concatenate(residual, axis=0) + product[at : at + 16]).astype(BF16)
        for to in range(count):
            side = to % 2
            out_ref[to * 64 + at : to * 64 + at + 16, :] = layer[:, side * half : (side + 1) * half]


def output(parts, weight):
    width, cols = weight.shape
    return pl.pallas_call(
        output_kernel,
        in_specs=[pl.BlockSpec(memory_space=pltpu.VMEM), pl.BlockSpec(memory_space=pltpu.HBM)],
        out_shape=jax.ShapeDtypeStruct((16 * 64, cols // 2), BF16),
        scratch_shapes=[
            pltpu.VMEM((64, width), BF16),
            pltpu.VMEM((width, cols), BF16),
            pltpu.SemaphoreType.DMA((8,)),
        ],
        compiler_params=params(50),
        name="output",
    )(parts, weight)


def swap(x, axis):
    return lax.ppermute(x, axis, [(0, 1), (1, 0)])


def exchange(x, axes):
    return lax.all_to_all(x, axes, 0, 0, tiled=True)


def body(patches, patch_weight, var_embed, agg_query, norm_gain, qkv_weight, out_weight, head_cot):
    core = lax.axis_index("c")
    width = out_weight.shape[1]

    keep, send = embed(patches.transpose(0, 2, 1), patch_weight, var_embed, agg_query.T)
    parts = pair(keep, swap(send, "c"))
    parts, cols = lax.optimization_barrier((parts, out_weight))

    cot = lax.all_gather(head_cot, SEQ, axis=0, tiled=True)
    cols = lax.dynamic_slice_in_dim(cols, lax.axis_index(BANDS) * 512, 512, 1)
    cols = lax.all_gather(cols, VAR, axis=0, tiled=True)

    parts = exchange(parts, CHIPS)
    normed, kept = merge(parts, norm_gain.reshape(1, width), 8)
    normed = exchange(normed, CHIPS)
    kv, query, query_send = project(normed, swap(normed, "c"), qkv_weight.transpose(1, 0, 2))
    query_got = swap(query_send, "z0")
    kv, cot = lax.optimization_barrier((exchange(kv, SEQ), cot))
    attended = attend(query, query_got, kv)
    attended = exchange(attended, VAR + ("z0",))
    sent = jnp.concatenate(
        [jnp.broadcast_to(attended[None], (8, 256, HD)), kept.reshape(8, 32, HD)], axis=1
    )
    got = exchange(sent, BANDS)
    layer = output(got, cols)
    layer = exchange(layer, CHIPS + ("z0",))
    cot = cot.reshape(8, 2, 8, 2, 8, 384).transpose(3, 2, 1, 0, 4, 5).reshape(2, 1024, 384)
    first = lax.dynamic_index_in_dim(cot, core, 0, keepdims=False)
    second = lax.dynamic_index_in_dim(cot, 1 - core, 0, keepdims=False)
    return dot(layer, first, TN) + dot(swap(layer, "c"), second, TN)


def solution(mesh):
    whole = Mesh(mesh.devices.reshape(4, 2, 2, 2, 4, 2), ("y", "xl", "c", "xh", "zq", "z0"))
    return jax.shard_map(
        body,
        mesh=whole,
        in_specs=(
            P(VAR, SEQ, None),
            P(VAR, None, None),
            P(VAR, None),
            P(),
            P(),
            P(None, None, VAR),
            P(VAR, None),
            P(SEQ, VAR),
        ),
        out_specs=P(SEQ, VAR),
        check_vma=False,
    )
```

```python
import math

import jax
import jax.numpy as jnp
from jax import lax
from jax.experimental import pallas as pl
from jax.experimental.pallas import tpu as pltpu
from jax.sharding import Mesh, PartitionSpec as P

EPS = 1e-05
HD = 128
F32 = jnp.float32
BF16 = jnp.bfloat16
VAR = ("y", "xl", "c")
CHIPS = ("y", "xl")
SEQ = ("xh", "zq", "z0")
BANDS = ("xh", "zq")
NT = (((1,), (1,)), ((), ()))
TN = (((0,), (0,)), ((), ()))
NN = (((1,), (0,)), ((), ()))
MB = 1024 * 1024


def dot(a, b, dims):
    return lax.dot_general(a, b, dims, preferred_element_type=F32)


def params(megabytes):
    return pltpu.CompilerParams(vmem_limit_bytes=megabytes * MB)


def in_three(x):
    high = x.astype(BF16).astype(F32)
    rest = x - high
    middle = rest.astype(BF16).astype(F32)
    return high, middle, rest - middle


def packed(peak, total):
    p0, p1, p2 = in_three(peak)
    t0, t1, t2 = in_three(total)
    blank = jnp.zeros_like(peak)
    parts = [p0, p1, p2, t0, t1, t2, blank, blank]
    return jnp.concatenate(parts, axis=1).astype(BF16)


def unpacked(stats):
    stats = stats.astype(F32)
    peak = stats[:, 0:32] + stats[:, 32:64] + stats[:, 64:96]
    total = stats[:, 96:128] + stats[:, 128:160] + stats[:, 160:192]
    return peak, total


def embed_kernel(
    pixels_ref, weight_ref, shift_ref, query_ref, rows_ref, keep_ref, send_ref, cols_ref, embedded, scores, held, sems
):
    core = lax.axis_index("c")
    part = lax.axis_index("xh") * 4 + lax.axis_index("zq")
    count, rows, width = embedded.shape
    heads = query_ref.shape[0]
    half = rows // 2
    copies = [
        pltpu.make_async_copy(weight_ref.at[v], held.at[v], sems.at[v]) for v in range(count)
    ]
    cut = cols_ref.shape[1]
    copies.append(
        pltpu.make_async_copy(
            rows_ref.at[:, pl.ds(pl.multiple_of(part * cut, cut), cut)], cols_ref, sems.at[count]
        )
    )
    for copy in copies:
        copy.start()
    new = lax.broadcasted_iota(jnp.int32, (rows, rows), 0)
    old = lax.broadcasted_iota(jnp.int32, (rows, rows), 1)
    group = (new % half) // 8 * 2 + jnp.where(new < half, core, 1 - core)
    order = jnp.where(old == group * 8 + new % 8, 1.0, 0.0).astype(BF16)
    step = 1024
    for v in range(count):
        tokens = dot(order, pixels_ref[v], NT).astype(BF16)
        copies[v].wait()
        total = jnp.zeros((rows, heads), F32)
        for at in range(0, width, step):
            block = dot(tokens, held[v, :, at : at + step], NN)
            shift = shift_ref[v : v + 1, at : at + step].astype(F32)
            block = (block + shift).astype(BF16)
            embedded[v, :, at : at + step] = block
            total = total + dot(block, query_ref[:, at : at + step], NT)
        scores[v] = total / math.sqrt(HD)
    every = scores[...]
    peak = jnp.max(every, axis=0)
    weights = jnp.exp(every - peak[None])
    total = jnp.sum(weights, axis=0)
    for h in range(heads):
        cols = slice(h * HD, (h + 1) * HD)
        numer = weights[0][:, h : h + 1] * embedded[0, :, cols].astype(F32)
        for v in range(1, count):
            numer = numer + weights[v][:, h : h + 1] * embedded[v, :, cols].astype(F32)
        keep_ref[:, cols] = numer[:half].astype(BF16)
        send_ref[:, cols] = numer[half:].astype(BF16)
    keep_ref[:, width:] = packed(peak[:half], total[:half])
    send_ref[:, width:] = packed(peak[half:], total[half:])
    copies[count].wait()


def embed(pixels, weight, shift, query, out_weight):
    count, depth, rows = pixels.shape
    width = weight.shape[2]
    heads = query.shape[0]
    vmem = pl.BlockSpec(memory_space=pltpu.VMEM)
    hbm = pl.BlockSpec(memory_space=pltpu.HBM)
    part = jax.ShapeDtypeStruct((rows // 2, width + 256), BF16)
    return pl.pallas_call(
        embed_kernel,
        in_specs=[vmem, hbm, vmem, vmem, hbm],
        out_specs=[vmem, vmem, hbm],
        out_shape=(part, part, jax.ShapeDtypeStruct((out_weight.shape[0], width // 8), BF16)),
        scratch_shapes=[
            pltpu.VMEM((count, rows, width), BF16),
            pltpu.VMEM((count, rows, heads), F32),
            pltpu.VMEM((count, depth, width), BF16),
            pltpu.SemaphoreType.DMA((count + 1,)),
        ],
        compiler_params=params(60),
        name="embed",
    )(pixels, weight, shift, query, out_weight)


def pair_kernel(mine_ref, other_ref, out_ref):
    rows, padded = mine_ref.shape
    width = padded - 256
    heads = width // HD
    peak_a, total_a = unpacked(mine_ref[:, width:])
    peak_b, total_b = unpacked(other_ref[:, width:])
    top = jnp.maximum(peak_a, peak_b)
    scale_a = jnp.exp(peak_a - top)
    scale_b = jnp.exp(peak_b - top)
    for h in range(heads):
        cols = slice(h * HD, (h + 1) * HD)
        first = mine_ref[:, cols].astype(F32) * scale_a[:, h : h + 1]
        second = other_ref[:, cols].astype(F32) * scale_b[:, h : h + 1]
        out_ref[:, cols] = (first + second).astype(BF16)
    out_ref[:, width:] = packed(top, total_a * scale_a + total_b * scale_b)


def pair(mine, other):
    return pl.pallas_call(
        pair_kernel,
        out_shape=jax.ShapeDtypeStruct(other.shape, BF16),
        compiler_params=params(12),
        name="pair",
    )(mine, other)


def merge_kernel(
    parts_ref, gain_ref, cot_ref, cot_got_ref, normed_ref, kept_ref, cot_out_ref, whole
):
    x_hi = lax.axis_index("xh")
    tokens = cot_ref.shape[0]
    cot_out_ref[pl.ds(pl.multiple_of(x_hi * tokens, tokens), tokens), :] = cot_ref[...]
    cot_out_ref[pl.ds(pl.multiple_of((1 - x_hi) * tokens, tokens), tokens), :] = cot_got_ref[...]
    rows, padded = parts_ref.shape
    width = padded - 256
    heads = width // HD
    share = 8
    sources = rows // share
    peak, total = unpacked(parts_ref[:, width:])
    peak = peak.reshape(sources, share, heads)
    total = total.reshape(sources, share, heads)
    top = jnp.max(peak, axis=0)
    scale = jnp.exp(peak - top[None])
    total = jnp.sum(total * scale, axis=0)
    scale = scale.reshape(rows, heads)
    sums = jnp.zeros((share, HD), F32)
    last = None
    for h in range(heads):
        cols = slice(h * HD, (h + 1) * HD)
        numer = jnp.zeros((share, HD), F32)
        for at in range(0, rows, 16):
            block = parts_ref[at : at + 16, cols].astype(F32) * scale[at : at + 16, h : h + 1]
            numer = numer + block[:8] + block[8:]
        value = (numer / total[:, h : h + 1]).astype(BF16).astype(F32)
        whole[:, cols] = value
        sums = sums + value
        if h % 2 == 0:
            last = value
        else:
            to = h // 2 * 16
            kept_ref[to : to + 16, :] = jnp.concatenate([last, value], axis=0).astype(BF16)
    center = jnp.sum(sums, axis=1, keepdims=True) / width
    squares = jnp.zeros((share, HD), F32)
    for h in range(heads):
        shifted = whole[:, h * HD : (h + 1) * HD] - center
        squares = squares + shifted * shifted
    factor = lax.rsqrt(jnp.sum(squares, axis=1, keepdims=True) / width + EPS)
    for h in range(heads):
        cols = slice(h * HD, (h + 1) * HD)
        value = (whole[:, cols] - center) * factor * gain_ref[:, cols].astype(F32)
        twice = jnp.concatenate([value, value], axis=0).astype(BF16)
        for at in range(0, normed_ref.shape[0], 16):
            normed_ref[at : at + 16, cols] = twice


def merge(parts, gain, copies, cot, cot_got):
    rows, padded = parts.shape
    tokens, cols = cot.shape
    width = padded - 256
    return pl.pallas_call(
        merge_kernel,
        out_shape=(
            jax.ShapeDtypeStruct((copies * 8, width), BF16),
            jax.ShapeDtypeStruct((width // 16, HD), BF16),
            jax.ShapeDtypeStruct((2 * tokens, cols), BF16),
        ),
        scratch_shapes=[pltpu.VMEM((8, width), F32)],
        compiler_params=params(12),
        name="merge",
    )(parts, gain, cot, cot_got)


def qkv_kernel(mine_ref, other_ref, weight_ref, kv_ref, query_ref, tokens, held, sems):
    core = lax.axis_index("c")
    z0 = lax.axis_index("z0")
    half, width = mine_ref.shape
    rows = 2 * half
    parts = sems.shape[1]
    depth = width // parts
    copies = [
        [
            pltpu.make_async_copy(
                weight_ref.at[k, pl.ds(part * depth, depth), pl.ds(pl.multiple_of(z0 * HD, HD), HD)],
                held.at[pl.ds(part * depth, depth), pl.ds(k * HD, HD)],
                sems.at[k, part],
            )
            for k in range(3)
        ]
        for part in range(parts)
    ]
    for part in range(parts):
        for copy in copies[part]:
            copy.start()
    tokens[pl.ds(pl.multiple_of(core * half, half), half), :] = mine_ref[...]
    tokens[pl.ds(pl.multiple_of((1 - core) * half, half), half), :] = other_ref[...]
    made = jnp.zeros((rows, 3 * HD), F32)
    for part in range(parts):
        for copy in copies[part]:
            copy.wait()
        at = slice(part * depth, (part + 1) * depth)
        made = made + dot(tokens[:, at], held[at, :], NN)
    made = made.astype(BF16)
    query_ref[...] = made[:, :HD]
    for to in range(kv_ref.shape[0] // rows):
        kv_ref[to * rows : (to + 1) * rows, :] = made[:, HD:]


def project(mine, other, weight, copies):
    half, width = mine.shape
    rows = 2 * half
    parts = 4
    vmem = pl.BlockSpec(memory_space=pltpu.VMEM)
    hbm = pl.BlockSpec(memory_space=pltpu.HBM)
    return pl.pallas_call(
        qkv_kernel,
        in_specs=[vmem, vmem, hbm],
        out_shape=(
            jax.ShapeDtypeStruct((copies * rows, 2 * HD), BF16),
            jax.ShapeDtypeStruct((rows, HD), BF16),
        ),
        scratch_shapes=[
            pltpu.VMEM((rows, width), BF16),
            pltpu.VMEM((width, 3 * HD), BF16),
            pltpu.SemaphoreType.DMA((3, parts)),
        ],
        compiler_params=params(50),
        name="project",
    )(mine, other, weight)


def attend_kernel(query_ref, kv_ref, out_ref, scores):
    count = kv_ref.shape[0]
    rows = scores.shape[0]
    step = 256
    for core in range(2):
        query = query_ref[core * rows : (core + 1) * rows, :]
        for at in range(0, count, step):
            scores[:, at : at + step] = dot(query, kv_ref[at : at + step, :HD], NT) / math.sqrt(HD)
        every = scores[...]
        peak = jnp.max(every, axis=1, keepdims=True)
        weights = jnp.exp(every - peak)
        total = jnp.sum(weights, axis=1, keepdims=True)
        mixed = (dot(weights.astype(BF16), kv_ref[:, HD:], NN) / total).astype(BF16)
        for chip in range(8):
            to = (chip * 2 + core) * 16
            out_ref[to : to + 16, :] = mixed[chip * 16 : chip * 16 + 16]


def attend(query, kv):
    rows = query.shape[0]
    return pl.pallas_call(
        attend_kernel,
        out_shape=jax.ShapeDtypeStruct((rows, HD), BF16),
        scratch_shapes=[pltpu.VMEM((rows // 2, kv.shape[0]), F32)],
        compiler_params=params(16),
        name="attend",
    )(query, kv)


def output_kernel(parts_ref, weight_ref, out_ref, attended, held, sems):
    bands = parts_ref.shape[0]
    width, cols = weight_ref.shape
    pieces = sems.shape[0]
    depth = width // pieces
    copies = [
        pltpu.make_async_copy(
            weight_ref.at[pl.ds(k * depth, depth), :], held.at[pl.ds(k * depth, depth), :], sems.at[k]
        )
        for k in range(pieces)
    ]
    for copy in copies:
        copy.start()
    for band in range(0, bands, 2):
        to = band * 8
        for source in range(16):
            at = source * 16
            a = parts_ref[band, at : at + 16, :].astype(F32)
            b = parts_ref[band + 1, at : at + 16, :].astype(F32)
            for side in range(2):
                head = 2 * source + side
                rows = slice(side * 8, side * 8 + 8)
                attended[to : to + 16, head * HD : (head + 1) * HD] = jnp.concatenate(
                    [a[rows], b[rows]], axis=0
                ).astype(BF16)
    product = jnp.zeros((attended.shape[0], cols), F32)
    for k in range(pieces):
        copies[k].wait()
        at = slice(k * depth, (k + 1) * depth)
        product = product + dot(attended[:, at], held[at, :], NN)
    half = cols // 2
    count = out_ref.shape[0] // 64
    for band in range(0, bands, 2):
        residual = []
        for b in (band, band + 1):
            kept = parts_ref[b, 256:288, :].astype(F32)
            residual.append(
                jnp.concatenate([kept[k : k + 8] for k in range(0, 32, 8)], axis=1)
            )
        at = band * 8
        layer = (jnp.concatenate(residual, axis=0) + product[at : at + 16]).astype(BF16)
        for to in range(count):
            side = to % 2
            out_ref[to * 64 + at : to * 64 + at + 16, :] = layer[:, side * half : (side + 1) * half]


def output(parts, weight):
    width, cols = weight.shape
    return pl.pallas_call(
        output_kernel,
        in_specs=[pl.BlockSpec(memory_space=pltpu.VMEM), pl.BlockSpec(memory_space=pltpu.HBM)],
        out_shape=jax.ShapeDtypeStruct((16 * 64, cols // 2), BF16),
        scratch_shapes=[
            pltpu.VMEM((64, width), BF16),
            pltpu.VMEM((width, cols), BF16),
            pltpu.SemaphoreType.DMA((8,)),
        ],
        compiler_params=params(50),
        name="output",
    )(parts, weight)


def swap(x, axis):
    return lax.ppermute(x, axis, [(0, 1), (1, 0)])


def exchange(x, axes):
    return lax.all_to_all(x, axes, 0, 0, tiled=True)


def body(patches, patch_weight, var_embed, agg_query, norm_gain, qkv_weight, out_weight, head_cot):
    core = lax.axis_index("c")
    width = out_weight.shape[1]

    cot_got = swap(head_cot, "xh")
    keep, send, cols = embed(
        patches.transpose(0, 2, 1), patch_weight, var_embed, agg_query.T, out_weight
    )
    cols = lax.all_gather(cols, VAR, axis=0, tiled=True)
    parts = pair(keep, swap(send, "c"))
    parts = exchange(parts, CHIPS)
    normed, kept, cot = merge(parts, norm_gain.reshape(1, width), 16, head_cot, cot_got)
    cot = lax.all_gather(cot, ("zq", "z0"), axis=0, tiled=True)
    normed = exchange(normed, CHIPS + ("z0",))
    kv, query = project(normed, swap(normed, "c"), qkv_weight.transpose(1, 0, 2), 8)
    kv, cols = lax.optimization_barrier((exchange(kv, BANDS), cols))
    attended = attend(query, kv)
    attended = exchange(attended, VAR + ("z0",))
    sent = jnp.concatenate(
        [jnp.broadcast_to(attended[None], (8, 256, HD)), kept.reshape(8, 32, HD)], axis=1
    )
    got, cot = lax.optimization_barrier((exchange(sent, BANDS), cot))
    layer = output(got, cols)
    layer = exchange(layer, CHIPS + ("z0",))
    cot = cot.reshape(4, 2, 2, 8, 2, 8, 384).transpose(4, 3, 1, 2, 0, 5, 6).reshape(2, 1024, 384)
    first = lax.dynamic_index_in_dim(cot, core, 0, keepdims=False)
    second = lax.dynamic_index_in_dim(cot, 1 - core, 0, keepdims=False)
    return dot(layer, first, TN) + dot(swap(layer, "c"), second, TN)


def solution(mesh):
    whole = Mesh(mesh.devices.reshape(4, 2, 2, 2, 4, 2), ("y", "xl", "c", "xh", "zq", "z0"))
    return jax.shard_map(
        body,
        mesh=whole,
        in_specs=(
            P(VAR, SEQ, None),
            P(VAR, None, None),
            P(VAR, None),
            P(),
            P(),
            P(None, None, VAR),
            P(VAR, None),
            P(SEQ, VAR),
        ),
        out_specs=P(SEQ, VAR),
        check_vma=False,
    )
```

```python
import math

import jax
import jax.numpy as jnp
from jax import lax
from jax.experimental import pallas as pl
from jax.experimental.pallas import tpu as pltpu
from jax.sharding import Mesh, PartitionSpec as P

EPS = 1e-05
HD = 128
F32 = jnp.float32
BF16 = jnp.bfloat16
VAR = ("y", "xl", "c")
CHIPS = ("y", "xl")
SEQ = ("xh", "zq", "z0")
BANDS = ("xh", "zq")
NT = (((1,), (1,)), ((), ()))
TN = (((0,), (0,)), ((), ()))
NN = (((1,), (0,)), ((), ()))
MB = 1024 * 1024


def dot(a, b, dims):
    return lax.dot_general(a, b, dims, preferred_element_type=F32)


def params(megabytes):
    return pltpu.CompilerParams(vmem_limit_bytes=megabytes * MB)


def in_three(x):
    high = x.astype(BF16).astype(F32)
    rest = x - high
    middle = rest.astype(BF16).astype(F32)
    return high, middle, rest - middle


def packed(peak, total):
    p0, p1, p2 = in_three(peak)
    t0, t1, t2 = in_three(total)
    blank = jnp.zeros_like(peak)
    parts = [p0, p1, p2, t0, t1, t2, blank, blank]
    return jnp.concatenate(parts, axis=1).astype(BF16)


def unpacked(stats):
    stats = stats.astype(F32)
    peak = stats[:, 0:32] + stats[:, 32:64] + stats[:, 64:96]
    total = stats[:, 96:128] + stats[:, 128:160] + stats[:, 160:192]
    return peak, total


def embed_kernel(
    pixels_ref, weight_ref, shift_ref, query_ref, rows_ref, keep_ref, send_ref, cols_ref, embedded, scores, held, sems
):
    core = lax.axis_index("c")
    part = lax.axis_index("xh") * 4 + lax.axis_index("zq")
    count, rows, width = embedded.shape
    heads = query_ref.shape[0]
    half = rows // 2
    copies = [
        pltpu.make_async_copy(weight_ref.at[v], held.at[v], sems.at[v]) for v in range(count)
    ]
    cut = cols_ref.shape[1]
    copies.append(
        pltpu.make_async_copy(
            rows_ref.at[:, pl.ds(pl.multiple_of(part * cut, cut), cut)], cols_ref, sems.at[count]
        )
    )
    for copy in copies:
        copy.start()
    new = lax.broadcasted_iota(jnp.int32, (rows, rows), 0)
    old = lax.broadcasted_iota(jnp.int32, (rows, rows), 1)
    group = (new % half) // 8 * 2 + jnp.where(new < half, core, 1 - core)
    order = jnp.where(old == group * 8 + new % 8, 1.0, 0.0).astype(BF16)
    step = 1024
    for v in range(count):
        tokens = dot(order, pixels_ref[v], NT).astype(BF16)
        copies[v].wait()
        total = jnp.zeros((rows, heads), F32)
        for at in range(0, width, step):
            block = dot(tokens, held[v, :, at : at + step], NN)
            shift = shift_ref[v : v + 1, at : at + step].astype(F32)
            block = (block + shift).astype(BF16)
            embedded[v, :, at : at + step] = block
            total = total + dot(block, query_ref[:, at : at + step], NT)
        scores[v] = total / math.sqrt(HD)
    every = scores[...]
    peak = jnp.max(every, axis=0)
    weights = jnp.exp(every - peak[None])
    total = jnp.sum(weights, axis=0)
    for h in range(heads):
        cols = slice(h * HD, (h + 1) * HD)
        numer = weights[0][:, h : h + 1] * embedded[0, :, cols].astype(F32)
        for v in range(1, count):
            numer = numer + weights[v][:, h : h + 1] * embedded[v, :, cols].astype(F32)
        keep_ref[:, cols] = numer[:half].astype(BF16)
        send_ref[:, cols] = numer[half:].astype(BF16)
    keep_ref[:, width:] = packed(peak[:half], total[:half])
    send_ref[:, width:] = packed(peak[half:], total[half:])
    copies[count].wait()


def embed(pixels, weight, shift, query, out_weight):
    count, depth, rows = pixels.shape
    width = weight.shape[2]
    heads = query.shape[0]
    vmem = pl.BlockSpec(memory_space=pltpu.VMEM)
    hbm = pl.BlockSpec(memory_space=pltpu.HBM)
    part = jax.ShapeDtypeStruct((rows // 2, width + 256), BF16)
    return pl.pallas_call(
        embed_kernel,
        in_specs=[vmem, hbm, vmem, vmem, hbm],
        out_specs=[vmem, vmem, hbm],
        out_shape=(part, part, jax.ShapeDtypeStruct((out_weight.shape[0], width // 8), BF16)),
        scratch_shapes=[
            pltpu.VMEM((count, rows, width), BF16),
            pltpu.VMEM((count, rows, heads), F32),
            pltpu.VMEM((count, depth, width), BF16),
            pltpu.SemaphoreType.DMA((count + 1,)),
        ],
        compiler_params=params(60),
        name="embed",
    )(pixels, weight, shift, query, out_weight)


def pair_kernel(mine_ref, other_ref, cot_ref, cot_got_ref, out_ref, cot_out_ref):
    x_hi = lax.axis_index("xh")
    tokens = cot_ref.shape[0]
    cot_out_ref[pl.ds(pl.multiple_of(x_hi * tokens, tokens), tokens), :] = cot_ref[...]
    cot_out_ref[pl.ds(pl.multiple_of((1 - x_hi) * tokens, tokens), tokens), :] = cot_got_ref[...]
    rows, padded = mine_ref.shape
    width = padded - 256
    heads = width // HD
    peak_a, total_a = unpacked(mine_ref[:, width:])
    peak_b, total_b = unpacked(other_ref[:, width:])
    top = jnp.maximum(peak_a, peak_b)
    scale_a = jnp.exp(peak_a - top)
    scale_b = jnp.exp(peak_b - top)
    for h in range(heads):
        cols = slice(h * HD, (h + 1) * HD)
        first = mine_ref[:, cols].astype(F32) * scale_a[:, h : h + 1]
        second = other_ref[:, cols].astype(F32) * scale_b[:, h : h + 1]
        out_ref[:, cols] = (first + second).astype(BF16)
    out_ref[:, width:] = packed(top, total_a * scale_a + total_b * scale_b)


def pair(mine, other, cot, cot_got):
    tokens, cols = cot.shape
    return pl.pallas_call(
        pair_kernel,
        out_shape=(
            jax.ShapeDtypeStruct(other.shape, BF16),
            jax.ShapeDtypeStruct((2 * tokens, cols), BF16),
        ),
        compiler_params=params(12),
        name="pair",
    )(mine, other, cot, cot_got)


def merge_kernel(parts_ref, gain_ref, normed_ref, kept_ref, whole):
    rows, padded = parts_ref.shape
    width = padded - 256
    heads = width // HD
    share = 8
    sources = rows // share
    peak, total = unpacked(parts_ref[:, width:])
    peak = peak.reshape(sources, share, heads)
    total = total.reshape(sources, share, heads)
    top = jnp.max(peak, axis=0)
    scale = jnp.exp(peak - top[None])
    total = jnp.sum(total * scale, axis=0)
    scale = scale.reshape(rows, heads)
    sums = jnp.zeros((share, HD), F32)
    last = None
    for h in range(heads):
        cols = slice(h * HD, (h + 1) * HD)
        numer = jnp.zeros((share, HD), F32)
        for at in range(0, rows, 16):
            block = parts_ref[at : at + 16, cols].astype(F32) * scale[at : at + 16, h : h + 1]
            numer = numer + block[:8] + block[8:]
        value = (numer / total[:, h : h + 1]).astype(BF16).astype(F32)
        whole[:, cols] = value
        sums = sums + value
        if h % 2 == 0:
            last = value
        else:
            to = h // 2 * 16
            kept_ref[to : to + 16, :] = jnp.concatenate([last, value], axis=0).astype(BF16)
    center = jnp.sum(sums, axis=1, keepdims=True) / width
    squares = jnp.zeros((share, HD), F32)
    for h in range(heads):
        shifted = whole[:, h * HD : (h + 1) * HD] - center
        squares = squares + shifted * shifted
    factor = lax.rsqrt(jnp.sum(squares, axis=1, keepdims=True) / width + EPS)
    for h in range(heads):
        cols = slice(h * HD, (h + 1) * HD)
        value = (whole[:, cols] - center) * factor * gain_ref[:, cols].astype(F32)
        twice = jnp.concatenate([value, value], axis=0).astype(BF16)
        for at in range(0, normed_ref.shape[0], 16):
            normed_ref[at : at + 16, cols] = twice


def merge(parts, gain, copies):
    rows, padded = parts.shape
    width = padded - 256
    return pl.pallas_call(
        merge_kernel,
        out_shape=(
            jax.ShapeDtypeStruct((copies * 8, width), BF16),
            jax.ShapeDtypeStruct((width // 16, HD), BF16),
        ),
        scratch_shapes=[pltpu.VMEM((8, width), F32)],
        compiler_params=params(12),
        name="merge",
    )(parts, gain)


def qkv_kernel(mine_ref, other_ref, weight_ref, kv_ref, query_ref, tokens, held, sems):
    core = lax.axis_index("c")
    z0 = lax.axis_index("z0")
    half, width = mine_ref.shape
    rows = 2 * half
    parts = sems.shape[1]
    depth = width // parts
    copies = [
        [
            pltpu.make_async_copy(
                weight_ref.at[k, pl.ds(part * depth, depth), pl.ds(pl.multiple_of(z0 * HD, HD), HD)],
                held.at[pl.ds(part * depth, depth), pl.ds(k * HD, HD)],
                sems.at[k, part],
            )
            for k in range(3)
        ]
        for part in range(parts)
    ]
    for part in range(parts):
        for copy in copies[part]:
            copy.start()
    tokens[pl.ds(pl.multiple_of(core * half, half), half), :] = mine_ref[...]
    tokens[pl.ds(pl.multiple_of((1 - core) * half, half), half), :] = other_ref[...]
    made = jnp.zeros((rows, 3 * HD), F32)
    for part in range(parts):
        for copy in copies[part]:
            copy.wait()
        at = slice(part * depth, (part + 1) * depth)
        made = made + dot(tokens[:, at], held[at, :], NN)
    made = made.astype(BF16)
    query_ref[...] = made[:, :HD]
    for to in range(kv_ref.shape[0] // rows):
        kv_ref[to * rows : (to + 1) * rows, :] = made[:, HD:]


def project(mine, other, weight, copies):
    half, width = mine.shape
    rows = 2 * half
    parts = 4
    vmem = pl.BlockSpec(memory_space=pltpu.VMEM)
    hbm = pl.BlockSpec(memory_space=pltpu.HBM)
    return pl.pallas_call(
        qkv_kernel,
        in_specs=[vmem, vmem, hbm],
        out_shape=(
            jax.ShapeDtypeStruct((copies * rows, 2 * HD), BF16),
            jax.ShapeDtypeStruct((rows, HD), BF16),
        ),
        scratch_shapes=[
            pltpu.VMEM((rows, width), BF16),
            pltpu.VMEM((width, 3 * HD), BF16),
            pltpu.SemaphoreType.DMA((3, parts)),
        ],
        compiler_params=params(50),
        name="project",
    )(mine, other, weight)


def attend_kernel(query_ref, kv_ref, out_ref, scores):
    count = kv_ref.shape[0]
    rows = scores.shape[0]
    step = 256
    for core in range(2):
        query = query_ref[core * rows : (core + 1) * rows, :]
        for at in range(0, count, step):
            scores[:, at : at + step] = dot(query, kv_ref[at : at + step, :HD], NT) / math.sqrt(HD)
        every = scores[...]
        peak = jnp.max(every, axis=1, keepdims=True)
        weights = jnp.exp(every - peak)
        total = jnp.sum(weights, axis=1, keepdims=True)
        mixed = (dot(weights.astype(BF16), kv_ref[:, HD:], NN) / total).astype(BF16)
        for chip in range(8):
            to = (chip * 2 + core) * 16
            out_ref[to : to + 16, :] = mixed[chip * 16 : chip * 16 + 16]


def attend(query, kv):
    rows = query.shape[0]
    return pl.pallas_call(
        attend_kernel,
        out_shape=jax.ShapeDtypeStruct((rows, HD), BF16),
        scratch_shapes=[pltpu.VMEM((rows // 2, kv.shape[0]), F32)],
        compiler_params=params(16),
        name="attend",
    )(query, kv)


def output_kernel(parts_ref, weight_ref, out_ref, attended, held, sems):
    bands = parts_ref.shape[0]
    width, cols = weight_ref.shape
    pieces = sems.shape[0]
    depth = width // pieces
    copies = [
        pltpu.make_async_copy(
            weight_ref.at[pl.ds(k * depth, depth), :], held.at[pl.ds(k * depth, depth), :], sems.at[k]
        )
        for k in range(pieces)
    ]
    for copy in copies:
        copy.start()
    for band in range(0, bands, 2):
        to = band * 8
        for source in range(16):
            at = source * 16
            a = parts_ref[band, at : at + 16, :].astype(F32)
            b = parts_ref[band + 1, at : at + 16, :].astype(F32)
            for side in range(2):
                head = 2 * source + side
                rows = slice(side * 8, side * 8 + 8)
                attended[to : to + 16, head * HD : (head + 1) * HD] = jnp.concatenate(
                    [a[rows], b[rows]], axis=0
                ).astype(BF16)
    product = jnp.zeros((attended.shape[0], cols), F32)
    for k in range(pieces):
        copies[k].wait()
        at = slice(k * depth, (k + 1) * depth)
        product = product + dot(attended[:, at], held[at, :], NN)
    half = cols // 2
    count = out_ref.shape[0] // 64
    for band in range(0, bands, 2):
        residual = []
        for b in (band, band + 1):
            kept = parts_ref[b, 256:288, :].astype(F32)
            residual.append(
                jnp.concatenate([kept[k : k + 8] for k in range(0, 32, 8)], axis=1)
            )
        at = band * 8
        layer = (jnp.concatenate(residual, axis=0) + product[at : at + 16]).astype(BF16)
        for to in range(count):
            side = to % 2
            out_ref[to * 64 + at : to * 64 + at + 16, :] = layer[:, side * half : (side + 1) * half]


def output(parts, weight):
    width, cols = weight.shape
    return pl.pallas_call(
        output_kernel,
        in_specs=[pl.BlockSpec(memory_space=pltpu.VMEM), pl.BlockSpec(memory_space=pltpu.HBM)],
        out_shape=jax.ShapeDtypeStruct((16 * 64, cols // 2), BF16),
        scratch_shapes=[
            pltpu.VMEM((64, width), BF16),
            pltpu.VMEM((width, cols), BF16),
            pltpu.SemaphoreType.DMA((8,)),
        ],
        compiler_params=params(50),
        name="output",
    )(parts, weight)


def swap(x, axis):
    return lax.ppermute(x, axis, [(0, 1), (1, 0)])


def exchange(x, axes):
    return lax.all_to_all(x, axes, 0, 0, tiled=True)


def body(patches, patch_weight, var_embed, agg_query, norm_gain, qkv_weight, out_weight, head_cot):
    core = lax.axis_index("c")
    width = out_weight.shape[1]

    cot_got = swap(head_cot, "xh")
    keep, send, cols = embed(
        patches.transpose(0, 2, 1), patch_weight, var_embed, agg_query.T, out_weight
    )
    parts, cot = pair(keep, swap(send, "c"), head_cot, cot_got)
    cot = lax.all_gather(cot, ("zq", "z0"), axis=0, tiled=True)
    parts, cols = lax.optimization_barrier((exchange(parts, CHIPS), cols))
    cols = lax.all_gather(cols, VAR, axis=0, tiled=True)
    normed, kept = merge(parts, norm_gain.reshape(1, width), 16)
    normed = exchange(normed, CHIPS + ("z0",))
    kv, query = project(normed, swap(normed, "c"), qkv_weight.transpose(1, 0, 2), 8)
    kv, cot = lax.optimization_barrier((exchange(kv, BANDS), cot))
    attended = attend(query, kv)
    attended = exchange(attended, VAR + ("z0",))
    sent = jnp.concatenate(
        [jnp.broadcast_to(attended[None], (8, 256, HD)), kept.reshape(8, 32, HD)], axis=1
    )
    got = exchange(sent, BANDS)
    layer = output(got, cols)
    layer = exchange(layer, CHIPS + ("z0",))
    cot = cot.reshape(4, 2, 2, 8, 2, 8, 384).transpose(4, 3, 1, 2, 0, 5, 6).reshape(2, 1024, 384)
    first = lax.dynamic_index_in_dim(cot, core, 0, keepdims=False)
    second = lax.dynamic_index_in_dim(cot, 1 - core, 0, keepdims=False)
    return dot(layer, first, TN) + dot(swap(layer, "c"), second, TN)


def solution(mesh):
    whole = Mesh(mesh.devices.reshape(4, 2, 2, 2, 4, 2), ("y", "xl", "c", "xh", "zq", "z0"))
    return jax.shard_map(
        body,
        mesh=whole,
        in_specs=(
            P(VAR, SEQ, None),
            P(VAR, None, None),
            P(VAR, None),
            P(),
            P(),
            P(None, None, VAR),
            P(VAR, None),
            P(SEQ, VAR),
        ),
        out_specs=P(SEQ, VAR),
        check_vma=False,
    )
```

```python
import math

import jax
import jax.numpy as jnp
from jax import lax
from jax.experimental import pallas as pl
from jax.experimental.pallas import tpu as pltpu
from jax.sharding import Mesh, PartitionSpec as P

EPS = 1e-05
HD = 128
F32 = jnp.float32
BF16 = jnp.bfloat16
VAR = ("y", "xl", "c")
CHIPS = ("y", "xl")
SEQ = ("xh", "zq", "z0")
BANDS = ("xh", "zq")
NT = (((1,), (1,)), ((), ()))
TN = (((0,), (0,)), ((), ()))
NN = (((1,), (0,)), ((), ()))
MB = 1024 * 1024


def dot(a, b, dims):
    return lax.dot_general(a, b, dims, preferred_element_type=F32)


def params(megabytes):
    return pltpu.CompilerParams(vmem_limit_bytes=megabytes * MB)


def in_three(x):
    high = x.astype(BF16).astype(F32)
    rest = x - high
    middle = rest.astype(BF16).astype(F32)
    return high, middle, rest - middle


def packed(peak, total):
    p0, p1, p2 = in_three(peak)
    t0, t1, t2 = in_three(total)
    blank = jnp.zeros_like(peak)
    parts = [p0, p1, p2, t0, t1, t2, blank, blank]
    return jnp.concatenate(parts, axis=1).astype(BF16)


def unpacked(stats):
    stats = stats.astype(F32)
    peak = stats[:, 0:32] + stats[:, 32:64] + stats[:, 64:96]
    total = stats[:, 96:128] + stats[:, 128:160] + stats[:, 160:192]
    return peak, total


def embed_kernel(
    pixels_ref, weight_ref, shift_ref, query_ref, rows_ref, keep_ref, send_ref, cols_ref, embedded, scores, held, sems
):
    core = lax.axis_index("c")
    part = lax.axis_index("xh") * 4 + lax.axis_index("zq")
    count, rows, width = embedded.shape
    heads = query_ref.shape[0]
    half = rows // 2
    copies = [
        pltpu.make_async_copy(weight_ref.at[v], held.at[v], sems.at[v]) for v in range(count)
    ]
    cut = cols_ref.shape[1]
    copies.append(
        pltpu.make_async_copy(
            rows_ref.at[:, pl.ds(pl.multiple_of(part * cut, cut), cut)], cols_ref, sems.at[count]
        )
    )
    for copy in copies:
        copy.start()
    new = lax.broadcasted_iota(jnp.int32, (rows, rows), 0)
    old = lax.broadcasted_iota(jnp.int32, (rows, rows), 1)
    group = (new % half) // 8 * 2 + jnp.where(new < half, core, 1 - core)
    order = jnp.where(old == group * 8 + new % 8, 1.0, 0.0).astype(BF16)
    step = 1024
    for v in range(count):
        tokens = dot(order, pixels_ref[v], NT).astype(BF16)
        copies[v].wait()
        total = jnp.zeros((rows, heads), F32)
        for at in range(0, width, step):
            block = dot(tokens, held[v, :, at : at + step], NN)
            shift = shift_ref[v : v + 1, at : at + step].astype(F32)
            block = (block + shift).astype(BF16)
            embedded[v, :, at : at + step] = block
            total = total + dot(block, query_ref[:, at : at + step], NT)
        scores[v] = total / math.sqrt(HD)
    every = scores[...]
    peak = jnp.max(every, axis=0)
    weights = jnp.exp(every - peak[None])
    total = jnp.sum(weights, axis=0)
    for h in range(heads):
        cols = slice(h * HD, (h + 1) * HD)
        numer = weights[0][:, h : h + 1] * embedded[0, :, cols].astype(F32)
        for v in range(1, count):
            numer = numer + weights[v][:, h : h + 1] * embedded[v, :, cols].astype(F32)
        keep_ref[:, cols] = numer[:half].astype(BF16)
        send_ref[:, cols] = numer[half:].astype(BF16)
    keep_ref[:, width:] = packed(peak[:half], total[:half])
    send_ref[:, width:] = packed(peak[half:], total[half:])
    copies[count].wait()


def embed(pixels, weight, shift, query, out_weight):
    count, depth, rows = pixels.shape
    width = weight.shape[2]
    heads = query.shape[0]
    vmem = pl.BlockSpec(memory_space=pltpu.VMEM)
    hbm = pl.BlockSpec(memory_space=pltpu.HBM)
    part = jax.ShapeDtypeStruct((rows // 2, width + 256), BF16)
    return pl.pallas_call(
        embed_kernel,
        in_specs=[vmem, hbm, vmem, vmem, hbm],
        out_specs=[vmem, vmem, hbm],
        out_shape=(part, part, jax.ShapeDtypeStruct((out_weight.shape[0], width // 8), BF16)),
        scratch_shapes=[
            pltpu.VMEM((count, rows, width), BF16),
            pltpu.VMEM((count, rows, heads), F32),
            pltpu.VMEM((count, depth, width), BF16),
            pltpu.SemaphoreType.DMA((count + 1,)),
        ],
        compiler_params=params(60),
        name="embed",
    )(pixels, weight, shift, query, out_weight)


def pair_kernel(mine_ref, other_ref, cot_ref, cot_got_ref, out_ref, cot_out_ref):
    x_hi = lax.axis_index("xh")
    tokens = cot_ref.shape[0]
    cot_out_ref[pl.ds(pl.multiple_of(x_hi * tokens, tokens), tokens), :] = cot_ref[...]
    cot_out_ref[pl.ds(pl.multiple_of((1 - x_hi) * tokens, tokens), tokens), :] = cot_got_ref[...]
    rows, padded = mine_ref.shape
    width = padded - 256
    heads = width // HD
    peak_a, total_a = unpacked(mine_ref[:, width:])
    peak_b, total_b = unpacked(other_ref[:, width:])
    top = jnp.maximum(peak_a, peak_b)
    scale_a = jnp.exp(peak_a - top)
    scale_b = jnp.exp(peak_b - top)
    for h in range(heads):
        cols = slice(h * HD, (h + 1) * HD)
        first = mine_ref[:, cols].astype(F32) * scale_a[:, h : h + 1]
        second = other_ref[:, cols].astype(F32) * scale_b[:, h : h + 1]
        out_ref[:, cols] = (first + second).astype(BF16)
    out_ref[:, width:] = packed(top, total_a * scale_a + total_b * scale_b)


def pair(mine, other, cot, cot_got):
    tokens, cols = cot.shape
    return pl.pallas_call(
        pair_kernel,
        out_shape=(
            jax.ShapeDtypeStruct(other.shape, BF16),
            jax.ShapeDtypeStruct((2 * tokens, cols), BF16),
        ),
        compiler_params=params(12),
        name="pair",
    )(mine, other, cot, cot_got)


def merge_kernel(parts_ref, gain_ref, normed_ref, kept_ref, whole):
    rows, padded = parts_ref.shape
    width = padded - 256
    heads = width // HD
    share = 8
    sources = rows // share
    peak, total = unpacked(parts_ref[:, width:])
    peak = peak.reshape(sources, share, heads)
    total = total.reshape(sources, share, heads)
    top = jnp.max(peak, axis=0)
    scale = jnp.exp(peak - top[None])
    total = jnp.sum(total * scale, axis=0)
    scale = scale.reshape(rows, heads)
    sums = jnp.zeros((share, HD), F32)
    last = None
    for h in range(heads):
        cols = slice(h * HD, (h + 1) * HD)
        numer = jnp.zeros((share, HD), F32)
        for at in range(0, rows, 16):
            block = parts_ref[at : at + 16, cols].astype(F32) * scale[at : at + 16, h : h + 1]
            numer = numer + block[:8] + block[8:]
        value = (numer / total[:, h : h + 1]).astype(BF16).astype(F32)
        whole[:, cols] = value
        sums = sums + value
        if h % 2 == 0:
            last = value
        else:
            to = h // 2 * 16
            kept_ref[to : to + 16, :] = jnp.concatenate([last, value], axis=0).astype(BF16)
    center = jnp.sum(sums, axis=1, keepdims=True) / width
    squares = jnp.zeros((share, HD), F32)
    for h in range(heads):
        shifted = whole[:, h * HD : (h + 1) * HD] - center
        squares = squares + shifted * shifted
    factor = lax.rsqrt(jnp.sum(squares, axis=1, keepdims=True) / width + EPS)
    for h in range(heads):
        cols = slice(h * HD, (h + 1) * HD)
        value = (whole[:, cols] - center) * factor * gain_ref[:, cols].astype(F32)
        twice = jnp.concatenate([value, value], axis=0).astype(BF16)
        for at in range(0, normed_ref.shape[0], 16):
            normed_ref[at : at + 16, cols] = twice


def merge(parts, gain, copies):
    rows, padded = parts.shape
    width = padded - 256
    return pl.pallas_call(
        merge_kernel,
        out_shape=(
            jax.ShapeDtypeStruct((copies * 8, width), BF16),
            jax.ShapeDtypeStruct((width // 16, HD), BF16),
        ),
        scratch_shapes=[pltpu.VMEM((8, width), F32)],
        compiler_params=params(12),
        name="merge",
    )(parts, gain)


def qkv_kernel(mine_ref, other_ref, weight_ref, kv_ref, keep_ref, send_ref, tokens, held, sems):
    core = lax.axis_index("c")
    z0 = lax.axis_index("z0")
    half, width = mine_ref.shape
    rows = 2 * half
    parts = sems.shape[1]
    depth = width // parts
    copies = [
        [
            pltpu.make_async_copy(
                weight_ref.at[k, pl.ds(part * depth, depth), :],
                held.at[k, pl.ds(part * depth, depth), :],
                sems.at[k, part],
            )
            for part in range(parts)
        ]
        for k in range(3)
    ]
    for k in range(3):
        for copy in copies[k]:
            copy.start()
    tokens[pl.ds(pl.multiple_of(core * half, half), half), :] = mine_ref[...]
    tokens[pl.ds(pl.multiple_of((1 - core) * half, half), half), :] = other_ref[...]
    for k in range(3):
        made = jnp.zeros((rows, 2 * HD), F32)
        for part in range(parts):
            copies[k][part].wait()
            at = slice(part * depth, (part + 1) * depth)
            made = made + dot(tokens[:, at], held[k, at, :], NN)
        first, second = made[:, :HD], made[:, HD:]
        if k == 0:
            keep_ref[...] = jnp.where(z0 == 0, first, second).astype(BF16)
            send_ref[...] = jnp.where(z0 == 0, second, first).astype(BF16)
        else:
            cols = slice((k - 1) * HD, k * HD)
            for to in range(16):
                value = first if to % 2 == 0 else second
                kv_ref[to * rows : (to + 1) * rows, cols] = value.astype(BF16)


def project(mine, other, weight):
    half, width = mine.shape
    cols = weight.shape[2]
    rows = 2 * half
    parts = 4
    vmem = pl.BlockSpec(memory_space=pltpu.VMEM)
    hbm = pl.BlockSpec(memory_space=pltpu.HBM)
    shapes = [(16 * rows, 2 * HD), (rows, HD), (rows, HD)]
    return pl.pallas_call(
        qkv_kernel,
        in_specs=[vmem, vmem, hbm],
        out_shape=[jax.ShapeDtypeStruct(shape, BF16) for shape in shapes],
        scratch_shapes=[
            pltpu.VMEM((rows, width), BF16),
            pltpu.VMEM((3, width, cols), BF16),
            pltpu.SemaphoreType.DMA((3, parts)),
        ],
        compiler_params=params(50),
        name="project",
    )(mine, other, weight)


def attend_kernel(keep_ref, got_ref, kv_ref, out_ref, scores):
    z0 = lax.axis_index("z0")
    count = kv_ref.shape[0]
    step = 256
    mixed = []
    for side in range(2):
        query = jnp.where(z0 == side, keep_ref[...], got_ref[...])
        for at in range(0, count, step):
            scores[:, at : at + step] = dot(query, kv_ref[at : at + step, :HD], NT) / math.sqrt(HD)
        every = scores[...]
        peak = jnp.max(every, axis=1, keepdims=True)
        weights = jnp.exp(every - peak)
        total = jnp.sum(weights, axis=1, keepdims=True)
        mixed.append(dot(weights.astype(BF16), kv_ref[:, HD:], NN) / total)
    for chip in range(8):
        for core in range(2):
            at = core * 64 + chip * 8
            to = (chip * 2 + core) * 16
            out_ref[to : to + 16, :] = jnp.concatenate(
                [mixed[0][at : at + 8], mixed[1][at : at + 8]], axis=0
            ).astype(BF16)


def attend(keep, got, kv):
    return pl.pallas_call(
        attend_kernel,
        out_shape=jax.ShapeDtypeStruct((256, HD), BF16),
        scratch_shapes=[pltpu.VMEM((128, 2048), F32)],
        compiler_params=params(16),
        name="attend",
    )(keep, got, kv)


def output_kernel(parts_ref, weight_ref, out_ref, attended, held, sems):
    bands = parts_ref.shape[0]
    width, cols = weight_ref.shape
    pieces = sems.shape[0]
    depth = width // pieces
    copies = [
        pltpu.make_async_copy(
            weight_ref.at[pl.ds(k * depth, depth), :], held.at[pl.ds(k * depth, depth), :], sems.at[k]
        )
        for k in range(pieces)
    ]
    for copy in copies:
        copy.start()
    for band in range(0, bands, 2):
        to = band * 8
        for source in range(16):
            at = source * 16
            a = parts_ref[band, at : at + 16, :].astype(F32)
            b = parts_ref[band + 1, at : at + 16, :].astype(F32)
            for side in range(2):
                head = 2 * source + side
                rows = slice(side * 8, side * 8 + 8)
                attended[to : to + 16, head * HD : (head + 1) * HD] = jnp.concatenate(
                    [a[rows], b[rows]], axis=0
                ).astype(BF16)
    product = jnp.zeros((attended.shape[0], cols), F32)
    for k in range(pieces):
        copies[k].wait()
        at = slice(k * depth, (k + 1) * depth)
        product = product + dot(attended[:, at], held[at, :], NN)
    half = cols // 2
    count = out_ref.shape[0] // 64
    for band in range(0, bands, 2):
        residual = []
        for b in (band, band + 1):
            kept = parts_ref[b, 256:288, :].astype(F32)
            residual.append(
                jnp.concatenate([kept[k : k + 8] for k in range(0, 32, 8)], axis=1)
            )
        at = band * 8
        layer = (jnp.concatenate(residual, axis=0) + product[at : at + 16]).astype(BF16)
        for to in range(count):
            side = to % 2
            out_ref[to * 64 + at : to * 64 + at + 16, :] = layer[:, side * half : (side + 1) * half]


def output(parts, weight):
    width, cols = weight.shape
    return pl.pallas_call(
        output_kernel,
        in_specs=[pl.BlockSpec(memory_space=pltpu.VMEM), pl.BlockSpec(memory_space=pltpu.HBM)],
        out_shape=jax.ShapeDtypeStruct((16 * 64, cols // 2), BF16),
        scratch_shapes=[
            pltpu.VMEM((64, width), BF16),
            pltpu.VMEM((width, cols), BF16),
            pltpu.SemaphoreType.DMA((8,)),
        ],
        compiler_params=params(50),
        name="output",
    )(parts, weight)


def swap(x, axis):
    return lax.ppermute(x, axis, [(0, 1), (1, 0)])


def exchange(x, axes):
    return lax.all_to_all(x, axes, 0, 0, tiled=True)


def body(patches, patch_weight, var_embed, agg_query, norm_gain, qkv_weight, out_weight, head_cot):
    core = lax.axis_index("c")
    width = out_weight.shape[1]

    cot_got = swap(head_cot, "xh")
    keep, send, cols = embed(
        patches.transpose(0, 2, 1), patch_weight, var_embed, agg_query.T, out_weight
    )
    parts, cot = pair(keep, swap(send, "c"), head_cot, cot_got)
    cot = lax.all_gather(cot, ("zq", "z0"), axis=0, tiled=True)
    parts, cols = lax.optimization_barrier((exchange(parts, CHIPS), cols))
    cols = lax.all_gather(cols, VAR, axis=0, tiled=True)
    normed, kept = merge(parts, norm_gain.reshape(1, width), 8)
    normed = exchange(normed, CHIPS)
    kv, query, query_send = project(normed, swap(normed, "c"), qkv_weight.transpose(1, 0, 2))
    query_got = swap(query_send, "z0")
    kv, cot = lax.optimization_barrier((exchange(kv, SEQ), cot))
    attended = attend(query, query_got, kv)
    attended = exchange(attended, VAR + ("z0",))
    sent = jnp.concatenate(
        [jnp.broadcast_to(attended[None], (8, 256, HD)), kept.reshape(8, 32, HD)], axis=1
    )
    got = exchange(sent, BANDS)
    layer = output(got, cols)
    layer = exchange(layer, CHIPS + ("z0",))
    cot = cot.reshape(4, 2, 2, 8, 2, 8, 384).transpose(4, 3, 1, 2, 0, 5, 6).reshape(2, 1024, 384)
    first = lax.dynamic_index_in_dim(cot, core, 0, keepdims=False)
    second = lax.dynamic_index_in_dim(cot, 1 - core, 0, keepdims=False)
    return dot(layer, first, TN) + dot(swap(layer, "c"), second, TN)


def solution(mesh):
    whole = Mesh(mesh.devices.reshape(4, 2, 2, 2, 4, 2), ("y", "xl", "c", "xh", "zq", "z0"))
    return jax.shard_map(
        body,
        mesh=whole,
        in_specs=(
            P(VAR, SEQ, None),
            P(VAR, None, None),
            P(VAR, None),
            P(),
            P(),
            P(None, None, VAR),
            P(VAR, None),
            P(SEQ, VAR),
        ),
        out_specs=P(SEQ, VAR),
        check_vma=False,
    )
```

```python
import math

import jax
import jax.numpy as jnp
from jax import lax
from jax.experimental import pallas as pl
from jax.experimental.pallas import tpu as pltpu
from jax.sharding import Mesh, PartitionSpec as P

EPS = 1e-05
HD = 128
F32 = jnp.float32
BF16 = jnp.bfloat16
VAR = ("y", "xl", "c")
CHIPS = ("y", "xl")
SEQ = ("xh", "z")
NT = (((1,), (1,)), ((), ()))
TN = (((0,), (0,)), ((), ()))
NN = (((1,), (0,)), ((), ()))
MB = 1024 * 1024


def dot(a, b, dims):
    return lax.dot_general(a, b, dims, preferred_element_type=F32)


def params(megabytes):
    return pltpu.CompilerParams(vmem_limit_bytes=megabytes * MB)


def in_three(x):
    high = x.astype(BF16).astype(F32)
    rest = x - high
    middle = rest.astype(BF16).astype(F32)
    return high, middle, rest - middle


def packed(peak, total):
    p0, p1, p2 = in_three(peak)
    t0, t1, t2 = in_three(total)
    blank = jnp.zeros_like(peak)
    parts = [p0, p1, p2, t0, t1, t2, blank, blank]
    return jnp.concatenate(parts, axis=1).astype(BF16)


def unpacked(stats):
    stats = stats.astype(F32)
    peak = stats[:, 0:32] + stats[:, 32:64] + stats[:, 64:96]
    total = stats[:, 96:128] + stats[:, 128:160] + stats[:, 160:192]
    return peak, total


def embed_kernel(
    pixels_hbm, weight_ref, shift_hbm, query_hbm, rows_ref, keep_ref, send_ref, cols_ref,
    pixels_ref, shift_ref, query_ref, embedded, scores, held, keep, send, sems, small_sems, out_sems,
):
    core = lax.axis_index("c")
    z = lax.axis_index("z")
    count, rows, width = embedded.shape
    heads = query_ref.shape[0]
    half = rows // 2
    small = [
        pltpu.make_async_copy(pixels_hbm, pixels_ref, small_sems.at[0]),
        pltpu.make_async_copy(shift_hbm, shift_ref, small_sems.at[1]),
        pltpu.make_async_copy(query_hbm, query_ref, small_sems.at[2]),
    ]
    copies = [
        pltpu.make_async_copy(weight_ref.at[v], held.at[v], sems.at[v]) for v in range(count)
    ]
    for copy in [small[0], copies[0], small[1], small[2]] + copies[1:]:
        copy.start()
    cut = cols_ref.shape[1] // 2
    slices = []
    for side in range(2):
        place = pl.multiple_of(side * (width // 2) + z * cut, cut)
        slices.append(
            pltpu.make_async_copy(
                rows_ref.at[:, pl.ds(place, cut)],
                cols_ref.at[:, pl.ds(side * cut, cut)],
                small_sems.at[3 + side],
            )
        )
        slices[side].start()
    new = lax.broadcasted_iota(jnp.int32, (rows, rows), 0)
    old = lax.broadcasted_iota(jnp.int32, (rows, rows), 1)
    group = (new % half) // 8 * 2 + jnp.where(new < half, core, 1 - core)
    order = jnp.where(old == group * 8 + new % 8, 1.0, 0.0).astype(BF16)
    step = 1024
    small[0].wait()
    for v in range(count):
        tokens = dot(order, pixels_ref[v], NT).astype(BF16)
        if v == 0:
            small[1].wait()
            small[2].wait()
        if v % 2 == 0:
            for copy in copies[v : v + 2]:
                copy.wait()
        total = jnp.zeros((rows, heads), F32)
        for at in range(0, width, step):
            block = dot(tokens, held[v, :, at : at + step], NN)
            shift = shift_ref[v : v + 1, at : at + step].astype(F32)
            block = (block + shift).astype(BF16)
            embedded[v, :, at : at + step] = block
            total = total + dot(block, query_ref[:, at : at + step], NT)
        scores[v] = total / math.sqrt(HD)
    every = scores[...]
    peak = jnp.max(every, axis=0)
    weights = jnp.exp(every - peak[None])
    total = jnp.sum(weights, axis=0)
    keep[:, width:] = packed(peak[:half], total[:half])
    send[:, width:] = packed(peak[half:], total[half:])
    leaving = []

    def leave(place, size):
        at = len(leaving) // 2
        for side, (source, target) in enumerate(((keep, keep_ref), (send, send_ref))):
            copy = pltpu.make_async_copy(
                source.at[:, pl.ds(place, size)], target.at[:, pl.ds(place, size)], out_sems.at[side, at]
            )
            copy.start()
            leaving.append(copy)

    leave(width, 256)
    for h in range(heads):
        cols = slice(h * HD, (h + 1) * HD)
        numer = weights[0][:, h : h + 1] * embedded[0, :, cols].astype(F32)
        for v in range(1, count):
            numer = numer + weights[v][:, h : h + 1] * embedded[v, :, cols].astype(F32)
        keep[:, cols] = numer[:half].astype(BF16)
        send[:, cols] = numer[half:].astype(BF16)
        if h % 8 == 7:
            leave((h - 7) * HD, 8 * HD)
    for copy in slices + leaving:
        copy.wait()


def embed(pixels, weight, shift, query, out_weight):
    count, depth, rows = pixels.shape
    width = weight.shape[2]
    heads = query.shape[0]
    half = rows // 2
    hbm = pl.BlockSpec(memory_space=pltpu.HBM)
    part = jax.ShapeDtypeStruct((half, width + 256), BF16)
    return pl.pallas_call(
        embed_kernel,
        in_specs=[hbm] * 5,
        out_specs=[hbm] * 3,
        out_shape=(part, part, jax.ShapeDtypeStruct((out_weight.shape[0], width // 8), BF16)),
        scratch_shapes=[
            pltpu.VMEM((count, depth, rows), BF16),
            pltpu.VMEM((count, width), BF16),
            pltpu.VMEM((heads, width), BF16),
            pltpu.VMEM((count, rows, width), BF16),
            pltpu.VMEM((count, rows, heads), F32),
            pltpu.VMEM((count, depth, width), BF16),
            pltpu.VMEM((half, width + 256), BF16),
            pltpu.VMEM((half, width + 256), BF16),
            pltpu.SemaphoreType.DMA((count,)),
            pltpu.SemaphoreType.DMA((5,)),
            pltpu.SemaphoreType.DMA((2, 5)),
        ],
        compiler_params=params(60),
        cost_estimate=pl.CostEstimate(
            flops=2 * count * rows * width * (depth + heads),
            bytes_accessed=4 * count * depth * width,
            transcendentals=count * rows * heads,
        ),
        name="embed",
    )(pixels, weight, shift, query, out_weight)


def pair_kernel(mine_ref, other_ref, cot_ref, cot_got_ref, out_ref, cot_out_ref):
    x_hi = lax.axis_index("xh")
    tokens = cot_ref.shape[0]
    cot_out_ref[pl.ds(pl.multiple_of(x_hi * tokens, tokens), tokens), :] = cot_ref[...]
    cot_out_ref[pl.ds(pl.multiple_of((1 - x_hi) * tokens, tokens), tokens), :] = cot_got_ref[...]
    rows, padded = mine_ref.shape
    width = padded - 256
    heads = width // HD
    peak_a, total_a = unpacked(mine_ref[:, width:])
    peak_b, total_b = unpacked(other_ref[:, width:])
    top = jnp.maximum(peak_a, peak_b)
    scale_a = jnp.exp(peak_a - top)
    scale_b = jnp.exp(peak_b - top)
    for h in range(heads):
        cols = slice(h * HD, (h + 1) * HD)
        first = mine_ref[:, cols].astype(F32) * scale_a[:, h : h + 1]
        second = other_ref[:, cols].astype(F32) * scale_b[:, h : h + 1]
        out_ref[:, cols] = (first + second).astype(BF16)
    out_ref[:, width:] = packed(top, total_a * scale_a + total_b * scale_b)


def pair(mine, other, cot, cot_got):
    tokens, cols = cot.shape
    return pl.pallas_call(
        pair_kernel,
        out_shape=(
            jax.ShapeDtypeStruct(other.shape, BF16),
            jax.ShapeDtypeStruct((2 * tokens, cols), BF16),
        ),
        compiler_params=params(12),
        name="pair",
    )(mine, other, cot, cot_got)


def merge_kernel(parts_ref, gain_ref, normed_ref, kept_ref, whole):
    rows, padded = parts_ref.shape
    width = padded - 256
    heads = width // HD
    share = 8
    sources = rows // share
    peak, total = unpacked(parts_ref[:, width:])
    peak = peak.reshape(sources, share, heads)
    total = total.reshape(sources, share, heads)
    top = jnp.max(peak, axis=0)
    scale = jnp.exp(peak - top[None])
    total = jnp.sum(total * scale, axis=0)
    scale = scale.reshape(rows, heads)
    sums = jnp.zeros((share, HD), F32)
    last = None
    for h in range(heads):
        cols = slice(h * HD, (h + 1) * HD)
        numer = jnp.zeros((share, HD), F32)
        for at in range(0, rows, 16):
            block = parts_ref[at : at + 16, cols].astype(F32) * scale[at : at + 16, h : h + 1]
            numer = numer + block[:8] + block[8:]
        value = (numer / total[:, h : h + 1]).astype(BF16).astype(F32)
        whole[:, cols] = value
        sums = sums + value
        if h % 2 == 0:
            last = value
        else:
            block = h // 2
            to = (block % 8 * 2 + block // 8) * 16
            kept_ref[to : to + 16, :] = jnp.concatenate([last, value], axis=0).astype(BF16)
    center = jnp.sum(sums, axis=1, keepdims=True) / width
    squares = jnp.zeros((share, HD), F32)
    for h in range(heads):
        shifted = whole[:, h * HD : (h + 1) * HD] - center
        squares = squares + shifted * shifted
    factor = lax.rsqrt(jnp.sum(squares, axis=1, keepdims=True) / width + EPS)
    for h in range(heads):
        cols = slice(h * HD, (h + 1) * HD)
        value = (whole[:, cols] - center) * factor * gain_ref[:, cols].astype(F32)
        twice = jnp.concatenate([value, value], axis=0).astype(BF16)
        for at in range(0, normed_ref.shape[0], 16):
            normed_ref[at : at + 16, cols] = twice


def merge(parts, gain, copies):
    rows, padded = parts.shape
    width = padded - 256
    return pl.pallas_call(
        merge_kernel,
        out_shape=(
            jax.ShapeDtypeStruct((copies * 8, width), BF16),
            jax.ShapeDtypeStruct((width // 16, HD), BF16),
        ),
        scratch_shapes=[pltpu.VMEM((8, width), F32)],
        compiler_params=params(12),
        name="merge",
    )(parts, gain)


def qkv_kernel(mine_ref, other_ref, weight_ref, kv_ref, keep_ref, send_ref, tokens, held, sems):
    core = lax.axis_index("c")
    x_hi = lax.axis_index("xh")
    half, width = mine_ref.shape
    rows = 2 * half
    parts = sems.shape[1]
    depth = width // parts
    copies = [
        [
            pltpu.make_async_copy(
                weight_ref.at[k, pl.ds(part * depth, depth), :],
                held.at[k, pl.ds(part * depth, depth), :],
                sems.at[k, part],
            )
            for part in range(parts)
        ]
        for k in range(3)
    ]
    for k in range(3):
        for copy in copies[k]:
            copy.start()
    tokens[pl.ds(pl.multiple_of(core * half, half), half), :] = mine_ref[...]
    tokens[pl.ds(pl.multiple_of((1 - core) * half, half), half), :] = other_ref[...]
    for k in range(3):
        for copy in copies[k]:
            copy.wait()
        made = dot(tokens[...], held[k], NN)
        first, second = made[:, :HD], made[:, HD:]
        if k == 0:
            keep_ref[...] = jnp.where(x_hi == 0, first, second).astype(BF16)
            send_ref[...] = jnp.where(x_hi == 0, second, first).astype(BF16)
        else:
            cols = slice((k - 1) * HD, k * HD)
            for to in range(16):
                value = first if to < 8 else second
                kv_ref[to * rows : (to + 1) * rows, cols] = value.astype(BF16)


def project(mine, other, weight):
    half, width = mine.shape
    cols = weight.shape[2]
    rows = 2 * half
    parts = 1
    vmem = pl.BlockSpec(memory_space=pltpu.VMEM)
    hbm = pl.BlockSpec(memory_space=pltpu.HBM)
    shapes = [(16 * rows, 2 * HD), (rows, HD), (rows, HD)]
    return pl.pallas_call(
        qkv_kernel,
        in_specs=[vmem, vmem, hbm],
        out_shape=[jax.ShapeDtypeStruct(shape, BF16) for shape in shapes],
        scratch_shapes=[
            pltpu.VMEM((rows, width), BF16),
            pltpu.VMEM((3, width, cols), BF16),
            pltpu.SemaphoreType.DMA((3, parts)),
        ],
        compiler_params=params(50),
        name="project",
    )(mine, other, weight)


def attend_kernel(keep_ref, got_ref, kv_ref, out_ref, scores):
    x_hi = lax.axis_index("xh")
    count = kv_ref.shape[0]
    step = 256
    mixed = []
    for side in range(2):
        query = jnp.where(x_hi == side, keep_ref[...], got_ref[...])
        for at in range(0, count, step):
            scores[:, at : at + step] = dot(query, kv_ref[at : at + step, :HD], NT) / math.sqrt(HD)
        every = scores[...]
        peak = jnp.max(every, axis=1, keepdims=True)
        weights = jnp.exp(every - peak)
        total = jnp.sum(weights, axis=1, keepdims=True)
        mixed.append(dot(weights.astype(BF16), kv_ref[:, HD:], NN) / total)
    for chip in range(8):
        for core in range(2):
            at = core * 64 + chip * 8
            to = (chip * 2 + core) * 16
            out_ref[to : to + 16, :] = jnp.concatenate(
                [mixed[0][at : at + 8], mixed[1][at : at + 8]], axis=0
            ).astype(BF16)


def attend(keep, got, kv):
    return pl.pallas_call(
        attend_kernel,
        out_shape=jax.ShapeDtypeStruct((256, HD), BF16),
        scratch_shapes=[pltpu.VMEM((128, 2048), F32)],
        compiler_params=params(16),
        name="attend",
    )(keep, got, kv)


def output_kernel(parts_ref, weight_ref, out_ref, attended, held, sems):
    bands = parts_ref.shape[0]
    width, cols = weight_ref.shape
    pieces = sems.shape[0]
    depth = width // pieces
    copies = [
        pltpu.make_async_copy(
            weight_ref.at[pl.ds(k * depth, depth), :], held.at[pl.ds(k * depth, depth), :], sems.at[k]
        )
        for k in range(pieces)
    ]
    for copy in copies:
        copy.start()
    for band in range(0, bands, 2):
        to = band * 8
        for source in range(16):
            at = source * 16
            a = parts_ref[band, at : at + 16, :].astype(F32)
            b = parts_ref[band + 1, at : at + 16, :].astype(F32)
            for side in range(2):
                head = 2 * source + side
                rows = slice(side * 8, side * 8 + 8)
                attended[to : to + 16, head * HD : (head + 1) * HD] = jnp.concatenate(
                    [a[rows], b[rows]], axis=0
                ).astype(BF16)
    product = jnp.zeros((attended.shape[0], cols), F32)
    for k in range(pieces):
        copies[k].wait()
        at = slice(k * depth, (k + 1) * depth)
        product = product + dot(attended[:, at], held[at, :], NN)
    half = cols // 2
    count = out_ref.shape[0] // 64
    for band in range(0, bands, 2):
        residual = []
        for b in (band, band + 1):
            kept = parts_ref[b, 256:288, :].astype(F32)
            residual.append(
                jnp.concatenate([kept[k : k + 8] for k in range(0, 32, 8)], axis=1)
            )
        at = band * 8
        layer = (jnp.concatenate(residual, axis=0) + product[at : at + 16]).astype(BF16)
        for to in range(count):
            side = to % 2
            out_ref[to * 64 + at : to * 64 + at + 16, :] = layer[:, side * half : (side + 1) * half]


def output(parts, weight):
    width, cols = weight.shape
    return pl.pallas_call(
        output_kernel,
        in_specs=[pl.BlockSpec(memory_space=pltpu.VMEM), pl.BlockSpec(memory_space=pltpu.HBM)],
        out_shape=jax.ShapeDtypeStruct((16 * 64, cols // 2), BF16),
        scratch_shapes=[
            pltpu.VMEM((64, width), BF16),
            pltpu.VMEM((width, cols), BF16),
            pltpu.SemaphoreType.DMA((8,)),
        ],
        compiler_params=params(50),
        name="output",
    )(parts, weight)


def swap(x, axis):
    return lax.ppermute(x, axis, [(0, 1), (1, 0)])


def exchange(x, axes):
    return lax.all_to_all(x, axes, 0, 0, tiled=True)


def body(patches, patch_weight, var_embed, agg_query, norm_gain, qkv_weight, out_weight, head_cot):
    core = lax.axis_index("c")
    width = out_weight.shape[1]

    cot_got = swap(head_cot, "xh")
    keep, send, cols = embed(
        patches.transpose(0, 2, 1), patch_weight, var_embed, agg_query.T, out_weight
    )
    send, cot_got = lax.optimization_barrier((send, cot_got))
    parts, cot = pair(keep, swap(send, "c"), head_cot, cot_got)
    cot = lax.all_gather(cot, "z", axis=0, tiled=True)
    parts, cols = lax.optimization_barrier((exchange(parts, CHIPS), cols))
    cols = lax.all_gather(cols, VAR, axis=0, tiled=True)
    normed, kept = merge(parts, norm_gain.reshape(1, width), 8)
    normed = exchange(normed, CHIPS)
    kv, query, query_send = project(normed, swap(normed, "c"), qkv_weight.transpose(1, 0, 2))
    query_got = swap(query_send, "xh")
    kv, cot = lax.optimization_barrier((exchange(kv, SEQ), cot))
    attended = attend(query, query_got, kv)
    attended = exchange(attended, VAR + ("xh",))
    sent = jnp.concatenate(
        [jnp.broadcast_to(attended[None], (8, 256, HD)), kept.reshape(8, 32, HD)], axis=1
    )
    got = exchange(sent, "z")
    layer = output(got, cols)
    layer = exchange(layer, CHIPS + ("xh",))
    cot = cot.reshape(8, 2, 8, 2, 8, 384).transpose(3, 2, 1, 0, 4, 5).reshape(2, 1024, 384)
    first = lax.dynamic_index_in_dim(cot, core, 0, keepdims=False)
    second = lax.dynamic_index_in_dim(cot, 1 - core, 0, keepdims=False)
    return dot(layer, first, TN) + dot(swap(layer, "c"), second, TN)


def solution(mesh):
    whole = Mesh(mesh.devices.reshape(4, 2, 2, 2, 8), ("y", "xl", "c", "xh", "z"))
    return jax.shard_map(
        body,
        mesh=whole,
        in_specs=(
            P(VAR, SEQ, None),
            P(VAR, None, None),
            P(VAR, None),
            P(),
            P(),
            P(None, None, VAR),
            P(VAR, None),
            P(SEQ, VAR),
        ),
        out_specs=P(SEQ, VAR),
        check_vma=False,
    )
```

```python
import math

import jax
import jax.numpy as jnp
from jax import lax
from jax.experimental import pallas as pl
from jax.experimental.pallas import tpu as pltpu
from jax.sharding import Mesh, PartitionSpec as P

EPS = 1e-05
HD = 128
F32 = jnp.float32
BF16 = jnp.bfloat16
VAR = ("y", "xl", "c")
CHIPS = ("y", "xl")
SEQ = ("xh", "z")
NT = (((1,), (1,)), ((), ()))
TN = (((0,), (0,)), ((), ()))
NN = (((1,), (0,)), ((), ()))
MB = 1024 * 1024


def dot(a, b, dims):
    return lax.dot_general(a, b, dims, preferred_element_type=F32)


def params(megabytes):
    return pltpu.CompilerParams(vmem_limit_bytes=megabytes * MB)


def packed(peak, total):
    blank = jnp.zeros_like(peak)
    return jnp.concatenate([peak, total, blank, blank], axis=1)


def unpacked(stats):
    return stats[:, 0:32], stats[:, 32:64]


def embed_kernel(
    pixels_hbm, weight_ref, shift_hbm, query_hbm, rows_ref, keep_ref, send_ref, cols_ref,
    pixels_ref, shift_ref, query_ref, embedded, scores, held, keep, send, sems, small_sems, out_sems,
):
    core = lax.axis_index("c")
    z = lax.axis_index("z")
    count, rows, width = embedded.shape
    heads = query_ref.shape[0]
    half = rows // 2
    small = [
        pltpu.make_async_copy(pixels_hbm, pixels_ref, small_sems.at[0]),
        pltpu.make_async_copy(shift_hbm, shift_ref, small_sems.at[1]),
        pltpu.make_async_copy(query_hbm, query_ref, small_sems.at[2]),
    ]
    copies = [
        pltpu.make_async_copy(weight_ref.at[v], held.at[v], sems.at[v]) for v in range(count)
    ]
    for copy in [small[0], copies[0], small[1], small[2]] + copies[1:]:
        copy.start()
    cut = cols_ref.shape[1] // 2
    slices = []
    for side in range(2):
        place = pl.multiple_of(side * (width // 2) + z * cut, cut)
        slices.append(
            pltpu.make_async_copy(
                rows_ref.at[:, pl.ds(place, cut)],
                cols_ref.at[:, pl.ds(side * cut, cut)],
                small_sems.at[3 + side],
            )
        )
        slices[side].start()
    new = lax.broadcasted_iota(jnp.int32, (rows, rows), 0)
    old = lax.broadcasted_iota(jnp.int32, (rows, rows), 1)
    group = (new % half) // 8 * 2 + jnp.where(new < half, core, 1 - core)
    order = jnp.where(old == group * 8 + new % 8, 1.0, 0.0).astype(BF16)
    step = 1024
    small[0].wait()
    for v in range(count):
        tokens = dot(order, pixels_ref[v], NT).astype(BF16)
        if v == 0:
            small[1].wait()
            small[2].wait()
        if v % 2 == 0:
            for copy in copies[v : v + 2]:
                copy.wait()
        total = jnp.zeros((rows, heads), F32)
        for at in range(0, width, step):
            block = dot(tokens, held[v, :, at : at + step], NN)
            shift = shift_ref[v : v + 1, at : at + step].astype(F32)
            block = (block + shift).astype(BF16)
            embedded[v, :, at : at + step] = block
            total = total + dot(block, query_ref[:, at : at + step], NT)
        scores[v] = total / math.sqrt(HD)
    every = scores[...]
    peak = jnp.max(every, axis=0)
    weights = jnp.exp(every - peak[None])
    total = jnp.sum(weights, axis=0)
    keep[:, width:] = packed(peak[:half], total[:half])
    send[:, width:] = packed(peak[half:], total[half:])
    leaving = []

    def leave(place, size):
        at = len(leaving) // 2
        for side, (source, target) in enumerate(((keep, keep_ref), (send, send_ref))):
            copy = pltpu.make_async_copy(
                source.at[:, pl.ds(place, size)], target.at[:, pl.ds(place, size)], out_sems.at[side, at]
            )
            copy.start()
            leaving.append(copy)

    leave(width, 128)
    for h in range(heads):
        cols = slice(h * HD, (h + 1) * HD)
        numer = weights[0][:, h : h + 1] * embedded[0, :, cols].astype(F32)
        for v in range(1, count):
            numer = numer + weights[v][:, h : h + 1] * embedded[v, :, cols].astype(F32)
        keep[:, cols] = numer[:half]
        send[:, cols] = numer[half:]
        if h % 8 == 7:
            leave((h - 7) * HD, 8 * HD)
    for copy in slices + leaving:
        copy.wait()


def embed(pixels, weight, shift, query, out_weight):
    count, depth, rows = pixels.shape
    width = weight.shape[2]
    heads = query.shape[0]
    half = rows // 2
    hbm = pl.BlockSpec(memory_space=pltpu.HBM)
    part = jax.ShapeDtypeStruct((half, width + 128), F32)
    return pl.pallas_call(
        embed_kernel,
        in_specs=[hbm] * 5,
        out_specs=[hbm] * 3,
        out_shape=(part, part, jax.ShapeDtypeStruct((out_weight.shape[0], width // 8), BF16)),
        scratch_shapes=[
            pltpu.VMEM((count, depth, rows), BF16),
            pltpu.VMEM((count, width), BF16),
            pltpu.VMEM((heads, width), BF16),
            pltpu.VMEM((count, rows, width), BF16),
            pltpu.VMEM((count, rows, heads), F32),
            pltpu.VMEM((count, depth, width), BF16),
            pltpu.VMEM((half, width + 128), F32),
            pltpu.VMEM((half, width + 128), F32),
            pltpu.SemaphoreType.DMA((count,)),
            pltpu.SemaphoreType.DMA((5,)),
            pltpu.SemaphoreType.DMA((2, 5)),
        ],
        compiler_params=params(60),
        cost_estimate=pl.CostEstimate(
            flops=2 * count * rows * width * (depth + heads),
            bytes_accessed=4 * count * depth * width,
            transcendentals=count * rows * heads,
        ),
        name="embed",
    )(pixels, weight, shift, query, out_weight)


def pair_kernel(mine_ref, other_ref, cot_ref, cot_got_ref, out_ref, cot_out_ref):
    x_hi = lax.axis_index("xh")
    tokens = cot_ref.shape[0]
    cot_out_ref[pl.ds(pl.multiple_of(x_hi * tokens, tokens), tokens), :] = cot_ref[...]
    cot_out_ref[pl.ds(pl.multiple_of((1 - x_hi) * tokens, tokens), tokens), :] = cot_got_ref[...]
    rows, padded = mine_ref.shape
    width = padded - 128
    heads = width // HD
    peak_a, total_a = unpacked(mine_ref[:, width:])
    peak_b, total_b = unpacked(other_ref[:, width:])
    top = jnp.maximum(peak_a, peak_b)
    scale_a = jnp.exp(peak_a - top)
    scale_b = jnp.exp(peak_b - top)
    for h in range(heads):
        cols = slice(h * HD, (h + 1) * HD)
        first = mine_ref[:, cols] * scale_a[:, h : h + 1]
        second = other_ref[:, cols] * scale_b[:, h : h + 1]
        out_ref[:, cols] = first + second
    out_ref[:, width:] = packed(top, total_a * scale_a + total_b * scale_b)


def pair(mine, other, cot, cot_got):
    tokens, cols = cot.shape
    return pl.pallas_call(
        pair_kernel,
        out_shape=(
            jax.ShapeDtypeStruct(other.shape, F32),
            jax.ShapeDtypeStruct((2 * tokens, cols), BF16),
        ),
        compiler_params=params(12),
        name="pair",
    )(mine, other, cot, cot_got)


def merge_kernel(parts_ref, gain_ref, normed_ref, kept_ref, whole):
    rows, padded = parts_ref.shape
    width = padded - 128
    heads = width // HD
    share = 8
    sources = rows // share
    peak, total = unpacked(parts_ref[:, width:])
    peak = peak.reshape(sources, share, heads)
    total = total.reshape(sources, share, heads)
    top = jnp.max(peak, axis=0)
    scale = jnp.exp(peak - top[None])
    total = jnp.sum(total * scale, axis=0)
    scale = scale.reshape(rows, heads)
    sums = jnp.zeros((share, HD), F32)
    last = None
    for h in range(heads):
        cols = slice(h * HD, (h + 1) * HD)
        numer = jnp.zeros((share, HD), F32)
        for at in range(0, rows, share):
            numer = numer + parts_ref[at : at + share, cols] * scale[at : at + share, h : h + 1]
        value = (numer / total[:, h : h + 1]).astype(BF16).astype(F32)
        whole[:, cols] = value
        sums = sums + value
        if h % 2 == 0:
            last = value
        else:
            block = h // 2
            to = (block % 8 * 2 + block // 8) * 16
            kept_ref[to : to + 16, :] = jnp.concatenate([last, value], axis=0).astype(BF16)
    center = jnp.sum(sums, axis=1, keepdims=True) / width
    squares = jnp.zeros((share, HD), F32)
    for h in range(heads):
        shifted = whole[:, h * HD : (h + 1) * HD] - center
        squares = squares + shifted * shifted
    factor = lax.rsqrt(jnp.sum(squares, axis=1, keepdims=True) / width + EPS)
    for h in range(heads):
        cols = slice(h * HD, (h + 1) * HD)
        value = (whole[:, cols] - center) * factor * gain_ref[:, cols].astype(F32)
        twice = jnp.concatenate([value, value], axis=0).astype(BF16)
        for at in range(0, normed_ref.shape[0], 16):
            normed_ref[at : at + 16, cols] = twice


def merge(parts, gain, copies):
    rows, padded = parts.shape
    width = padded - 128
    return pl.pallas_call(
        merge_kernel,
        out_shape=(
            jax.ShapeDtypeStruct((copies * 8, width), BF16),
            jax.ShapeDtypeStruct((width // 16, HD), BF16),
        ),
        scratch_shapes=[pltpu.VMEM((8, width), F32)],
        compiler_params=params(12),
        name="merge",
    )(parts, gain)


def qkv_kernel(mine_ref, other_ref, weight_ref, kv_ref, keep_ref, send_ref, tokens, held, sems):
    core = lax.axis_index("c")
    x_hi = lax.axis_index("xh")
    half, width = mine_ref.shape
    rows = 2 * half
    parts = sems.shape[1]
    depth = width // parts
    copies = [
        [
            pltpu.make_async_copy(
                weight_ref.at[k, pl.ds(part * depth, depth), :],
                held.at[k, pl.ds(part * depth, depth), :],
                sems.at[k, part],
            )
            for part in range(parts)
        ]
        for k in range(3)
    ]
    for k in range(3):
        for copy in copies[k]:
            copy.start()
    tokens[pl.ds(pl.multiple_of(core * half, half), half), :] = mine_ref[...]
    tokens[pl.ds(pl.multiple_of((1 - core) * half, half), half), :] = other_ref[...]
    for k in range(3):
        for copy in copies[k]:
            copy.wait()
        made = dot(tokens[...], held[k], NN)
        first, second = made[:, :HD], made[:, HD:]
        if k == 0:
            keep_ref[...] = jnp.where(x_hi == 0, first, second).astype(BF16)
            send_ref[...] = jnp.where(x_hi == 0, second, first).astype(BF16)
        else:
            cols = slice((k - 1) * HD, k * HD)
            for to in range(16):
                value = first if to < 8 else second
                kv_ref[to * rows : (to + 1) * rows, cols] = value.astype(BF16)


def project(mine, other, weight):
    half, width = mine.shape
    cols = weight.shape[2]
    rows = 2 * half
    parts = 1
    vmem = pl.BlockSpec(memory_space=pltpu.VMEM)
    hbm = pl.BlockSpec(memory_space=pltpu.HBM)
    shapes = [(16 * rows, 2 * HD), (rows, HD), (rows, HD)]
    return pl.pallas_call(
        qkv_kernel,
        in_specs=[vmem, vmem, hbm],
        out_shape=[jax.ShapeDtypeStruct(shape, BF16) for shape in shapes],
        scratch_shapes=[
            pltpu.VMEM((rows, width), BF16),
            pltpu.VMEM((3, width, cols), BF16),
            pltpu.SemaphoreType.DMA((3, parts)),
        ],
        compiler_params=params(50),
        name="project",
    )(mine, other, weight)


def attend_kernel(keep_ref, got_ref, kv_ref, out_ref, scores):
    x_hi = lax.axis_index("xh")
    count = kv_ref.shape[0]
    step = 256
    mixed = []
    for side in range(2):
        query = jnp.where(x_hi == side, keep_ref[...], got_ref[...])
        for at in range(0, count, step):
            scores[:, at : at + step] = dot(query, kv_ref[at : at + step, :HD], NT) / math.sqrt(HD)
        every = scores[...]
        peak = jnp.max(every, axis=1, keepdims=True)
        weights = jnp.exp(every - peak)
        total = jnp.sum(weights, axis=1, keepdims=True)
        mixed.append(dot(weights.astype(BF16), kv_ref[:, HD:], NN) / total)
    for chip in range(8):
        for core in range(2):
            at = core * 64 + chip * 8
            to = (chip * 2 + core) * 16
            out_ref[to : to + 16, :] = jnp.concatenate(
                [mixed[0][at : at + 8], mixed[1][at : at + 8]], axis=0
            ).astype(BF16)


def attend(keep, got, kv):
    return pl.pallas_call(
        attend_kernel,
        out_shape=jax.ShapeDtypeStruct((256, HD), BF16),
        scratch_shapes=[pltpu.VMEM((128, 2048), F32)],
        compiler_params=params(16),
        name="attend",
    )(keep, got, kv)


def output_kernel(parts_ref, weight_ref, out_ref, attended, held, sems):
    bands = parts_ref.shape[0]
    width, cols = weight_ref.shape
    pieces = sems.shape[0]
    depth = width // pieces
    copies = [
        pltpu.make_async_copy(
            weight_ref.at[pl.ds(k * depth, depth), :], held.at[pl.ds(k * depth, depth), :], sems.at[k]
        )
        for k in range(pieces)
    ]
    for copy in copies:
        copy.start()
    for band in range(0, bands, 2):
        to = band * 8
        for source in range(16):
            at = source * 16
            a = parts_ref[band, at : at + 16, :].astype(F32)
            b = parts_ref[band + 1, at : at + 16, :].astype(F32)
            for side in range(2):
                head = 2 * source + side
                rows = slice(side * 8, side * 8 + 8)
                attended[to : to + 16, head * HD : (head + 1) * HD] = jnp.concatenate(
                    [a[rows], b[rows]], axis=0
                ).astype(BF16)
    product = jnp.zeros((attended.shape[0], cols), F32)
    for k in range(pieces):
        copies[k].wait()
        at = slice(k * depth, (k + 1) * depth)
        product = product + dot(attended[:, at], held[at, :], NN)
    half = cols // 2
    count = out_ref.shape[0] // 64
    for band in range(0, bands, 2):
        residual = []
        for b in (band, band + 1):
            kept = parts_ref[b, 256:288, :].astype(F32)
            residual.append(
                jnp.concatenate([kept[k : k + 8] for k in range(0, 32, 8)], axis=1)
            )
        at = band * 8
        layer = (jnp.concatenate(residual, axis=0) + product[at : at + 16]).astype(BF16)
        for to in range(count):
            side = to % 2
            out_ref[to * 64 + at : to * 64 + at + 16, :] = layer[:, side * half : (side + 1) * half]


def output(parts, weight):
    width, cols = weight.shape
    return pl.pallas_call(
        output_kernel,
        in_specs=[pl.BlockSpec(memory_space=pltpu.VMEM), pl.BlockSpec(memory_space=pltpu.HBM)],
        out_shape=jax.ShapeDtypeStruct((16 * 64, cols // 2), BF16),
        scratch_shapes=[
            pltpu.VMEM((64, width), BF16),
            pltpu.VMEM((width, cols), BF16),
            pltpu.SemaphoreType.DMA((8,)),
        ],
        compiler_params=params(50),
        name="output",
    )(parts, weight)


def swap(x, axis):
    return lax.ppermute(x, axis, [(0, 1), (1, 0)])


def exchange(x, axes):
    return lax.all_to_all(x, axes, 0, 0, tiled=True)


def body(patches, patch_weight, var_embed, agg_query, norm_gain, qkv_weight, out_weight, head_cot):
    core = lax.axis_index("c")
    width = out_weight.shape[1]

    cot_got = swap(head_cot, "xh")
    keep, send, cols = embed(
        patches.transpose(0, 2, 1), patch_weight, var_embed, agg_query.T, out_weight
    )
    send, cot_got = lax.optimization_barrier((send, cot_got))
    parts, cot = pair(keep, swap(send, "c"), head_cot, cot_got)
    cot = lax.all_gather(cot, "z", axis=0, tiled=True)
    parts, cols = lax.optimization_barrier((exchange(parts, CHIPS), cols))
    cols = lax.all_gather(cols, VAR, axis=0, tiled=True)
    normed, kept = merge(parts, norm_gain.reshape(1, width), 8)
    normed = exchange(normed, CHIPS)
    kv, query, query_send = project(normed, swap(normed, "c"), qkv_weight.transpose(1, 0, 2))
    query_got = swap(query_send, "xh")
    kv, cot = lax.optimization_barrier((exchange(kv, SEQ), cot))
    attended = attend(query, query_got, kv)
    attended = exchange(attended, VAR + ("xh",))
    sent = jnp.concatenate(
        [jnp.broadcast_to(attended[None], (8, 256, HD)), kept.reshape(8, 32, HD)], axis=1
    )
    got = exchange(sent, "z")
    layer = output(got, cols)
    layer = exchange(layer, CHIPS + ("xh",))
    cot = cot.reshape(8, 2, 8, 2, 8, 384).transpose(3, 2, 1, 0, 4, 5).reshape(2, 1024, 384)
    first = lax.dynamic_index_in_dim(cot, core, 0, keepdims=False)
    second = lax.dynamic_index_in_dim(cot, 1 - core, 0, keepdims=False)
    return dot(layer, first, TN) + dot(swap(layer, "c"), second, TN)


def solution(mesh):
    whole = Mesh(mesh.devices.reshape(4, 2, 2, 2, 8), ("y", "xl", "c", "xh", "z"))
    return jax.shard_map(
        body,
        mesh=whole,
        in_specs=(
            P(VAR, SEQ, None),
            P(VAR, None, None),
            P(VAR, None),
            P(),
            P(),
            P(None, None, VAR),
            P(VAR, None),
            P(SEQ, VAR),
        ),
        out_specs=P(SEQ, VAR),
        check_vma=False,
    )
```

```python
import math

import jax
import jax.numpy as jnp
from jax import lax
from jax.experimental import pallas as pl
from jax.experimental.pallas import tpu as pltpu
from jax.sharding import Mesh, PartitionSpec as P

EPS = 1e-05
HD = 128
F32 = jnp.float32
BF16 = jnp.bfloat16
VAR = ("y", "xl", "c")
CHIPS = ("y", "xl")
SEQ = ("xh", "z")
NT = (((1,), (1,)), ((), ()))
TN = (((0,), (0,)), ((), ()))
NN = (((1,), (0,)), ((), ()))
MB = 1024 * 1024


def dot(a, b, dims):
    return lax.dot_general(a, b, dims, preferred_element_type=F32)


def params(megabytes):
    return pltpu.CompilerParams(vmem_limit_bytes=megabytes * MB)


def packed(peak, total):
    blank = jnp.zeros_like(peak)
    return jnp.concatenate([peak, total, blank, blank], axis=1)


def unpacked(stats):
    return stats[:, 0:32], stats[:, 32:64]


def embed_kernel(
    pixels_hbm, weight_ref, shift_hbm, query_hbm, rows_ref, keep_ref, send_ref, cols_ref,
    pixels_ref, shift_ref, query_ref, embedded, scores, held, keep, send, sems, small_sems, out_sems,
):
    core = lax.axis_index("c")
    z = lax.axis_index("z")
    count, rows, width = embedded.shape
    heads = query_ref.shape[0]
    half = rows // 2
    small = [
        pltpu.make_async_copy(pixels_hbm, pixels_ref, small_sems.at[0]),
        pltpu.make_async_copy(shift_hbm, shift_ref, small_sems.at[1]),
        pltpu.make_async_copy(query_hbm, query_ref, small_sems.at[2]),
    ]
    copies = [
        pltpu.make_async_copy(weight_ref.at[v], held.at[v], sems.at[v]) for v in range(count)
    ]
    for copy in [small[0], copies[0], small[1], small[2]] + copies[1:]:
        copy.start()
    cut = cols_ref.shape[1] // 2
    slices = []
    for side in range(2):
        place = pl.multiple_of(side * (width // 2) + z * cut, cut)
        slices.append(
            pltpu.make_async_copy(
                rows_ref.at[:, pl.ds(place, cut)],
                cols_ref.at[:, pl.ds(side * cut, cut)],
                small_sems.at[3 + side],
            )
        )
        slices[side].start()
    new = lax.broadcasted_iota(jnp.int32, (rows, rows), 0)
    old = lax.broadcasted_iota(jnp.int32, (rows, rows), 1)
    group = (new % half) // 8 * 2 + jnp.where(new < half, core, 1 - core)
    order = jnp.where(old == group * 8 + new % 8, 1.0, 0.0).astype(BF16)
    step = 1024
    small[0].wait()
    for v in range(count):
        tokens = dot(order, pixels_ref[v], NT).astype(BF16)
        if v == 0:
            small[1].wait()
            small[2].wait()
        if v % 2 == 0:
            for copy in copies[v : v + 2]:
                copy.wait()
        total = jnp.zeros((rows, heads), F32)
        for at in range(0, width, step):
            block = dot(tokens, held[v, :, at : at + step], NN)
            shift = shift_ref[v : v + 1, at : at + step].astype(F32)
            block = (block + shift).astype(BF16)
            embedded[v, :, at : at + step] = block
            total = total + dot(block, query_ref[:, at : at + step], NT)
        scores[v] = total / math.sqrt(HD)
    every = scores[...]
    peak = jnp.max(every, axis=0)
    weights = jnp.exp(every - peak[None])
    total = jnp.sum(weights, axis=0)
    keep[:, width:] = packed(peak[:half], total[:half])
    send[:, width:] = packed(peak[half:], total[half:])
    leaving = []

    def leave(place, size):
        at = len(leaving) // 2
        for side, (source, target) in enumerate(((keep, keep_ref), (send, send_ref))):
            copy = pltpu.make_async_copy(
                source.at[:, pl.ds(place, size)], target.at[:, pl.ds(place, size)], out_sems.at[side, at]
            )
            copy.start()
            leaving.append(copy)

    leave(width, 128)
    for h in range(heads):
        cols = slice(h * HD, (h + 1) * HD)
        numer = weights[0][:, h : h + 1] * embedded[0, :, cols].astype(F32)
        for v in range(1, count):
            numer = numer + weights[v][:, h : h + 1] * embedded[v, :, cols].astype(F32)
        keep[:, cols] = numer[:half]
        send[:, cols] = numer[half:]
        if h % 8 == 7:
            leave((h - 7) * HD, 8 * HD)
    for copy in slices + leaving:
        copy.wait()


def embed(pixels, weight, shift, query, out_weight):
    count, depth, rows = pixels.shape
    width = weight.shape[2]
    heads = query.shape[0]
    half = rows // 2
    hbm = pl.BlockSpec(memory_space=pltpu.HBM)
    part = jax.ShapeDtypeStruct((half, width + 128), F32)
    return pl.pallas_call(
        embed_kernel,
        in_specs=[hbm] * 5,
        out_specs=[hbm] * 3,
        out_shape=(part, part, jax.ShapeDtypeStruct((out_weight.shape[0], width // 8), BF16)),
        scratch_shapes=[
            pltpu.VMEM((count, depth, rows), BF16),
            pltpu.VMEM((count, width), BF16),
            pltpu.VMEM((heads, width), BF16),
            pltpu.VMEM((count, rows, width), BF16),
            pltpu.VMEM((count, rows, heads), F32),
            pltpu.VMEM((count, depth, width), BF16),
            pltpu.VMEM((half, width + 128), F32),
            pltpu.VMEM((half, width + 128), F32),
            pltpu.SemaphoreType.DMA((count,)),
            pltpu.SemaphoreType.DMA((5,)),
            pltpu.SemaphoreType.DMA((2, 5)),
        ],
        compiler_params=params(60),
        cost_estimate=pl.CostEstimate(
            flops=2 * count * rows * width * (depth + heads),
            bytes_accessed=4 * count * depth * width,
            transcendentals=count * rows * heads,
        ),
        name="embed",
    )(pixels, weight, shift, query, out_weight)


def stage_kernel(source_ref, target_ref):
    target_ref[...] = source_ref[...]


def stage(source):
    return pl.pallas_call(
        stage_kernel,
        out_shape=jax.ShapeDtypeStruct(source.shape, F32),
        compiler_params=params(12),
        cost_estimate=pl.CostEstimate(flops=0, bytes_accessed=8 * MB, transcendentals=0),
        name="stage",
    )(source)


def pair_kernel(mine_ref, other_ref, cot_ref, cot_got_ref, out_ref, cot_out_ref):
    x_hi = lax.axis_index("xh")
    tokens = cot_ref.shape[0]
    cot_out_ref[pl.ds(pl.multiple_of(x_hi * tokens, tokens), tokens), :] = cot_ref[...]
    cot_out_ref[pl.ds(pl.multiple_of((1 - x_hi) * tokens, tokens), tokens), :] = cot_got_ref[...]
    rows, padded = mine_ref.shape
    width = padded - 128
    heads = width // HD
    peak_a, total_a = unpacked(mine_ref[:, width:])
    peak_b, total_b = unpacked(other_ref[:, width:])
    top = jnp.maximum(peak_a, peak_b)
    scale_a = jnp.exp(peak_a - top)
    scale_b = jnp.exp(peak_b - top)
    for h in range(heads):
        cols = slice(h * HD, (h + 1) * HD)
        first = mine_ref[:, cols] * scale_a[:, h : h + 1]
        second = other_ref[:, cols] * scale_b[:, h : h + 1]
        out_ref[:, cols] = first + second
    out_ref[:, width:] = packed(top, total_a * scale_a + total_b * scale_b)


def pair(mine, other, cot, cot_got):
    tokens, cols = cot.shape
    return pl.pallas_call(
        pair_kernel,
        out_shape=(
            jax.ShapeDtypeStruct(other.shape, F32),
            jax.ShapeDtypeStruct((2 * tokens, cols), BF16),
        ),
        compiler_params=params(12),
        name="pair",
    )(mine, other, cot, cot_got)


def merge_kernel(parts_ref, gain_ref, normed_ref, kept_ref, whole):
    rows, padded = parts_ref.shape
    width = padded - 128
    heads = width // HD
    share = 8
    sources = rows // share
    peak, total = unpacked(parts_ref[:, width:])
    peak = peak.reshape(sources, share, heads)
    total = total.reshape(sources, share, heads)
    top = jnp.max(peak, axis=0)
    scale = jnp.exp(peak - top[None])
    total = jnp.sum(total * scale, axis=0)
    scale = scale.reshape(rows, heads)
    sums = jnp.zeros((share, HD), F32)
    last = None
    for h in range(heads):
        cols = slice(h * HD, (h + 1) * HD)
        numer = jnp.zeros((share, HD), F32)
        for at in range(0, rows, share):
            numer = numer + parts_ref[at : at + share, cols] * scale[at : at + share, h : h + 1]
        value = (numer / total[:, h : h + 1]).astype(BF16).astype(F32)
        whole[:, cols] = value
        sums = sums + value
        if h % 2 == 0:
            last = value
        else:
            block = h // 2
            to = (block % 8 * 2 + block // 8) * 16
            kept_ref[to : to + 16, :] = jnp.concatenate([last, value], axis=0).astype(BF16)
    center = jnp.sum(sums, axis=1, keepdims=True) / width
    squares = jnp.zeros((share, HD), F32)
    for h in range(heads):
        shifted = whole[:, h * HD : (h + 1) * HD] - center
        squares = squares + shifted * shifted
    factor = lax.rsqrt(jnp.sum(squares, axis=1, keepdims=True) / width + EPS)
    for h in range(heads):
        cols = slice(h * HD, (h + 1) * HD)
        value = (whole[:, cols] - center) * factor * gain_ref[:, cols].astype(F32)
        twice = jnp.concatenate([value, value], axis=0).astype(BF16)
        for at in range(0, normed_ref.shape[0], 16):
            normed_ref[at : at + 16, cols] = twice


def merge(parts, gain, copies):
    rows, padded = parts.shape
    width = padded - 128
    return pl.pallas_call(
        merge_kernel,
        out_shape=(
            jax.ShapeDtypeStruct((copies * 8, width), BF16),
            jax.ShapeDtypeStruct((width // 16, HD), BF16),
        ),
        scratch_shapes=[pltpu.VMEM((8, width), F32)],
        compiler_params=params(12),
        name="merge",
    )(parts, gain)


def qkv_kernel(mine_ref, other_ref, weight_ref, kv_ref, keep_ref, send_ref, tokens, held, sems):
    core = lax.axis_index("c")
    x_hi = lax.axis_index("xh")
    half, width = mine_ref.shape
    rows = 2 * half
    parts = sems.shape[1]
    depth = width // parts
    copies = [
        [
            pltpu.make_async_copy(
                weight_ref.at[k, pl.ds(part * depth, depth), :],
                held.at[k, pl.ds(part * depth, depth), :],
                sems.at[k, part],
            )
            for part in range(parts)
        ]
        for k in range(3)
    ]
    for k in range(3):
        for copy in copies[k]:
            copy.start()
    tokens[pl.ds(pl.multiple_of(core * half, half), half), :] = mine_ref[...]
    tokens[pl.ds(pl.multiple_of((1 - core) * half, half), half), :] = other_ref[...]
    for k in range(3):
        for copy in copies[k]:
            copy.wait()
        made = dot(tokens[...], held[k], NN)
        first, second = made[:, :HD], made[:, HD:]
        if k == 0:
            keep_ref[...] = jnp.where(x_hi == 0, first, second).astype(BF16)
            send_ref[...] = jnp.where(x_hi == 0, second, first).astype(BF16)
        else:
            cols = slice((k - 1) * HD, k * HD)
            for to in range(16):
                value = first if to < 8 else second
                kv_ref[to * rows : (to + 1) * rows, cols] = value.astype(BF16)


def project(mine, other, weight):
    half, width = mine.shape
    cols = weight.shape[2]
    rows = 2 * half
    parts = 1
    vmem = pl.BlockSpec(memory_space=pltpu.VMEM)
    hbm = pl.BlockSpec(memory_space=pltpu.HBM)
    shapes = [(16 * rows, 2 * HD), (rows, HD), (rows, HD)]
    return pl.pallas_call(
        qkv_kernel,
        in_specs=[vmem, vmem, hbm],
        out_shape=[jax.ShapeDtypeStruct(shape, BF16) for shape in shapes],
        scratch_shapes=[
            pltpu.VMEM((rows, width), BF16),
            pltpu.VMEM((3, width, cols), BF16),
            pltpu.SemaphoreType.DMA((3, parts)),
        ],
        compiler_params=params(50),
        name="project",
    )(mine, other, weight)


def attend_kernel(keep_ref, got_ref, kv_ref, out_ref, scores):
    x_hi = lax.axis_index("xh")
    count = kv_ref.shape[0]
    step = 256
    mixed = []
    for side in range(2):
        query = jnp.where(x_hi == side, keep_ref[...], got_ref[...])
        for at in range(0, count, step):
            scores[:, at : at + step] = dot(query, kv_ref[at : at + step, :HD], NT) / math.sqrt(HD)
        every = scores[...]
        peak = jnp.max(every, axis=1, keepdims=True)
        weights = jnp.exp(every - peak)
        total = jnp.sum(weights, axis=1, keepdims=True)
        mixed.append(dot(weights.astype(BF16), kv_ref[:, HD:], NN) / total)
    for chip in range(8):
        for core in range(2):
            at = core * 64 + chip * 8
            to = (chip * 2 + core) * 16
            out_ref[to : to + 16, :] = jnp.concatenate(
                [mixed[0][at : at + 8], mixed[1][at : at + 8]], axis=0
            ).astype(BF16)


def attend(keep, got, kv):
    return pl.pallas_call(
        attend_kernel,
        out_shape=jax.ShapeDtypeStruct((256, HD), BF16),
        scratch_shapes=[pltpu.VMEM((128, 2048), F32)],
        compiler_params=params(16),
        name="attend",
    )(keep, got, kv)


def output_kernel(parts_ref, weight_ref, out_ref, attended, held, sems):
    bands = parts_ref.shape[0]
    width, cols = weight_ref.shape
    pieces = sems.shape[0]
    depth = width // pieces
    copies = [
        pltpu.make_async_copy(
            weight_ref.at[pl.ds(k * depth, depth), :], held.at[pl.ds(k * depth, depth), :], sems.at[k]
        )
        for k in range(pieces)
    ]
    for copy in copies:
        copy.start()
    for band in range(0, bands, 2):
        to = band * 8
        for source in range(16):
            at = source * 16
            a = parts_ref[band, at : at + 16, :].astype(F32)
            b = parts_ref[band + 1, at : at + 16, :].astype(F32)
            for side in range(2):
                head = 2 * source + side
                rows = slice(side * 8, side * 8 + 8)
                attended[to : to + 16, head * HD : (head + 1) * HD] = jnp.concatenate(
                    [a[rows], b[rows]], axis=0
                ).astype(BF16)
    product = jnp.zeros((attended.shape[0], cols), F32)
    for k in range(pieces):
        copies[k].wait()
        at = slice(k * depth, (k + 1) * depth)
        product = product + dot(attended[:, at], held[at, :], NN)
    half = cols // 2
    count = out_ref.shape[0] // 64
    for band in range(0, bands, 2):
        residual = []
        for b in (band, band + 1):
            kept = parts_ref[b, 256:288, :].astype(F32)
            residual.append(
                jnp.concatenate([kept[k : k + 8] for k in range(0, 32, 8)], axis=1)
            )
        at = band * 8
        layer = (jnp.concatenate(residual, axis=0) + product[at : at + 16]).astype(BF16)
        for to in range(count):
            side = to % 2
            out_ref[to * 64 + at : to * 64 + at + 16, :] = layer[:, side * half : (side + 1) * half]


def output(parts, weight):
    width, cols = weight.shape
    return pl.pallas_call(
        output_kernel,
        in_specs=[pl.BlockSpec(memory_space=pltpu.VMEM), pl.BlockSpec(memory_space=pltpu.HBM)],
        out_shape=jax.ShapeDtypeStruct((16 * 64, cols // 2), BF16),
        scratch_shapes=[
            pltpu.VMEM((64, width), BF16),
            pltpu.VMEM((width, cols), BF16),
            pltpu.SemaphoreType.DMA((8,)),
        ],
        compiler_params=params(50),
        name="output",
    )(parts, weight)


def swap(x, axis):
    return lax.ppermute(x, axis, [(0, 1), (1, 0)])


def exchange(x, axes):
    return lax.all_to_all(x, axes, 0, 0, tiled=True)


def body(patches, patch_weight, var_embed, agg_query, norm_gain, qkv_weight, out_weight, head_cot):
    core = lax.axis_index("c")
    width = out_weight.shape[1]

    cot_got = swap(head_cot, "xh")
    keep, send, cols = embed(
        patches.transpose(0, 2, 1), patch_weight, var_embed, agg_query.T, out_weight
    )
    send, cot_got = lax.optimization_barrier((send, cot_got))
    parts, cot = pair(stage(keep), swap(send, "c"), head_cot, cot_got)
    cot = lax.all_gather(cot, "z", axis=0, tiled=True)
    parts, cols = lax.optimization_barrier((exchange(parts, CHIPS), cols))
    cols = lax.all_gather(cols, VAR, axis=0, tiled=True)
    normed, kept = merge(parts, norm_gain.reshape(1, width), 8)
    normed = exchange(normed, CHIPS)
    kv, query, query_send = project(normed, swap(normed, "c"), qkv_weight.transpose(1, 0, 2))
    query_got = swap(query_send, "xh")
    kv, cot = lax.optimization_barrier((exchange(kv, SEQ), cot))
    attended = attend(query, query_got, kv)
    attended = exchange(attended, VAR + ("xh",))
    sent = jnp.concatenate(
        [jnp.broadcast_to(attended[None], (8, 256, HD)), kept.reshape(8, 32, HD)], axis=1
    )
    got = exchange(sent, "z")
    layer = output(got, cols)
    layer = exchange(layer, CHIPS + ("xh",))
    cot = cot.reshape(8, 2, 8, 2, 8, 384).transpose(3, 2, 1, 0, 4, 5).reshape(2, 1024, 384)
    first = lax.dynamic_index_in_dim(cot, core, 0, keepdims=False)
    second = lax.dynamic_index_in_dim(cot, 1 - core, 0, keepdims=False)
    return dot(layer, first, TN) + dot(swap(layer, "c"), second, TN)


def solution(mesh):
    whole = Mesh(mesh.devices.reshape(4, 2, 2, 2, 8), ("y", "xl", "c", "xh", "z"))
    return jax.shard_map(
        body,
        mesh=whole,
        in_specs=(
            P(VAR, SEQ, None),
            P(VAR, None, None),
            P(VAR, None),
            P(),
            P(),
            P(None, None, VAR),
            P(VAR, None),
            P(SEQ, VAR),
        ),
        out_specs=P(SEQ, VAR),
        check_vma=False,
    )
```

```python
import math

import jax
import jax.numpy as jnp
from jax import lax
from jax.experimental import pallas as pl
from jax.experimental.pallas import tpu as pltpu
from jax.sharding import Mesh, PartitionSpec as P

EPS = 1e-05
HD = 128
F32 = jnp.float32
BF16 = jnp.bfloat16
VAR = ("y", "xl", "c")
CHIPS = ("y", "xl")
SEQ = ("xh", "z")
NT = (((1,), (1,)), ((), ()))
TN = (((0,), (0,)), ((), ()))
NN = (((1,), (0,)), ((), ()))
MB = 1024 * 1024


def dot(a, b, dims):
    return lax.dot_general(a, b, dims, preferred_element_type=F32)


def params(megabytes):
    return pltpu.CompilerParams(vmem_limit_bytes=megabytes * MB)


def packed(peak, total):
    blank = jnp.zeros_like(peak)
    return jnp.concatenate([peak, total, blank, blank], axis=1)


def unpacked(stats):
    return stats[:, 0:32], stats[:, 32:64]


def embed_kernel(
    pixels_hbm, weight_ref, shift_ref, query_hbm, rows_ref, keep_ref, send_ref, cols_ref,
    pixels_ref, query_ref, embedded, scores, held, keep, send, sems, small_sems, out_sems,
):
    core = lax.axis_index("c")
    z = lax.axis_index("z")
    count, rows, width = embedded.shape
    heads = query_ref.shape[0]
    half = rows // 2
    small = [
        pltpu.make_async_copy(pixels_hbm, pixels_ref, small_sems.at[0]),
        pltpu.make_async_copy(query_hbm, query_ref, small_sems.at[1]),
    ]
    copies = [
        pltpu.make_async_copy(weight_ref.at[v], held.at[v], sems.at[v]) for v in range(count)
    ]
    for copy in [small[0], copies[0], small[1]] + copies[1:]:
        copy.start()
    cut = cols_ref.shape[1] // 2
    slices = []
    for side in range(2):
        place = pl.multiple_of(side * (width // 2) + z * cut, cut)
        slices.append(
            pltpu.make_async_copy(
                rows_ref.at[:, pl.ds(place, cut)],
                cols_ref.at[:, pl.ds(side * cut, cut)],
                small_sems.at[2 + side],
            )
        )
        slices[side].start()
    new = lax.broadcasted_iota(jnp.int32, (rows, rows), 0)
    old = lax.broadcasted_iota(jnp.int32, (rows, rows), 1)
    group = (new % half) // 8 * 2 + jnp.where(new < half, core, 1 - core)
    order = jnp.where(old == group * 8 + new % 8, 1.0, 0.0).astype(BF16)
    step = 1024
    shifts = shift_ref[...].astype(F32)
    row = lax.broadcasted_iota(jnp.int32, shifts.shape, 0)
    small[0].wait()
    for v in range(count):
        tokens = dot(order, pixels_ref[v], NT).astype(BF16)
        if v == 0:
            small[1].wait()
        if v % 2 == 0:
            for copy in copies[v : v + 2]:
                copy.wait()
        total = jnp.zeros((rows, heads), F32)
        shift = jnp.sum(jnp.where(row == v, shifts, 0.0), axis=0, keepdims=True)
        for at in range(0, width, step):
            block = dot(tokens, held[v, :, at : at + step], NN)
            block = (block + shift[:, at : at + step]).astype(BF16)
            embedded[v, :, at : at + step] = block
            total = total + dot(block, query_ref[:, at : at + step], NT)
        scores[v] = total / math.sqrt(HD)
    every = scores[...]
    peak = jnp.max(every, axis=0)
    weights = jnp.exp(every - peak[None])
    total = jnp.sum(weights, axis=0)
    keep[:, width:] = packed(peak[:half], total[:half])
    send[:, width:] = packed(peak[half:], total[half:])
    leaving = []

    def leave(place, size):
        at = len(leaving) // 2
        for side, (source, target) in enumerate(((keep, keep_ref), (send, send_ref))):
            copy = pltpu.make_async_copy(
                source.at[:, pl.ds(place, size)], target.at[:, pl.ds(place, size)], out_sems.at[side, at]
            )
            copy.start()
            leaving.append(copy)

    leave(width, 128)
    for h in range(heads):
        cols = slice(h * HD, (h + 1) * HD)
        numer = weights[0][:, h : h + 1] * embedded[0, :, cols].astype(F32)
        for v in range(1, count):
            numer = numer + weights[v][:, h : h + 1] * embedded[v, :, cols].astype(F32)
        keep[:, cols] = numer[:half]
        send[:, cols] = numer[half:]
        if h % 8 == 7:
            leave((h - 7) * HD, 8 * HD)
    for copy in slices + leaving:
        copy.wait()


def embed(pixels, weight, shift, query, out_weight):
    count, depth, rows = pixels.shape
    width = weight.shape[2]
    heads = query.shape[0]
    half = rows // 2
    hbm = pl.BlockSpec(memory_space=pltpu.HBM)
    part = jax.ShapeDtypeStruct((half, width + 128), F32)
    return pl.pallas_call(
        embed_kernel,
        in_specs=[hbm, hbm, pl.BlockSpec(memory_space=pltpu.VMEM), hbm, hbm],
        out_specs=[hbm] * 3,
        out_shape=(part, part, jax.ShapeDtypeStruct((out_weight.shape[0], width // 8), BF16)),
        scratch_shapes=[
            pltpu.VMEM((count, depth, rows), BF16),
            pltpu.VMEM((heads, width), BF16),
            pltpu.VMEM((count, rows, width), BF16),
            pltpu.VMEM((count, rows, heads), F32),
            pltpu.VMEM((count, depth, width), BF16),
            pltpu.VMEM((half, width + 128), F32),
            pltpu.VMEM((half, width + 128), F32),
            pltpu.SemaphoreType.DMA((count,)),
            pltpu.SemaphoreType.DMA((4,)),
            pltpu.SemaphoreType.DMA((2, 5)),
        ],
        compiler_params=params(60),
        cost_estimate=pl.CostEstimate(
            flops=2 * count * rows * width * (depth + heads),
            bytes_accessed=4 * count * depth * width,
            transcendentals=count * rows * heads,
        ),
        name="embed",
    )(pixels, weight, shift, query, out_weight)


def stage_kernel(source_ref, target_ref):
    target_ref[...] = source_ref[...]


def stage(source):
    return pl.pallas_call(
        stage_kernel,
        out_shape=jax.ShapeDtypeStruct(source.shape, F32),
        compiler_params=params(12),
        cost_estimate=pl.CostEstimate(flops=0, bytes_accessed=8 * MB, transcendentals=0),
        name="stage",
    )(source)


def pair_kernel(mine_ref, other_ref, cot_ref, cot_got_ref, out_ref, cot_out_ref):
    x_hi = lax.axis_index("xh")
    tokens = cot_ref.shape[0]
    cot_out_ref[pl.ds(pl.multiple_of(x_hi * tokens, tokens), tokens), :] = cot_ref[...]
    cot_out_ref[pl.ds(pl.multiple_of((1 - x_hi) * tokens, tokens), tokens), :] = cot_got_ref[...]
    rows, padded = mine_ref.shape
    width = padded - 128
    heads = width // HD
    peak_a, total_a = unpacked(mine_ref[:, width:])
    peak_b, total_b = unpacked(other_ref[:, width:])
    top = jnp.maximum(peak_a, peak_b)
    scale_a = jnp.exp(peak_a - top)
    scale_b = jnp.exp(peak_b - top)
    for h in range(heads):
        cols = slice(h * HD, (h + 1) * HD)
        first = mine_ref[:, cols] * scale_a[:, h : h + 1]
        second = other_ref[:, cols] * scale_b[:, h : h + 1]
        out_ref[:, cols] = first + second
    out_ref[:, width:] = packed(top, total_a * scale_a + total_b * scale_b)


def pair(mine, other, cot, cot_got):
    tokens, cols = cot.shape
    return pl.pallas_call(
        pair_kernel,
        out_shape=(
            jax.ShapeDtypeStruct(other.shape, F32),
            jax.ShapeDtypeStruct((2 * tokens, cols), BF16),
        ),
        compiler_params=params(12),
        name="pair",
    )(mine, other, cot, cot_got)


def merge_kernel(parts_ref, gain_ref, normed_ref, kept_ref, whole):
    rows, padded = parts_ref.shape
    width = padded - 128
    heads = width // HD
    share = 8
    sources = rows // share
    peak, total = unpacked(parts_ref[:, width:])
    peak = peak.reshape(sources, share, heads)
    total = total.reshape(sources, share, heads)
    top = jnp.max(peak, axis=0)
    scale = jnp.exp(peak - top[None])
    total = jnp.sum(total * scale, axis=0)
    scale = scale.reshape(rows, heads)
    sums = jnp.zeros((share, HD), F32)
    last = None
    for h in range(heads):
        cols = slice(h * HD, (h + 1) * HD)
        numer = jnp.zeros((share, HD), F32)
        for at in range(0, rows, share):
            numer = numer + parts_ref[at : at + share, cols] * scale[at : at + share, h : h + 1]
        value = (numer / total[:, h : h + 1]).astype(BF16).astype(F32)
        whole[:, cols] = value
        sums = sums + value
        if h % 2 == 0:
            last = value
        else:
            block = h // 2
            to = (block % 8 * 2 + block // 8) * 16
            kept_ref[to : to + 16, :] = jnp.concatenate([last, value], axis=0).astype(BF16)
    center = jnp.sum(sums, axis=1, keepdims=True) / width
    squares = jnp.zeros((share, HD), F32)
    for h in range(heads):
        shifted = whole[:, h * HD : (h + 1) * HD] - center
        squares = squares + shifted * shifted
    factor = lax.rsqrt(jnp.sum(squares, axis=1, keepdims=True) / width + EPS)
    for h in range(heads):
        cols = slice(h * HD, (h + 1) * HD)
        value = (whole[:, cols] - center) * factor * gain_ref[:, cols].astype(F32)
        twice = jnp.concatenate([value, value], axis=0).astype(BF16)
        for at in range(0, normed_ref.shape[0], 16):
            normed_ref[at : at + 16, cols] = twice


def merge(parts, gain, copies):
    rows, padded = parts.shape
    width = padded - 128
    return pl.pallas_call(
        merge_kernel,
        out_shape=(
            jax.ShapeDtypeStruct((copies * 8, width), BF16),
            jax.ShapeDtypeStruct((width // 16, HD), BF16),
        ),
        scratch_shapes=[pltpu.VMEM((8, width), F32)],
        compiler_params=params(12),
        name="merge",
    )(parts, gain)


def qkv_kernel(mine_ref, other_ref, weight_ref, kv_ref, keep_ref, send_ref, tokens, held, sems):
    core = lax.axis_index("c")
    x_hi = lax.axis_index("xh")
    half, width = mine_ref.shape
    rows = 2 * half
    parts = sems.shape[1]
    depth = width // parts
    copies = [
        [
            pltpu.make_async_copy(
                weight_ref.at[k, pl.ds(part * depth, depth), :],
                held.at[k, pl.ds(part * depth, depth), :],
                sems.at[k, part],
            )
            for part in range(parts)
        ]
        for k in range(3)
    ]
    for k in range(3):
        for copy in copies[k]:
            copy.start()
    tokens[pl.ds(pl.multiple_of(core * half, half), half), :] = mine_ref[...]
    tokens[pl.ds(pl.multiple_of((1 - core) * half, half), half), :] = other_ref[...]
    for k in range(3):
        for copy in copies[k]:
            copy.wait()
        made = dot(tokens[...], held[k], NN)
        first, second = made[:, :HD], made[:, HD:]
        if k == 0:
            keep_ref[...] = jnp.where(x_hi == 0, first, second).astype(BF16)
            send_ref[...] = jnp.where(x_hi == 0, second, first).astype(BF16)
        else:
            cols = slice((k - 1) * HD, k * HD)
            for to in range(16):
                value = first if to < 8 else second
                kv_ref[to * rows : (to + 1) * rows, cols] = value.astype(BF16)


def project(mine, other, weight):
    half, width = mine.shape
    cols = weight.shape[2]
    rows = 2 * half
    parts = 1
    vmem = pl.BlockSpec(memory_space=pltpu.VMEM)
    hbm = pl.BlockSpec(memory_space=pltpu.HBM)
    shapes = [(16 * rows, 2 * HD), (rows, HD), (rows, HD)]
    return pl.pallas_call(
        qkv_kernel,
        in_specs=[vmem, vmem, hbm],
        out_shape=[jax.ShapeDtypeStruct(shape, BF16) for shape in shapes],
        scratch_shapes=[
            pltpu.VMEM((rows, width), BF16),
            pltpu.VMEM((3, width, cols), BF16),
            pltpu.SemaphoreType.DMA((3, parts)),
        ],
        compiler_params=params(50),
        name="project",
    )(mine, other, weight)


def attend_kernel(keep_ref, got_ref, kv_ref, out_ref, scores):
    x_hi = lax.axis_index("xh")
    count = kv_ref.shape[0]
    step = 256
    mixed = []
    for side in range(2):
        query = jnp.where(x_hi == side, keep_ref[...], got_ref[...])
        for at in range(0, count, step):
            scores[:, at : at + step] = dot(query, kv_ref[at : at + step, :HD], NT) / math.sqrt(HD)
        every = scores[...]
        peak = jnp.max(every, axis=1, keepdims=True)
        weights = jnp.exp(every - peak)
        total = jnp.sum(weights, axis=1, keepdims=True)
        mixed.append(dot(weights.astype(BF16), kv_ref[:, HD:], NN) / total)
    for chip in range(8):
        for core in range(2):
            at = core * 64 + chip * 8
            to = (chip * 2 + core) * 16
            out_ref[to : to + 16, :] = jnp.concatenate(
                [mixed[0][at : at + 8], mixed[1][at : at + 8]], axis=0
            ).astype(BF16)


def attend(keep, got, kv):
    return pl.pallas_call(
        attend_kernel,
        out_shape=jax.ShapeDtypeStruct((256, HD), BF16),
        scratch_shapes=[pltpu.VMEM((128, 2048), F32)],
        compiler_params=params(16),
        name="attend",
    )(keep, got, kv)


def output_kernel(parts_ref, weight_ref, out_ref, attended, held, sems):
    bands = parts_ref.shape[0]
    width, cols = weight_ref.shape
    pieces = sems.shape[0]
    depth = width // pieces
    copies = [
        pltpu.make_async_copy(
            weight_ref.at[pl.ds(k * depth, depth), :], held.at[pl.ds(k * depth, depth), :], sems.at[k]
        )
        for k in range(pieces)
    ]
    for copy in copies:
        copy.start()
    for band in range(0, bands, 2):
        to = band * 8
        for source in range(16):
            at = source * 16
            a = parts_ref[band, at : at + 16, :].astype(F32)
            b = parts_ref[band + 1, at : at + 16, :].astype(F32)
            for side in range(2):
                head = 2 * source + side
                rows = slice(side * 8, side * 8 + 8)
                attended[to : to + 16, head * HD : (head + 1) * HD] = jnp.concatenate(
                    [a[rows], b[rows]], axis=0
                ).astype(BF16)
    product = jnp.zeros((attended.shape[0], cols), F32)
    for k in range(pieces):
        copies[k].wait()
        at = slice(k * depth, (k + 1) * depth)
        product = product + dot(attended[:, at], held[at, :], NN)
    half = cols // 2
    count = out_ref.shape[0] // 64
    for band in range(0, bands, 2):
        residual = []
        for b in (band, band + 1):
            kept = parts_ref[b, 256:288, :].astype(F32)
            residual.append(
                jnp.concatenate([kept[k : k + 8] for k in range(0, 32, 8)], axis=1)
            )
        at = band * 8
        layer = (jnp.concatenate(residual, axis=0) + product[at : at + 16]).astype(BF16)
        for to in range(count):
            side = to % 2
            out_ref[to * 64 + at : to * 64 + at + 16, :] = layer[:, side * half : (side + 1) * half]


def output(parts, weight):
    width, cols = weight.shape
    return pl.pallas_call(
        output_kernel,
        in_specs=[pl.BlockSpec(memory_space=pltpu.VMEM), pl.BlockSpec(memory_space=pltpu.HBM)],
        out_shape=jax.ShapeDtypeStruct((16 * 64, cols // 2), BF16),
        scratch_shapes=[
            pltpu.VMEM((64, width), BF16),
            pltpu.VMEM((width, cols), BF16),
            pltpu.SemaphoreType.DMA((8,)),
        ],
        compiler_params=params(50),
        name="output",
    )(parts, weight)


def swap(x, axis):
    return lax.ppermute(x, axis, [(0, 1), (1, 0)])


def exchange(x, axes):
    return lax.all_to_all(x, axes, 0, 0, tiled=True)


def body(patches, patch_weight, var_embed, agg_query, norm_gain, qkv_weight, out_weight, head_cot):
    core = lax.axis_index("c")
    width = out_weight.shape[1]

    cot_got = swap(head_cot, "xh")
    keep, send, cols = embed(
        patches.transpose(0, 2, 1), patch_weight, var_embed, agg_query.T, out_weight
    )
    send, cot_got = lax.optimization_barrier((send, cot_got))
    parts, cot = pair(stage(keep), swap(send, "c"), head_cot, cot_got)
    cot = lax.all_gather(cot, "z", axis=0, tiled=True)
    parts, cols = lax.optimization_barrier((exchange(parts, CHIPS), cols))
    cols = lax.all_gather(cols, VAR, axis=0, tiled=True)
    normed, kept = merge(parts, norm_gain.reshape(1, width), 8)
    normed = exchange(normed, CHIPS)
    kv, query, query_send = project(normed, swap(normed, "c"), qkv_weight.transpose(1, 0, 2))
    query_got = swap(query_send, "xh")
    kv, cot = lax.optimization_barrier((exchange(kv, SEQ), cot))
    attended = attend(query, query_got, kv)
    attended = exchange(attended, VAR + ("xh",))
    sent = jnp.concatenate(
        [jnp.broadcast_to(attended[None], (8, 256, HD)), kept.reshape(8, 32, HD)], axis=1
    )
    got = exchange(sent, "z")
    layer = output(got, cols)
    layer = exchange(layer, CHIPS + ("xh",))
    cot = cot.reshape(8, 2, 8, 2, 8, 384).transpose(3, 2, 1, 0, 4, 5).reshape(2, 1024, 384)
    first = lax.dynamic_index_in_dim(cot, core, 0, keepdims=False)
    second = lax.dynamic_index_in_dim(cot, 1 - core, 0, keepdims=False)
    return dot(layer, first, TN) + dot(swap(layer, "c"), second, TN)


def solution(mesh):
    whole = Mesh(mesh.devices.reshape(4, 2, 2, 2, 8), ("y", "xl", "c", "xh", "z"))
    return jax.shard_map(
        body,
        mesh=whole,
        in_specs=(
            P(VAR, SEQ, None),
            P(VAR, None, None),
            P(VAR, None),
            P(),
            P(),
            P(None, None, VAR),
            P(VAR, None),
            P(SEQ, VAR),
        ),
        out_specs=P(SEQ, VAR),
        check_vma=False,
    )
```

```python
import math

import jax
import jax.numpy as jnp
from jax import lax
from jax.experimental import pallas as pl
from jax.experimental.pallas import tpu as pltpu
from jax.sharding import Mesh, PartitionSpec as P

EPS = 1e-05
HD = 128
F32 = jnp.float32
BF16 = jnp.bfloat16
VAR = ("y", "xl", "c")
CHIPS = ("y", "xl")
SEQ = ("xh", "z")
NT = (((1,), (1,)), ((), ()))
TN = (((0,), (0,)), ((), ()))
NN = (((1,), (0,)), ((), ()))
MB = 1024 * 1024


def dot(a, b, dims):
    return lax.dot_general(a, b, dims, preferred_element_type=F32)


def params(megabytes):
    return pltpu.CompilerParams(vmem_limit_bytes=megabytes * MB)


def packed(peak, total):
    blank = jnp.zeros_like(peak)
    return jnp.concatenate([peak, total, blank, blank], axis=1)


def unpacked(stats):
    return stats[:, 0:32], stats[:, 32:64]


def embed_kernel(
    pixels_hbm, weight_ref, shift_ref, query_hbm, rows_ref, keep_ref, send_ref, cols_ref,
    pixels_ref, shifts, query_ref, embedded, scores, held, keep, send, sems, small_sems, out_sems,
):
    core = lax.axis_index("c")
    z = lax.axis_index("z")
    count, rows, width = embedded.shape
    heads = query_ref.shape[0]
    half = rows // 2
    small = [
        pltpu.make_async_copy(pixels_hbm, pixels_ref, small_sems.at[0]),
        pltpu.make_async_copy(query_hbm, query_ref, small_sems.at[1]),
    ]
    copies = [
        pltpu.make_async_copy(weight_ref.at[v], held.at[v], sems.at[v]) for v in range(count)
    ]
    for copy in [small[0], copies[0], small[1]] + copies[1:]:
        copy.start()
    cut = cols_ref.shape[1] // 2
    slices = []
    for side in range(2):
        place = pl.multiple_of(side * (width // 2) + z * cut, cut)
        slices.append(
            pltpu.make_async_copy(
                rows_ref.at[:, pl.ds(place, cut)],
                cols_ref.at[:, pl.ds(side * cut, cut)],
                small_sems.at[2 + side],
            )
        )
        slices[side].start()
    new = lax.broadcasted_iota(jnp.int32, (rows, rows), 0)
    old = lax.broadcasted_iota(jnp.int32, (rows, rows), 1)
    group = (new % half) // 8 * 2 + jnp.where(new < half, core, 1 - core)
    order = jnp.where(old == group * 8 + new % 8, 1.0, 0.0).astype(BF16)
    step = 1024
    shifts[...] = shift_ref[...].astype(F32)
    small[0].wait()
    for v in range(count):
        tokens = dot(order, pixels_ref[v], NT).astype(BF16)
        if v == 0:
            small[1].wait()
        if v % 2 == 0:
            for copy in copies[v : v + 2]:
                copy.wait()
        total = jnp.zeros((rows, heads), F32)
        for at in range(0, width, step):
            block = dot(tokens, held[v, :, at : at + step], NN)
            block = (block + shifts[v : v + 1, at : at + step]).astype(BF16)
            embedded[v, :, at : at + step] = block
            total = total + dot(block, query_ref[:, at : at + step], NT)
        scores[v] = total / math.sqrt(HD)
    every = scores[...]
    peak = jnp.max(every, axis=0)
    weights = jnp.exp(every - peak[None])
    total = jnp.sum(weights, axis=0)
    keep[:, width:] = packed(peak[:half], total[:half])
    send[:, width:] = packed(peak[half:], total[half:])
    leaving = []

    def leave(place, size):
        at = len(leaving) // 2
        for side, (source, target) in enumerate(((keep, keep_ref), (send, send_ref))):
            copy = pltpu.make_async_copy(
                source.at[:, pl.ds(place, size)], target.at[:, pl.ds(place, size)], out_sems.at[side, at]
            )
            copy.start()
            leaving.append(copy)

    leave(width, 128)
    for h in range(heads):
        cols = slice(h * HD, (h + 1) * HD)
        numer = weights[0][:, h : h + 1] * embedded[0, :, cols].astype(F32)
        for v in range(1, count):
            numer = numer + weights[v][:, h : h + 1] * embedded[v, :, cols].astype(F32)
        keep[:, cols] = numer[:half]
        send[:, cols] = numer[half:]
        if h % 8 == 7:
            leave((h - 7) * HD, 8 * HD)
    for copy in slices + leaving:
        copy.wait()


def embed(pixels, weight, shift, query, out_weight):
    count, depth, rows = pixels.shape
    width = weight.shape[2]
    heads = query.shape[0]
    half = rows // 2
    hbm = pl.BlockSpec(memory_space=pltpu.HBM)
    part = jax.ShapeDtypeStruct((half, width + 128), F32)
    return pl.pallas_call(
        embed_kernel,
        in_specs=[hbm, hbm, pl.BlockSpec(memory_space=pltpu.VMEM), hbm, hbm],
        out_specs=[hbm] * 3,
        out_shape=(part, part, jax.ShapeDtypeStruct((out_weight.shape[0], width // 8), BF16)),
        scratch_shapes=[
            pltpu.VMEM((count, depth, rows), BF16),
            pltpu.VMEM((count, width), F32),
            pltpu.VMEM((heads, width), BF16),
            pltpu.VMEM((count, rows, width), BF16),
            pltpu.VMEM((count, rows, heads), F32),
            pltpu.VMEM((count, depth, width), BF16),
            pltpu.VMEM((half, width + 128), F32),
            pltpu.VMEM((half, width + 128), F32),
            pltpu.SemaphoreType.DMA((count,)),
            pltpu.SemaphoreType.DMA((4,)),
            pltpu.SemaphoreType.DMA((2, 5)),
        ],
        compiler_params=params(60),
        cost_estimate=pl.CostEstimate(
            flops=2 * count * rows * width * (depth + heads),
            bytes_accessed=4 * count * depth * width,
            transcendentals=count * rows * heads,
        ),
        name="embed",
    )(pixels, weight, shift, query, out_weight)


def stage_kernel(source_ref, target_ref):
    target_ref[...] = source_ref[...]


def stage(source):
    return pl.pallas_call(
        stage_kernel,
        out_shape=jax.ShapeDtypeStruct(source.shape, F32),
        compiler_params=params(12),
        cost_estimate=pl.CostEstimate(flops=0, bytes_accessed=8 * MB, transcendentals=0),
        name="stage",
    )(source)


def pair_kernel(mine_ref, other_ref, cot_ref, cot_got_ref, out_ref, cot_out_ref):
    x_hi = lax.axis_index("xh")
    tokens = cot_ref.shape[0]
    cot_out_ref[pl.ds(pl.multiple_of(x_hi * tokens, tokens), tokens), :] = cot_ref[...]
    cot_out_ref[pl.ds(pl.multiple_of((1 - x_hi) * tokens, tokens), tokens), :] = cot_got_ref[...]
    rows, padded = mine_ref.shape
    width = padded - 128
    heads = width // HD
    peak_a, total_a = unpacked(mine_ref[:, width:])
    peak_b, total_b = unpacked(other_ref[:, width:])
    top = jnp.maximum(peak_a, peak_b)
    scale_a = jnp.exp(peak_a - top)
    scale_b = jnp.exp(peak_b - top)
    for h in range(heads):
        cols = slice(h * HD, (h + 1) * HD)
        first = mine_ref[:, cols] * scale_a[:, h : h + 1]
        second = other_ref[:, cols] * scale_b[:, h : h + 1]
        out_ref[:, cols] = first + second
    out_ref[:, width:] = packed(top, total_a * scale_a + total_b * scale_b)


def pair(mine, other, cot, cot_got):
    tokens, cols = cot.shape
    return pl.pallas_call(
        pair_kernel,
        out_shape=(
            jax.ShapeDtypeStruct(other.shape, F32),
            jax.ShapeDtypeStruct((2 * tokens, cols), BF16),
        ),
        compiler_params=params(12),
        name="pair",
    )(mine, other, cot, cot_got)


def merge_kernel(parts_ref, gain_ref, normed_ref, kept_ref, whole):
    rows, padded = parts_ref.shape
    width = padded - 128
    heads = width // HD
    share = 8
    sources = rows // share
    peak, total = unpacked(parts_ref[:, width:])
    peak = peak.reshape(sources, share, heads)
    total = total.reshape(sources, share, heads)
    top = jnp.max(peak, axis=0)
    scale = jnp.exp(peak - top[None])
    total = jnp.sum(total * scale, axis=0)
    scale = scale.reshape(rows, heads)
    sums = jnp.zeros((share, HD), F32)
    last = None
    for h in range(heads):
        cols = slice(h * HD, (h + 1) * HD)
        numer = jnp.zeros((share, HD), F32)
        for at in range(0, rows, share):
            numer = numer + parts_ref[at : at + share, cols] * scale[at : at + share, h : h + 1]
        value = (numer / total[:, h : h + 1]).astype(BF16).astype(F32)
        whole[:, cols] = value
        sums = sums + value
        if h % 2 == 0:
            last = value
        else:
            block = h // 2
            to = (block % 8 * 2 + block // 8) * 16
            kept_ref[to : to + 16, :] = jnp.concatenate([last, value], axis=0).astype(BF16)
    center = jnp.sum(sums, axis=1, keepdims=True) / width
    squares = jnp.zeros((share, HD), F32)
    for h in range(heads):
        shifted = whole[:, h * HD : (h + 1) * HD] - center
        squares = squares + shifted * shifted
    factor = lax.rsqrt(jnp.sum(squares, axis=1, keepdims=True) / width + EPS)
    for h in range(heads):
        cols = slice(h * HD, (h + 1) * HD)
        value = (whole[:, cols] - center) * factor * gain_ref[:, cols].astype(F32)
        twice = jnp.concatenate([value, value], axis=0).astype(BF16)
        for at in range(0, normed_ref.shape[0], 16):
            normed_ref[at : at + 16, cols] = twice


def merge(parts, gain, copies):
    rows, padded = parts.shape
    width = padded - 128
    return pl.pallas_call(
        merge_kernel,
        out_shape=(
            jax.ShapeDtypeStruct((copies * 8, width), BF16),
            jax.ShapeDtypeStruct((width // 16, HD), BF16),
        ),
        scratch_shapes=[pltpu.VMEM((8, width), F32)],
        compiler_params=params(12),
        name="merge",
    )(parts, gain)


def qkv_kernel(mine_ref, other_ref, weight_ref, kv_ref, keep_ref, send_ref, tokens, held, sems):
    core = lax.axis_index("c")
    x_hi = lax.axis_index("xh")
    half, width = mine_ref.shape
    rows = 2 * half
    parts = sems.shape[1]
    depth = width // parts
    copies = [
        [
            pltpu.make_async_copy(
                weight_ref.at[k, pl.ds(part * depth, depth), :],
                held.at[k, pl.ds(part * depth, depth), :],
                sems.at[k, part],
            )
            for part in range(parts)
        ]
        for k in range(3)
    ]
    for k in range(3):
        for copy in copies[k]:
            copy.start()
    tokens[pl.ds(pl.multiple_of(core * half, half), half), :] = mine_ref[...]
    tokens[pl.ds(pl.multiple_of((1 - core) * half, half), half), :] = other_ref[...]
    for k in range(3):
        for copy in copies[k]:
            copy.wait()
        made = dot(tokens[...], held[k], NN)
        first, second = made[:, :HD], made[:, HD:]
        if k == 0:
            keep_ref[...] = jnp.where(x_hi == 0, first, second).astype(BF16)
            send_ref[...] = jnp.where(x_hi == 0, second, first).astype(BF16)
        else:
            cols = slice((k - 1) * HD, k * HD)
            for to in range(16):
                value = first if to < 8 else second
                kv_ref[to * rows : (to + 1) * rows, cols] = value.astype(BF16)


def project(mine, other, weight):
    half, width = mine.shape
    cols = weight.shape[2]
    rows = 2 * half
    parts = 1
    vmem = pl.BlockSpec(memory_space=pltpu.VMEM)
    hbm = pl.BlockSpec(memory_space=pltpu.HBM)
    shapes = [(16 * rows, 2 * HD), (rows, HD), (rows, HD)]
    return pl.pallas_call(
        qkv_kernel,
        in_specs=[vmem, vmem, hbm],
        out_shape=[jax.ShapeDtypeStruct(shape, BF16) for shape in shapes],
        scratch_shapes=[
            pltpu.VMEM((rows, width), BF16),
            pltpu.VMEM((3, width, cols), BF16),
            pltpu.SemaphoreType.DMA((3, parts)),
        ],
        compiler_params=params(50),
        name="project",
    )(mine, other, weight)


def attend_kernel(keep_ref, got_ref, kv_ref, out_ref, scores):
    x_hi = lax.axis_index("xh")
    count = kv_ref.shape[0]
    step = 256
    mixed = []
    for side in range(2):
        query = jnp.where(x_hi == side, keep_ref[...], got_ref[...])
        for at in range(0, count, step):
            scores[:, at : at + step] = dot(query, kv_ref[at : at + step, :HD], NT) / math.sqrt(HD)
        every = scores[...]
        peak = jnp.max(every, axis=1, keepdims=True)
        weights = jnp.exp(every - peak)
        total = jnp.sum(weights, axis=1, keepdims=True)
        mixed.append(dot(weights.astype(BF16), kv_ref[:, HD:], NN) / total)
    for chip in range(8):
        for core in range(2):
            at = core * 64 + chip * 8
            to = (chip * 2 + core) * 16
            out_ref[to : to + 16, :] = jnp.concatenate(
                [mixed[0][at : at + 8], mixed[1][at : at + 8]], axis=0
            ).astype(BF16)


def attend(keep, got, kv):
    return pl.pallas_call(
        attend_kernel,
        out_shape=jax.ShapeDtypeStruct((256, HD), BF16),
        scratch_shapes=[pltpu.VMEM((128, 2048), F32)],
        compiler_params=params(16),
        name="attend",
    )(keep, got, kv)


def output_kernel(parts_ref, weight_ref, out_ref, attended, held, sems):
    bands = parts_ref.shape[0]
    width, cols = weight_ref.shape
    pieces = sems.shape[0]
    depth = width // pieces
    copies = [
        pltpu.make_async_copy(
            weight_ref.at[pl.ds(k * depth, depth), :], held.at[pl.ds(k * depth, depth), :], sems.at[k]
        )
        for k in range(pieces)
    ]
    for copy in copies:
        copy.start()
    for band in range(0, bands, 2):
        to = band * 8
        for source in range(16):
            at = source * 16
            a = parts_ref[band, at : at + 16, :].astype(F32)
            b = parts_ref[band + 1, at : at + 16, :].astype(F32)
            for side in range(2):
                head = 2 * source + side
                rows = slice(side * 8, side * 8 + 8)
                attended[to : to + 16, head * HD : (head + 1) * HD] = jnp.concatenate(
                    [a[rows], b[rows]], axis=0
                ).astype(BF16)
    product = jnp.zeros((attended.shape[0], cols), F32)
    for k in range(pieces):
        copies[k].wait()
        at = slice(k * depth, (k + 1) * depth)
        product = product + dot(attended[:, at], held[at, :], NN)
    half = cols // 2
    count = out_ref.shape[0] // 64
    for band in range(0, bands, 2):
        residual = []
        for b in (band, band + 1):
            kept = parts_ref[b, 256:288, :].astype(F32)
            residual.append(
                jnp.concatenate([kept[k : k + 8] for k in range(0, 32, 8)], axis=1)
            )
        at = band * 8
        layer = (jnp.concatenate(residual, axis=0) + product[at : at + 16]).astype(BF16)
        for to in range(count):
            side = to % 2
            out_ref[to * 64 + at : to * 64 + at + 16, :] = layer[:, side * half : (side + 1) * half]


def output(parts, weight):
    width, cols = weight.shape
    return pl.pallas_call(
        output_kernel,
        in_specs=[pl.BlockSpec(memory_space=pltpu.VMEM), pl.BlockSpec(memory_space=pltpu.HBM)],
        out_shape=jax.ShapeDtypeStruct((16 * 64, cols // 2), BF16),
        scratch_shapes=[
            pltpu.VMEM((64, width), BF16),
            pltpu.VMEM((width, cols), BF16),
            pltpu.SemaphoreType.DMA((8,)),
        ],
        compiler_params=params(50),
        name="output",
    )(parts, weight)


def swap(x, axis):
    return lax.ppermute(x, axis, [(0, 1), (1, 0)])


def exchange(x, axes):
    return lax.all_to_all(x, axes, 0, 0, tiled=True)


def body(patches, patch_weight, var_embed, agg_query, norm_gain, qkv_weight, out_weight, head_cot):
    core = lax.axis_index("c")
    width = out_weight.shape[1]

    cot_got = swap(head_cot, "xh")
    keep, send, cols = embed(
        patches.transpose(0, 2, 1), patch_weight, var_embed, agg_query.T, out_weight
    )
    send, cot_got = lax.optimization_barrier((send, cot_got))
    parts, cot = pair(stage(keep), swap(send, "c"), head_cot, cot_got)
    cot = lax.all_gather(cot, "z", axis=0, tiled=True)
    parts, cols = lax.optimization_barrier((exchange(parts, CHIPS), cols))
    cols = lax.all_gather(cols, VAR, axis=0, tiled=True)
    normed, kept = merge(parts, norm_gain.reshape(1, width), 8)
    normed = exchange(normed, CHIPS)
    kv, query, query_send = project(normed, swap(normed, "c"), qkv_weight.transpose(1, 0, 2))
    query_got = swap(query_send, "xh")
    kv, cot = lax.optimization_barrier((exchange(kv, SEQ), cot))
    attended = attend(query, query_got, kv)
    attended = exchange(attended, VAR + ("xh",))
    sent = jnp.concatenate(
        [jnp.broadcast_to(attended[None], (8, 256, HD)), kept.reshape(8, 32, HD)], axis=1
    )
    got = exchange(sent, "z")
    layer = output(got, cols)
    layer = exchange(layer, CHIPS + ("xh",))
    cot = cot.reshape(8, 2, 8, 2, 8, 384).transpose(3, 2, 1, 0, 4, 5).reshape(2, 1024, 384)
    first = lax.dynamic_index_in_dim(cot, core, 0, keepdims=False)
    second = lax.dynamic_index_in_dim(cot, 1 - core, 0, keepdims=False)
    return dot(layer, first, TN) + dot(swap(layer, "c"), second, TN)


def solution(mesh):
    whole = Mesh(mesh.devices.reshape(4, 2, 2, 2, 8), ("y", "xl", "c", "xh", "z"))
    return jax.shard_map(
        body,
        mesh=whole,
        in_specs=(
            P(VAR, SEQ, None),
            P(VAR, None, None),
            P(VAR, None),
            P(),
            P(),
            P(None, None, VAR),
            P(VAR, None),
            P(SEQ, VAR),
        ),
        out_specs=P(SEQ, VAR),
        check_vma=False,
    )
```
